32 devices in a mesh: batch: 32 (over z, y, x, core).
Axes of the slice: x: 2, y: 2, z: 4, core: 2. Of those that a mesh axis runs over, the one named last changes fastest.
Arguments:
- tokens: bfloat16 [32768, 768], P('batch'), may hold values from -6 to 6
- segment_ids: int32 [64, 512], P('batch'), may hold values from -1 to 7, as said below
- pair_index: int32 [512], P('batch'), may hold values from 0 to 511, as said below
- qkv_weight: bfloat16 [768, 2304], replicated, may hold values from -0.21875 to 0.21875
- query_bias: float32 [768], replicated, may hold values from -1.75 to 1.75
- value_bias: float32 [768], replicated, may hold values from -1.75 to 1.75
- proj_weight: bfloat16 [768, 768], replicated, may hold values from -0.875 to 0.875
- proj_bias: float32 [768], replicated, may hold values from -1.75 to 1.75
- attn_gain: float32 [768], replicated, may hold values from 0.5 to 1.5
- attn_shift: float32 [768], replicated, may hold values from -1.75 to 1.75
- up_weight: bfloat16 [768, 3072], replicated, may hold values from -0.21875 to 0.21875
- up_bias: float32 [3072], replicated, may hold values from -1.75 to 1.75
- down_weight: bfloat16 [3072, 768], replicated, may hold values from -0.109375 to 0.109375
- down_bias: float32 [768], replicated, may hold values from -1.75 to 1.75
- ffn_gain: float32 [768], replicated, may hold values from 0.5 to 1.5
- ffn_shift: float32 [768], replicated, may hold values from -1.75 to 1.75
Outputs:
- loss: float32 [], replicated
- layer_out: bfloat16 [32768, 768], P('batch')
- tokens_grad: float32 [32768, 768], P('batch')
- qkv_weight_grad: float32 [1769472], P('batch')
- proj_weight_grad: float32 [589824], P('batch')
- up_weight_grad: float32 [2359296], P('batch')
- down_weight_grad: float32 [2359296], P('batch')
- query_bias_grad: float32 [768], replicated
- value_bias_grad: float32 [768], replicated
- proj_bias_grad: float32 [768], replicated
- attn_gain_grad: float32 [768], replicated
- attn_shift_grad: float32 [768], replicated
- up_bias_grad: float32 [3072], replicated
- down_bias_grad: float32 [768], replicated
- ffn_gain_grad: float32 [768], replicated
- ffn_shift_grad: float32 [768], replicated
The draws below stay inside these ranges and needn't reach their ends.
Inputs may be any that keep to these rules, and one draw needn't show every extreme that they name: `segment_ids`: each row holds segments 0 to 7 in this order, each of one or more tokens, followed by eight or more padding tokens of -1. `pair_index`: each segment is the positive of exactly one query and no query is its own positive.
All inputs are finite; a program needn't handle non-finite values.
Results may differ from the reference program's by a relative error of at most 0.012.
Values may be sent and summed in bfloat16 or wider, within the bound.
A program may use at most 192 MiB of HBM per device.

```python
from functools import partial
import jax
import jax.numpy as jnp
from jax import lax

D = 768
HEADS = 12
HEAD_DIM = 64
FF = 3072
SEQ_LEN = 512
SEGS = 8
SEG_DEV = 16
ROWS = 64
TOKENS = 32768
N_SEG = 512
N_BATCH = 32


def draw_segment_ids(key, part):
    key = jax.random.fold_in(key, 11)
    longest = (SEQ_LEN - 8) // SEGS
    spans = jax.random.randint(key, (ROWS, SEGS), 1, longest + 1)
    ends = jnp.cumsum(spans, axis=1)
    places = jnp.arange(SEQ_LEN, dtype=jnp.int32)
    seg_index = jnp.sum((places[None, None, :] >= ends[:, :, None]).astype(jnp.int32), axis=1)
    return jnp.where(seg_index >= SEGS, -1, seg_index).astype(jnp.int32)


def draw_pair_index(key, part):
    key = jax.random.fold_in(key, 23)
    shuffled = jax.random.permutation(key, N_SEG).astype(jnp.int32)
    follower = jnp.roll(shuffled, -1)
    return jnp.zeros((N_SEG,), jnp.int32).at[shuffled].set(follower)


def block_levels(own_key, extent, shards, smallest, largest):
    factor_of, own = 1.0, jax.random.fold_in(own_key, 6)
    for axis_at, shards_of in shards:
        steps = jnp.exp(jax.random.uniform(jax.random.fold_in(own, axis_at), (shards_of,), jnp.float32, smallest / len(shards), largest / len(shards)))
        factor_of = factor_of * jnp.repeat(steps, extent[axis_at] // shards_of).reshape([-1 if axis == axis_at else 1 for axis in range(len(extent))])
    return factor_of


def normal_values(own_key, extent, width, most, shards=(), kind=jnp.bfloat16):
    array = jax.random.normal(own_key, extent, jnp.float32) * width
    if len(shards) > 0:
        array = block_levels(own_key, extent, shards, -0.22, 0.18) * array
    return jnp.clip(array, min=-most, max=most).astype(kind)


def setup_inputs(seed: int = 0) -> dict:
    splits = jax.random.split(jax.random.key(seed), 17)
    return {
        "tokens": normal_values(splits[0], (TOKENS, D), 1.0, 6.0, ((0, 32),)),
        "segment_ids": draw_segment_ids(jax.random.fold_in(splits[16], 71), 0),
        "pair_index": draw_pair_index(jax.random.fold_in(splits[16], 71), 0),
        "qkv_weight": normal_values(splits[3], (D, 3 * D), D ** -0.5, 0.21875),
        "query_bias": normal_values(splits[4], (D,), 0.3, 1.75, (), jnp.float32),
        "value_bias": normal_values(splits[5], (D,), 0.3, 1.75, (), jnp.float32),
        "proj_weight": normal_values(splits[6], (D, D), (D // 16) ** -0.5, 0.875),
        "proj_bias": normal_values(splits[7], (D,), 0.3, 1.75, (), jnp.float32),
        "attn_gain": jnp.clip(1.0 + 0.1 * jax.random.normal(splits[8], (D,), jnp.float32), 0.5, 1.5),
        "attn_shift": normal_values(splits[9], (D,), 0.3, 1.75, (), jnp.float32),
        "up_weight": normal_values(splits[10], (D, FF), D ** -0.5, 0.21875),
        "up_bias": normal_values(splits[11], (FF,), 0.3, 1.75, (), jnp.float32),
        "down_weight": normal_values(splits[12], (FF, D), FF ** -0.5, 0.109375),
        "down_bias": normal_values(splits[13], (D,), 0.3, 1.75, (), jnp.float32),
        "ffn_gain": jnp.clip(1.0 + 0.1 * jax.random.normal(splits[14], (D,), jnp.float32), 0.5, 1.5),
        "ffn_shift": normal_values(splits[15], (D,), 0.3, 1.75, (), jnp.float32),
    }


@jax.custom_vjp
def low(v):
    return lax.optimization_barrier(v.astype(jnp.bfloat16)).astype(jnp.float32)

@jax.custom_vjp
def low_back(v):
    return v

def low_keep(v):
    return (low(v), None)

def low_pass(kept, grad):
    return (grad,)

def back_keep(v):
    return (v, None)

def back_low(kept, grad):
    return (low(grad),)
low.defvjp(low_keep, low_pass)
low_back.defvjp(back_keep, back_low)
inv_temp = 100.0
ln_eps = 1e-12
norm_eps = 1e-06
neg_fill = -1000000000.0

def hi_dot(left, right):
    return jnp.dot(left, right, precision=lax.Precision.HIGHEST)

def layer_norm(resid, gain, shift):
    average = lax.optimization_barrier(jnp.mean(resid, axis=-1, keepdims=True))
    centred = resid - average
    variance = lax.optimization_barrier(jnp.mean(centred * centred, axis=-1, keepdims=True))
    return centred * lax.rsqrt(variance + ln_eps) * gain + shift

def encode_row(params, entry):
    qkv_weight, query_bias, value_bias, proj_weight, proj_bias, attn_gain, attn_shift, up_weight, up_bias, down_weight, down_bias, ffn_gain, ffn_shift = params
    row_tokens, row_ids = entry
    row_len = row_tokens.shape[0]
    bias_full = jnp.concatenate([query_bias, jnp.zeros_like(query_bias), value_bias])
    qkv_all = low(low_back(hi_dot(row_tokens, qkv_weight) + bias_full))
    split_qkv = qkv_all.reshape(row_len, 3, HEADS, HEAD_DIM)
    scores = low_back(jnp.einsum('qhd,khd->hqk', split_qkv[:, 0], split_qkv[:, 1], precision=lax.Precision.HIGHEST) * HEAD_DIM ** (-0.5))
    same_segment = row_ids[:, None] == row_ids[None, :]
    masked = jnp.where(same_segment[None], scores, neg_fill)
    peak_val = lax.optimization_barrier(jnp.max(masked, axis=-1, keepdims=True))
    exponent = jnp.exp(masked - peak_val)
    attn_probs = low(exponent / lax.optimization_barrier(jnp.sum(exponent, axis=-1, keepdims=True)))
    context = low(low_back(jnp.einsum('hqk,khd->qhd', attn_probs, split_qkv[:, 2], precision=lax.Precision.HIGHEST)))
    context = context.reshape(row_len, HEADS * HEAD_DIM)
    attended = low_back(hi_dot(context, proj_weight) + proj_bias)
    first_norm = layer_norm(row_tokens + attended, attn_gain, attn_shift)
    up_pre = low_back(hi_dot(low(first_norm), up_weight) + up_bias)
    down_out = low_back(hi_dot(low(jax.nn.gelu(up_pre, approximate=False)), down_weight) + down_bias)
    return layer_norm(first_norm + down_out, ffn_gain, ffn_shift)

def forward(segment_ids, pair_index, tokens_all, params):
    row_tokens = tokens_all.reshape(ROWS, SEQ_LEN, D)
    outputs = lax.map(jax.checkpoint(partial(encode_row, params)), (row_tokens, segment_ids))
    outputs = outputs.reshape(TOKENS, D)
    row_base = (jnp.arange(ROWS, dtype=jnp.int32) * SEGS)[:, None]
    global_ids = jnp.where(segment_ids >= 0, segment_ids + row_base, N_SEG).astype(jnp.int32).reshape(TOKENS)
    sums = jax.ops.segment_sum(outputs, global_ids, num_segments=N_SEG + 1)[:N_SEG]
    counts = jax.ops.segment_sum(jnp.ones((TOKENS,), jnp.float32), global_ids, num_segments=N_SEG + 1)[:N_SEG]
    pooled = sums / counts[:, None]
    embedding = low(pooled * lax.rsqrt(lax.optimization_barrier(jnp.sum(pooled * pooled, axis=1, keepdims=True)) + norm_eps))
    blocks = embedding.reshape(N_BATCH, SEG_DEV, D)
    starts = jnp.arange(N_BATCH, dtype=jnp.int32) * SEG_DEV
    pair_blocks = pair_index.reshape(N_BATCH, SEG_DEV)
    columns = jnp.arange(N_SEG, dtype=jnp.int32)

    def block_loss(entry):
        queries, start_row, pairs = entry
        contrast = low_back(hi_dot(queries, embedding.T) * inv_temp)
        own_rows = start_row + jnp.arange(SEG_DEV, dtype=jnp.int32)
        masked = jnp.where(columns[None, :] == own_rows[:, None], neg_fill, contrast)
        peak_val = lax.optimization_barrier(jnp.max(masked, axis=1, keepdims=True))
        log_norm = peak_val[:, 0] + jnp.log(lax.optimization_barrier(jnp.sum(jnp.exp(masked - peak_val), axis=1)))
        positive = lax.optimization_barrier(jnp.sum(jnp.where(columns[None, :] == pairs[:, None], contrast, 0.0), axis=1))
        return jnp.sum(log_norm - positive)
    terms = lax.map(jax.checkpoint(block_loss), (blocks, starts, pair_blocks))
    return (outputs, jnp.sum(terms))

def reference(tokens, segment_ids, pair_index, qkv_weight, query_bias, value_bias, proj_weight, proj_bias, attn_gain, attn_shift, up_weight, up_bias, down_weight, down_bias, ffn_gain, ffn_shift):
    params = (qkv_weight.astype(jnp.float32), query_bias, value_bias, proj_weight.astype(jnp.float32), proj_bias, attn_gain, attn_shift, up_weight.astype(jnp.float32), up_bias, down_weight.astype(jnp.float32), down_bias, ffn_gain, ffn_shift)
    tokens_all = tokens.astype(jnp.float32)
    (outputs, loss_sum), pullback = jax.vjp(partial(forward, segment_ids, pair_index), tokens_all, params)
    tokens_grad, grads = pullback((jnp.zeros_like(outputs), jnp.ones_like(loss_sum)))
    return (loss_sum / N_SEG, outputs.astype(jnp.bfloat16), tokens_grad, grads[0].reshape(-1), grads[3].reshape(-1), grads[7].reshape(-1), grads[9].reshape(-1), grads[1], grads[2], grads[4], grads[5], grads[6], grads[8], grads[10], grads[11], grads[12])
```

```python
import functools
import jax
import jax.numpy as jnp
from jax import lax
from jax.experimental import pallas as pl
from jax.experimental.pallas import tpu as pltpu

F32 = jnp.float32
BF16 = jnp.bfloat16
HEADS = 12
HEAD_DIM = 64
SEGS = 8
PAIR = 2 * HEAD_DIM
LN_EPS = 1e-12
NORM_EPS = 1e-06
MIB = 2**20


def dot_nn(a, b):
    return lax.dot_general(a, b, (((1,), (0,)), ((), ())), preferred_element_type=F32)


def dot_nt(a, b):
    return lax.dot_general(a, b, (((1,), (1,)), ((), ())), preferred_element_type=F32)


def dot_tn(a, b):
    return lax.dot_general(a, b, (((0,), (0,)), ((), ())), preferred_element_type=F32)


def gelu_parts(pre):
    half = 0.5 * pre
    cdf = 0.5 + 0.5 * lax.erf(pre * 0.7071067811865476)
    pdf = jnp.exp(-half * pre) * 0.3989422804014327
    return pre * cdf, cdf + pre * pdf


def normalize(resid):
    width = resid.shape[-1]
    average = jnp.sum(resid, axis=-1, keepdims=True) * (1.0 / width)
    centred = resid - average
    variance = jnp.sum(centred * centred, axis=-1, keepdims=True) * (1.0 / width)
    inv_std = lax.rsqrt(variance + LN_EPS)
    return centred * inv_std, inv_std


def forward_kernel(
    ids_ref, qb_ref, vb_ref, pb_ref, ag_ref, as_ref, ub_ref, db_ref, fg_ref, fs_ref,
    tok_hbm, wqkv_hbm, wp_hbm, wu_hbm, wd_hbm,
    exp_hbm, qkv_hbm, ctx_hbm, rinv_hbm, n1_hbm, low_hbm, act_hbm, der_hbm, n2_hbm, out_hbm,
    inv1_ref, inv2_ref, emb_ref, z_ref, invn_ref, cnt_ref,
    tok_s, wqkv_s, wp_s, wu_s, wd_s, qkv_s, ctx_s, rinv_s, bias_s, exp_s,
    n1_s, low_s, act_s, der_s, n2_s, out_s, in_sem, out_sem, exp_sem,
):
    rows, row_len = ids_ref.shape
    toks, width = tok_s.shape
    pairs = width // PAIR
    ff = wu_s.shape[1]

    loads = [
        pltpu.make_async_copy(src, dst, in_sem.at[i])
        for i, (src, dst) in enumerate(
            [(tok_hbm, tok_s), (wqkv_hbm, wqkv_s), (wp_hbm, wp_s), (wu_hbm, wu_s), (wd_hbm, wd_s)]
        )
    ]
    for cp in loads:
        cp.start()
    loads[0].wait()
    loads[1].wait()

    tok = tok_s[...]
    blk = 256
    for j in range(3 * width // blk):
        piece = dot_nn(tok, wqkv_s[:, j * blk : (j + 1) * blk])
        third, off = divmod(j * blk, width)
        if third == 0:
            piece = piece + qb_ref[:, off : off + blk]
        elif third == 2:
            piece = piece + vb_ref[:, off : off + blk]
        qkv_s[:, j * blk : (j + 1) * blk] = piece.astype(BF16)
    qkv_out = pltpu.make_async_copy(qkv_s, qkv_hbm, out_sem.at[0])
    qkv_out.start()

    lane = lax.broadcasted_iota(jnp.int32, (row_len, PAIR), 1)
    first = lane < HEAD_DIM
    ones = jnp.ones((row_len, PAIR), BF16)

    for r in range(rows):
        ids_row = ids_ref[r : r + 1, :].astype(F32)
        ids_col = jnp.transpose(jnp.broadcast_to(ids_row, (128, row_len)))
        for c in range(row_len // 128):
            bias_s[r, :, c * 128 : (c + 1) * 128] = jnp.where(
                ids_col == ids_row[:, c * 128 : (c + 1) * 128], 0.0, -1e9
            )

    def attend(it, carry):
        r = it // pairs
        p = it % pairs
        rsl = pl.ds(pl.multiple_of(r * row_len, row_len), row_len)
        col = lambda third: pl.ds(pl.multiple_of(third * width + p * PAIR, PAIR), PAIR)
        q = qkv_s[rsl, col(0)] * jnp.asarray(HEAD_DIM**-0.5, BF16)
        k = qkv_s[rsl, col(1)]
        v = jnp.concatenate([qkv_s[rsl, col(2)], ones], axis=1)
        slot = lax.rem(it, 2)

        @pl.when(it >= 2)
        def _():
            pltpu.make_async_copy(exp_s.at[slot], exp_hbm.at[it], exp_sem.at[slot]).wait()

        parts = []
        for h in range(2):
            qh = jnp.where(first if h == 0 else ~first, q, jnp.zeros_like(q))
            s = dot_nt(qh, k) + bias_s[r]
            e = jnp.exp(s - jnp.max(s, axis=1, keepdims=True)).astype(BF16)
            exp_s[slot, h] = e
            oe = dot_nn(e, v)
            rinv = 1.0 / oe[:, PAIR:]
            parts.append((oe[:, :PAIR] * rinv, rinv))
        ctx_s[rsl, pl.ds(pl.multiple_of(p * PAIR, PAIR), PAIR)] = jnp.where(
            first, parts[0][0], parts[1][0]
        ).astype(BF16)
        rinv_s[rsl, pl.ds(pl.multiple_of(p * PAIR, PAIR), PAIR)] = jnp.where(
            first, parts[0][1], parts[1][1]
        )
        pltpu.make_async_copy(exp_s.at[slot], exp_hbm.at[it], exp_sem.at[slot]).start()
        return carry

    lax.fori_loop(0, rows * pairs, attend, 0)
    ctx_out = pltpu.make_async_copy(ctx_s, ctx_hbm, out_sem.at[1])
    ctx_out.start()
    rinv_out = pltpu.make_async_copy(rinv_s, rinv_hbm, out_sem.at[2])
    rinv_out.start()
    for cp in loads[2:]:
        cp.wait()

    outs = [(n1_s, n1_hbm), (low_s, low_hbm), (act_s, act_hbm), (der_s, der_hbm), (n2_s, n2_hbm), (out_s, out_hbm)]

    def ffn(r, carry):
        rsl = pl.ds(pl.multiple_of(r * row_len, row_len), row_len)
        resid = tok_s[rsl, :].astype(F32) + (dot_nn(ctx_s[rsl, :], wp_s[...]) + pb_ref[...])
        normed, inv_std = normalize(resid)
        n1_s[rsl, :] = normed
        inv1_ref[rsl, :] = jnp.broadcast_to(inv_std, (row_len, 128))
        first_norm = normed * ag_ref[...] + as_ref[...]
        low = first_norm.astype(BF16)
        low_s[rsl, :] = low
        for j in range(ff // blk):
            pre = dot_nn(low, wu_s[:, j * blk : (j + 1) * blk]) + ub_ref[:, j * blk : (j + 1) * blk]
            act, der = gelu_parts(pre)
            act_s[rsl, j * blk : (j + 1) * blk] = act.astype(BF16)
            der_s[rsl, j * blk : (j + 1) * blk] = der.astype(BF16)
        down = dot_nn(act_s[rsl, :], wd_s[...]) + db_ref[...]
        normed2, inv_std2 = normalize(first_norm + down)
        n2_s[rsl, :] = normed2
        inv2_ref[rsl, :] = jnp.broadcast_to(inv_std2, (row_len, 128))
        y = normed2 * fg_ref[...] + fs_ref[...]
        high = y.astype(BF16)
        out_s[rsl, :] = high
        rest = (y - high.astype(F32)).astype(BF16)
        seg = lax.broadcasted_iota(jnp.int32, (SEGS, row_len), 0)
        member = (seg == ids_ref[pl.ds(r, 1), :]).astype(F32)
        count = jnp.sum(member, axis=1, keepdims=True)
        member = member.astype(BF16)
        pooled = (dot_nn(member, high) + dot_nn(member, rest)) / count
        inv_norm = lax.rsqrt(jnp.sum(pooled * pooled, axis=1, keepdims=True) + NORM_EPS)
        z = pooled * inv_norm
        ssl = pl.ds(pl.multiple_of(r * SEGS, SEGS), SEGS)
        z_ref[ssl, :] = z
        invn_ref[ssl, :] = jnp.broadcast_to(inv_norm, (SEGS, 128))
        cnt_ref[ssl, :] = jnp.broadcast_to(count, (SEGS, 128))
        for i, (src, dst) in enumerate(outs):
            pltpu.make_async_copy(src.at[rsl, :], dst.at[rsl, :], out_sem.at[3 + i]).start()
        return carry

    lax.fori_loop(0, rows, ffn, 0)
    emb_ref[...] = z_ref[...].astype(BF16)
    for i, (src, dst) in enumerate(outs):
        pltpu.make_async_copy(src, dst, out_sem.at[3 + i]).wait()
    qkv_out.wait()
    ctx_out.wait()
    rinv_out.wait()
    for slot in range(2):
        pltpu.make_async_copy(exp_s.at[slot], exp_hbm.at[0], exp_sem.at[slot]).wait()


def forward_call(tokens, ids, wqkv, qb, vb, wp, pb, ag, ash, wu, ub, wd, db, fg, fs):
    toks, width = tokens.shape
    rows, row_len = ids.shape
    ff = wu.shape[1]
    pairs = width // PAIR
    segs = rows * SEGS
    sds = jax.ShapeDtypeStruct
    row = lambda v: v.reshape(1, -1)
    vm = pl.BlockSpec(memory_space=pltpu.VMEM)
    hb = pl.BlockSpec(memory_space=pl.ANY)
    return pl.pallas_call(
        forward_kernel,
        out_shape=(
            sds((rows * pairs, 2, row_len, row_len), BF16),
            sds((toks, 3 * width), BF16),
            sds((toks, width), BF16),
            sds((toks, width), F32),
            sds((toks, width), F32),
            sds((toks, width), BF16),
            sds((toks, ff), BF16),
            sds((toks, ff), BF16),
            sds((toks, width), F32),
            sds((toks, width), BF16),
            sds((toks, 128), F32),
            sds((toks, 128), F32),
            sds((segs, width), BF16),
            sds((segs, width), F32),
            sds((segs, 128), F32),
            sds((segs, 128), F32),
        ),
        in_specs=[vm] * 10 + [hb] * 5,
        out_specs=[hb] * 10 + [vm] * 6,
        scratch_shapes=[
            pltpu.VMEM((toks, width), BF16),
            pltpu.VMEM(wqkv.shape, BF16),
            pltpu.VMEM(wp.shape, BF16),
            pltpu.VMEM(wu.shape, BF16),
            pltpu.VMEM(wd.shape, BF16),
            pltpu.VMEM((toks, 3 * width), BF16),
            pltpu.VMEM((toks, width), BF16),
            pltpu.VMEM((toks, width), F32),
            pltpu.VMEM((rows, row_len, row_len), F32),
            pltpu.VMEM((2, 2, row_len, row_len), BF16),
            pltpu.VMEM((toks, width), F32),
            pltpu.VMEM((toks, width), BF16),
            pltpu.VMEM((toks, ff), BF16),
            pltpu.VMEM((toks, ff), BF16),
            pltpu.VMEM((toks, width), F32),
            pltpu.VMEM((toks, width), BF16),
            pltpu.SemaphoreType.DMA((5,)),
            pltpu.SemaphoreType.DMA((9,)),
            pltpu.SemaphoreType.DMA((2,)),
        ],
        compiler_params=pltpu.CompilerParams(vmem_limit_bytes=60 * MIB),
        name="forward",
    )(ids, row(qb), row(vb), row(pb), row(ag), row(ash), row(ub), row(db), row(fg), row(fs), tokens, wqkv, wp, wu, wd)


MESH = pl.DeviceIdType.MESH
INV_TEMP = 100.0
NEG = -1000000000.0


def axis_groups(n):
    groups = []
    rest = n // 2
    while rest > 1:
        size = 4 if rest % 4 == 0 else (2 if rest % 2 == 0 else rest)
        groups.append(size)
        rest //= size
    return groups + [2]


def digits_of(me, groups):
    digits = []
    for size in reversed(groups):
        digits.append(lax.rem(me, size))
        me = me // size
    return digits[::-1]


def index_of(digits, groups):
    me = 0
    for digit, size in zip(digits, groups):
        me = me * size + digit
    return me


def contrast_kernel(groups, msg_ref, z_ref, invn_ref, cnt_ref, loss_ref, gp_ref, all_s, send_sem, recv_sem):
    n = 1
    for size in groups:
        n *= size
    me = lax.axis_index("batch")
    mine = digits_of(me, groups)
    seg_here, wide = msg_ref.shape
    width = z_ref.shape[1]
    total = n * seg_here
    stages = len(groups)

    def peer(stage, step):
        other = lax.rem(mine[stage] + step, groups[stage])
        return other, index_of(mine[:stage] + [other] + mine[stage + 1 :], groups)

    barrier = pltpu.get_barrier_semaphore()
    hops = 0
    for stage in range(stages):
        for step in range(1, groups[stage]):
            pl.semaphore_signal(barrier, inc=1, device_id=(peer(stage, step)[1],), device_id_type=MESH)
            hops += 1
    all_s[tuple(mine)] = msg_ref[...]
    pl.semaphore_wait(barrier, hops)

    slot = 0
    for stage in range(stages):
        copies = []
        for step in range(1, groups[stage]):
            block = all_s.at[(slice(None),) * stage + tuple(mine[stage:])]
            copies.append(
                pltpu.make_async_remote_copy(
                    src_ref=block,
                    dst_ref=block,
                    send_sem=send_sem.at[slot],
                    recv_sem=recv_sem.at[slot],
                    device_id=(peer(stage, step)[1],),
                    device_id_type=MESH,
                )
            )
            slot += 1
        for cp in copies:
            cp.start()
        for cp in copies:
            cp.wait()

    every = all_s[...].reshape(total, wide)
    emb = every[:, :width]
    own = msg_ref[:, :width]
    z = z_ref[...]
    own_row = (me * seg_here).astype(F32)
    own_pair = msg_ref[:, width : width + 128].astype(F32)
    own_pair = own_pair[:, 0:1] * 256.0 + own_pair[:, 1:2]

    scores = dot_nt(own, emb) * INV_TEMP
    column = lax.broadcasted_iota(jnp.int32, scores.shape, 1).astype(F32)
    row = lax.broadcasted_iota(jnp.int32, scores.shape, 0).astype(F32) + own_row
    masked = jnp.where(column == row, NEG, scores)
    peak = jnp.max(masked, axis=1, keepdims=True)
    log_norm = peak + jnp.log(jnp.sum(jnp.exp(masked - peak), axis=1, keepdims=True))
    weight = jnp.exp(masked - log_norm) - (column == own_pair).astype(F32)
    grad = dot_nn(weight.astype(BF16), emb)

    blk = min(total, 512)
    loss = jnp.zeros((1, 1), F32)
    for b in range(total // blk):
        part = emb[b * blk : (b + 1) * blk]
        pair = every[b * blk : (b + 1) * blk, width:].astype(F32)
        pair = pair[:, 0:1] * 256.0 + pair[:, 1:2]
        scores = dot_nt(part, emb) * INV_TEMP
        column = lax.broadcasted_iota(jnp.int32, scores.shape, 1).astype(F32)
        row = lax.broadcasted_iota(jnp.int32, scores.shape, 0).astype(F32) + float(b * blk)
        masked = jnp.where(column == row, NEG, scores)
        peak = jnp.max(masked, axis=1, keepdims=True)
        log_norm = peak + jnp.log(jnp.sum(jnp.exp(masked - peak), axis=1, keepdims=True))
        positive = jnp.sum(jnp.where(column == pair, scores, 0.0), axis=1, keepdims=True)
        loss = loss + jnp.sum(log_norm - positive, axis=0, keepdims=True)
        scores = dot_nt(part, own) * INV_TEMP
        column = lax.broadcasted_iota(jnp.int32, scores.shape, 1).astype(F32) + own_row
        row = lax.broadcasted_iota(jnp.int32, scores.shape, 0).astype(F32) + float(b * blk)
        weight = jnp.where(column == row, 0.0, jnp.exp(jnp.where(column == row, NEG, scores) - log_norm))
        weight = weight - (column == pair).astype(F32)
        grad = grad + dot_tn(weight.astype(BF16), part)
    loss_ref[...] = jnp.broadcast_to(loss * (1.0 / total), loss_ref.shape)
    grad = grad * INV_TEMP
    pooled_grad = invn_ref[:, 0:1] * (grad - z * jnp.sum(grad * z, axis=1, keepdims=True))
    gp_ref[...] = pooled_grad / cnt_ref[:, 0:1]


def contrast_call(n, emb_low, z, invn, cnt, pair_index):
    groups = axis_groups(n)
    seg_here, width = emb_low.shape
    high = (pair_index // 256).astype(BF16)[:, None]
    rest = (pair_index % 256).astype(BF16)[:, None]
    msg = jnp.concatenate([emb_low, high, rest, jnp.zeros((seg_here, 126), BF16)], axis=1)
    copies = sum(size - 1 for size in groups)
    vm = pl.BlockSpec(memory_space=pltpu.VMEM)
    return pl.pallas_call(
        functools.partial(contrast_kernel, groups),
        out_shape=(jax.ShapeDtypeStruct((8, 128), F32), jax.ShapeDtypeStruct((seg_here, width), F32)),
        in_specs=[vm] * 4,
        out_specs=[vm] * 2,
        scratch_shapes=[
            pltpu.VMEM(tuple(groups) + msg.shape, BF16),
            pltpu.SemaphoreType.DMA((copies,)),
            pltpu.SemaphoreType.DMA((copies,)),
        ],
        compiler_params=pltpu.CompilerParams(collective_id=0, has_side_effects=True, vmem_limit_bytes=56 * MIB),
        name="contrast",
    )(msg, z, invn, cnt)

from jax.sharding import PartitionSpec as P


def norm_back(grad_out, normed, inv_std, gain):
    grad_n = grad_out * gain
    return inv_std * (
        grad_n
        - jnp.mean(grad_n, axis=-1, keepdims=True)
        - normed * jnp.mean(grad_n * normed, axis=-1, keepdims=True)
    )


def attend_back(entry):
    qkv_row, exps, rinv, ctx, grad_row = entry
    row_len = qkv_row.shape[0]
    split = qkv_row.reshape(row_len, 3, HEADS, HEAD_DIM)
    queries, key_vecs, values = split[:, 0], split[:, 1], split[:, 2]
    exps = exps.reshape(HEADS, row_len, row_len)
    scaled = (grad_row.astype(F32) * rinv).astype(BF16)
    delta = jnp.sum(scaled.astype(F32).reshape(row_len, HEADS, HEAD_DIM) * ctx.astype(F32).reshape(row_len, HEADS, HEAD_DIM), axis=-1)
    scaled = scaled.reshape(row_len, HEADS, HEAD_DIM)
    grad_probs = jnp.einsum("qhd,khd->hqk", scaled, values, preferred_element_type=F32)
    grad_values = jnp.einsum("hqk,qhd->khd", exps, scaled, preferred_element_type=F32)
    grad_scores = (exps.astype(F32) * (grad_probs - delta.T[..., None])).astype(BF16)
    grad_queries = jnp.einsum("hqk,khd->qhd", grad_scores, key_vecs, preferred_element_type=F32) * HEAD_DIM**-0.5
    grad_keys = jnp.einsum("hqk,qhd->khd", grad_scores, queries, preferred_element_type=F32) * HEAD_DIM**-0.5
    stacked = jnp.stack([grad_queries, grad_keys, grad_values], axis=1)
    return stacked.reshape(row_len, 3 * HEADS * HEAD_DIM).astype(BF16)


def per_device(
    tokens, segment_ids, pair_index, qkv_weight, query_bias, value_bias, proj_weight, proj_bias,
    attn_gain, attn_shift, up_weight, up_bias, down_weight, down_bias, ffn_gain, ffn_shift,
):
    n = lax.axis_size("batch")
    rows, row_len = segment_ids.shape
    toks, width = tokens.shape
    (exps, qkv, context, rinv, normed_one, first_low, acted, deriv, normed_two, layer_out,
     inv_one, inv_two, emb_low, z, invn, cnt) = forward_call(
        tokens, segment_ids, qkv_weight, query_bias, value_bias, proj_weight, proj_bias, attn_gain, attn_shift,
        up_weight, up_bias, down_weight, down_bias, ffn_gain, ffn_shift)
    loss, grad_seg = contrast_call(n, emb_low, z, invn, cnt, pair_index)
    inv_one = inv_one[:, :1]
    inv_two = inv_two[:, :1]
    row_base = (jnp.arange(rows, dtype=jnp.int32) * SEGS)[:, None]
    local_ids = jnp.where(segment_ids >= 0, segment_ids + row_base, -1).reshape(toks)
    member = (local_ids[None, :] == jnp.arange(rows * SEGS, dtype=jnp.int32)[:, None]).astype(F32)
    grad_y = lax.dot_general(member, grad_seg, (((0,), (0,)), ((), ())), precision=lax.Precision.HIGHEST)
    ffn_gain_part = jnp.sum(grad_y * normed_two, axis=0)
    ffn_shift_part = jnp.sum(grad_y, axis=0)
    grad_r2 = norm_back(grad_y, normed_two, inv_two, ffn_gain)
    grad_down_low = grad_r2.astype(BF16)
    down_bias_part = jnp.sum(grad_down_low.astype(F32), axis=0)
    down_weight_part = dot_tn(acted, grad_down_low)
    grad_up_low = (dot_nt(grad_down_low, down_weight) * deriv.astype(F32)).astype(BF16)
    up_bias_part = jnp.sum(grad_up_low.astype(F32), axis=0)
    up_weight_part = dot_tn(first_low, grad_up_low)
    grad_first = grad_r2 + dot_nt(grad_up_low, up_weight)
    attn_gain_part = jnp.sum(grad_first * normed_one, axis=0)
    attn_shift_part = jnp.sum(grad_first, axis=0)
    grad_r1 = norm_back(grad_first, normed_one, inv_one, attn_gain)
    grad_att_low = grad_r1.astype(BF16)
    proj_bias_part = jnp.sum(grad_att_low.astype(F32), axis=0)
    proj_weight_part = dot_tn(context, grad_att_low)
    grad_context = dot_nt(grad_att_low, proj_weight).astype(BF16)
    by_row = lambda v: v.reshape(rows, row_len, -1)
    grad_qkv = lax.map(
        attend_back,
        (by_row(qkv), exps.reshape(rows, -1, 2, row_len, row_len), by_row(rinv), by_row(context), by_row(grad_context)),
    ).reshape(toks, 3 * width)
    qkv_bias_part = jnp.sum(grad_qkv.astype(F32), axis=0)
    qkv_weight_part = dot_tn(tokens, grad_qkv)
    tokens_grad = grad_r1 + dot_nt(grad_qkv, qkv_weight)
    scatter = lambda v: lax.psum_scatter(v.reshape(-1), "batch", scatter_dimension=0, tiled=True)
    sums = lax.psum(
        (qkv_bias_part[:width], qkv_bias_part[2 * width :], proj_bias_part, attn_gain_part, attn_shift_part,
         up_bias_part, down_bias_part, ffn_gain_part, ffn_shift_part),
        "batch",
    )
    return (loss[0, 0], layer_out, tokens_grad, scatter(qkv_weight_part), scatter(proj_weight_part),
            scatter(up_weight_part), scatter(down_weight_part)) + tuple(sums)


def solution(mesh):
    split, whole = P("batch"), P()
    return jax.shard_map(
        per_device,
        mesh=mesh,
        in_specs=(P("batch", None), P("batch", None), split) + (whole,) * 13,
        out_specs=(whole, P("batch", None), P("batch", None)) + (split,) * 4 + (whole,) * 9,
        check_vma=False,
    )
```

```python
import functools
import jax
import jax.numpy as jnp
from jax import lax
from jax.experimental import pallas as pl
from jax.experimental.pallas import tpu as pltpu
from jax.sharding import PartitionSpec as P

F32 = jnp.float32
BF16 = jnp.bfloat16
HEADS = 12
HEAD_DIM = 64
SEGS = 8
PAIR = 2 * HEAD_DIM
LN_EPS = 1e-12
NORM_EPS = 1e-06
MIB = 2**20


def dot_nn(a, b):
    return lax.dot_general(a, b, (((1,), (0,)), ((), ())), preferred_element_type=F32)


def dot_nt(a, b):
    return lax.dot_general(a, b, (((1,), (1,)), ((), ())), preferred_element_type=F32)


def dot_tn(a, b):
    return lax.dot_general(a, b, (((0,), (0,)), ((), ())), preferred_element_type=F32)


def gelu_parts(pre):
    half = 0.5 * pre
    cdf = 0.5 + 0.5 * lax.erf(pre * 0.7071067811865476)
    pdf = jnp.exp(-half * pre) * 0.3989422804014327
    return pre * cdf, cdf + pre * pdf


def normalize(resid):
    width = resid.shape[-1]
    average = jnp.sum(resid, axis=-1, keepdims=True) * (1.0 / width)
    centred = resid - average
    variance = jnp.sum(centred * centred, axis=-1, keepdims=True) * (1.0 / width)
    inv_std = lax.rsqrt(variance + LN_EPS)
    return centred * inv_std, inv_std


def forward_kernel(
    ids_ref, qb_ref, vb_ref, pb_ref, ag_ref, as_ref, ub_ref, db_ref, fg_ref, fs_ref,
    tok_hbm, wqkv_hbm, wp_hbm, wu_hbm, wd_hbm,
    exp_hbm, qkv_hbm, ctx_hbm, rinv_hbm, n1_hbm, low_hbm, act_hbm, der_hbm, n2_hbm, out_hbm,
    inv1_ref, inv2_ref, emb_ref, z_ref, invn_ref, cnt_ref,
    tok_s, wqkv_s, wp_s, wu_s, wd_s, qkv_s, ctx_s, rinv_s, bias_s, exp_s,
    n1_s, low_s, act_s, der_s, n2_s, out_s, in_sem, out_sem, exp_sem,
):
    rows, row_len = ids_ref.shape
    toks, width = tok_s.shape
    pairs = width // PAIR
    ff = wu_s.shape[1]
    qb, vb, pb, ag, ash, db, fg, fs = (
        ref[...].reshape(1, width) for ref in (qb_ref, vb_ref, pb_ref, ag_ref, as_ref, db_ref, fg_ref, fs_ref)
    )
    ub = ub_ref[...].reshape(1, ff)

    loads = [
        pltpu.make_async_copy(src, dst, in_sem.at[i])
        for i, (src, dst) in enumerate(
            [(tok_hbm, tok_s), (wqkv_hbm, wqkv_s), (wp_hbm, wp_s), (wu_hbm, wu_s), (wd_hbm, wd_s)]
        )
    ]
    for cp in loads:
        cp.start()
    loads[0].wait()
    loads[1].wait()

    tok = tok_s[...]
    blk = 256
    for j in range(3 * width // blk):
        piece = dot_nn(tok, wqkv_s[:, j * blk : (j + 1) * blk])
        third, off = divmod(j * blk, width)
        if third == 0:
            piece = piece + qb[:, off : off + blk]
        elif third == 2:
            piece = piece + vb[:, off : off + blk]
        qkv_s[:, j * blk : (j + 1) * blk] = piece.astype(BF16)
    qkv_out = pltpu.make_async_copy(qkv_s, qkv_hbm, out_sem.at[0])
    qkv_out.start()

    lane = lax.broadcasted_iota(jnp.int32, (row_len, PAIR), 1)
    first = lane < HEAD_DIM
    ones = jnp.ones((row_len, PAIR), BF16)

    for r in range(rows):
        ids_row = ids_ref[r : r + 1, :].astype(F32)
        ids_col = jnp.transpose(jnp.broadcast_to(ids_row, (128, row_len)))
        for c in range(row_len // 128):
            bias_s[r, :, c * 128 : (c + 1) * 128] = jnp.where(
                ids_col == ids_row[:, c * 128 : (c + 1) * 128], 0.0, -1e9
            )

    def attend(it, carry):
        r = it // pairs
        p = it % pairs
        rsl = pl.ds(pl.multiple_of(r * row_len, row_len), row_len)
        col = lambda third: pl.ds(pl.multiple_of(third * width + p * PAIR, PAIR), PAIR)
        q = qkv_s[rsl, col(0)] * jnp.asarray(HEAD_DIM**-0.5, BF16)
        k = qkv_s[rsl, col(1)]
        v = jnp.concatenate([qkv_s[rsl, col(2)], ones], axis=1)
        slot = lax.rem(it, 2)

        @pl.when(it >= 2)
        def _():
            pltpu.make_async_copy(exp_s.at[slot], exp_hbm.at[it], exp_sem.at[slot]).wait()

        parts = []
        for h in range(2):
            qh = jnp.where(first if h == 0 else ~first, q, jnp.zeros_like(q))
            s = dot_nt(qh, k) + bias_s[r]
            e = jnp.exp(s - jnp.max(s, axis=1, keepdims=True)).astype(BF16)
            exp_s[slot, h] = e
            oe = dot_nn(e, v)
            rinv = 1.0 / oe[:, PAIR:]
            parts.append((oe[:, :PAIR] * rinv, rinv))
        ctx_s[rsl, pl.ds(pl.multiple_of(p * PAIR, PAIR), PAIR)] = jnp.where(
            first, parts[0][0], parts[1][0]
        ).astype(BF16)
        rinv_s[rsl, pl.ds(pl.multiple_of(p * PAIR, PAIR), PAIR)] = jnp.where(
            first, parts[0][1], parts[1][1]
        )
        pltpu.make_async_copy(exp_s.at[slot], exp_hbm.at[it], exp_sem.at[slot]).start()
        return carry

    lax.fori_loop(0, rows * pairs, attend, 0)
    ctx_out = pltpu.make_async_copy(ctx_s, ctx_hbm, out_sem.at[1])
    ctx_out.start()
    rinv_out = pltpu.make_async_copy(rinv_s, rinv_hbm, out_sem.at[2])
    rinv_out.start()
    for cp in loads[2:]:
        cp.wait()

    outs = [(n1_s, n1_hbm), (low_s, low_hbm), (act_s, act_hbm), (der_s, der_hbm), (n2_s, n2_hbm), (out_s, out_hbm)]

    def ffn(r, carry):
        rsl = pl.ds(pl.multiple_of(r * row_len, row_len), row_len)
        resid = tok_s[rsl, :].astype(F32) + (dot_nn(ctx_s[rsl, :], wp_s[...]) + pb)
        normed, inv_std = normalize(resid)
        n1_s[rsl, :] = normed
        inv1_ref[rsl, :] = jnp.broadcast_to(inv_std, (row_len, 128))
        first_norm = normed * ag + ash
        low = first_norm.astype(BF16)
        low_s[rsl, :] = low
        for j in range(ff // blk):
            pre = dot_nn(low, wu_s[:, j * blk : (j + 1) * blk]) + ub[:, j * blk : (j + 1) * blk]
            act, der = gelu_parts(pre)
            act_s[rsl, j * blk : (j + 1) * blk] = act.astype(BF16)
            der_s[rsl, j * blk : (j + 1) * blk] = der.astype(BF16)
        down = dot_nn(act_s[rsl, :], wd_s[...]) + db
        normed2, inv_std2 = normalize(first_norm + down)
        n2_s[rsl, :] = normed2
        inv2_ref[rsl, :] = jnp.broadcast_to(inv_std2, (row_len, 128))
        y = normed2 * fg + fs
        high = y.astype(BF16)
        out_s[rsl, :] = high
        rest = (y - high.astype(F32)).astype(BF16)
        seg = lax.broadcasted_iota(jnp.int32, (SEGS, row_len), 0)
        member = (seg == ids_ref[pl.ds(r, 1), :]).astype(F32)
        count = jnp.sum(member, axis=1, keepdims=True)
        member = member.astype(BF16)
        pooled = (dot_nn(member, high) + dot_nn(member, rest)) / count
        inv_norm = lax.rsqrt(jnp.sum(pooled * pooled, axis=1, keepdims=True) + NORM_EPS)
        z = pooled * inv_norm
        ssl = pl.ds(pl.multiple_of(r * SEGS, SEGS), SEGS)
        z_ref[ssl, :] = z
        invn_ref[ssl, :] = jnp.broadcast_to(inv_norm, (SEGS, 128))
        cnt_ref[ssl, :] = jnp.broadcast_to(count, (SEGS, 128))
        for i, (src, dst) in enumerate(outs):
            pltpu.make_async_copy(src.at[rsl, :], dst.at[rsl, :], out_sem.at[3 + i]).start()
        return carry

    lax.fori_loop(0, rows, ffn, 0)
    emb_ref[...] = z_ref[...].astype(BF16)
    for i, (src, dst) in enumerate(outs):
        pltpu.make_async_copy(src, dst, out_sem.at[3 + i]).wait()
    qkv_out.wait()
    ctx_out.wait()
    rinv_out.wait()
    for slot in range(2):
        pltpu.make_async_copy(exp_s.at[slot], exp_hbm.at[0], exp_sem.at[slot]).wait()


def forward_call(tokens, ids, wqkv, qb, vb, wp, pb, ag, ash, wu, ub, wd, db, fg, fs):
    toks, width = tokens.shape
    rows, row_len = ids.shape
    ff = wu.shape[1]
    pairs = width // PAIR
    segs = rows * SEGS
    sds = jax.ShapeDtypeStruct
    vm = pl.BlockSpec(memory_space=pltpu.VMEM)
    hb = pl.BlockSpec(memory_space=pl.ANY)
    return pl.pallas_call(
        forward_kernel,
        out_shape=(
            sds((rows * pairs, 2, row_len, row_len), BF16),
            sds((toks, 3 * width), BF16),
            sds((toks, width), BF16),
            sds((toks, width), F32),
            sds((toks, width), F32),
            sds((toks, width), BF16),
            sds((toks, ff), BF16),
            sds((toks, ff), BF16),
            sds((toks, width), F32),
            sds((toks, width), BF16),
            sds((toks, 128), F32),
            sds((toks, 128), F32),
            sds((segs, width), BF16),
            sds((segs, width), F32),
            sds((segs, 128), F32),
            sds((segs, 128), F32),
        ),
        in_specs=[vm] * 10 + [hb] * 5,
        out_specs=[hb] * 10 + [vm] * 6,
        scratch_shapes=[
            pltpu.VMEM((toks, width), BF16),
            pltpu.VMEM(wqkv.shape, BF16),
            pltpu.VMEM(wp.shape, BF16),
            pltpu.VMEM(wu.shape, BF16),
            pltpu.VMEM(wd.shape, BF16),
            pltpu.VMEM((toks, 3 * width), BF16),
            pltpu.VMEM((toks, width), BF16),
            pltpu.VMEM((toks, width), F32),
            pltpu.VMEM((rows, row_len, row_len), F32),
            pltpu.VMEM((2, 2, row_len, row_len), BF16),
            pltpu.VMEM((toks, width), F32),
            pltpu.VMEM((toks, width), BF16),
            pltpu.VMEM((toks, ff), BF16),
            pltpu.VMEM((toks, ff), BF16),
            pltpu.VMEM((toks, width), F32),
            pltpu.VMEM((toks, width), BF16),
            pltpu.SemaphoreType.DMA((5,)),
            pltpu.SemaphoreType.DMA((9,)),
            pltpu.SemaphoreType.DMA((2,)),
        ],
        compiler_params=pltpu.CompilerParams(vmem_limit_bytes=60 * MIB),
        name="forward",
    )(ids, qb, vb, pb, ag, ash, ub, db, fg, fs, tokens, wqkv, wp, wu, wd)

MESH = pl.DeviceIdType.MESH
INV_TEMP = 100.0
NEG = -1000000000.0


def axis_groups(n):
    groups = []
    rest = n // 2
    while rest > 1:
        size = 4 if rest % 4 == 0 else (2 if rest % 2 == 0 else rest)
        groups.append(size)
        rest //= size
    return groups + [2]


def digits_of(me, groups):
    digits = []
    for size in reversed(groups):
        digits.append(lax.rem(me, size))
        me = me // size
    return digits[::-1]


def index_of(digits, groups):
    me = 0
    for digit, size in zip(digits, groups):
        me = me * size + digit
    return me


def contrast_kernel(groups, msg_ref, z_ref, invn_ref, cnt_ref, loss_ref, gp_ref, all_s, send_sem, recv_sem):
    n = 1
    for size in groups:
        n *= size
    me = lax.axis_index("batch")
    mine = digits_of(me, groups)
    seg_here, wide = msg_ref.shape
    width = z_ref.shape[1]
    total = n * seg_here
    stages = len(groups)

    def peer(stage, step):
        other = lax.rem(mine[stage] + step, groups[stage])
        return other, index_of(mine[:stage] + [other] + mine[stage + 1 :], groups)

    barrier = pltpu.get_barrier_semaphore()
    hops = 0
    for stage in range(stages):
        for step in range(1, groups[stage]):
            pl.semaphore_signal(barrier, inc=1, device_id=(peer(stage, step)[1],), device_id_type=MESH)
            hops += 1
    all_s[tuple(mine)] = msg_ref[...]
    pl.semaphore_wait(barrier, hops)

    slot = 0
    for stage in range(stages):
        copies = []
        for step in range(1, groups[stage]):
            block = all_s.at[(slice(None),) * stage + tuple(mine[stage:])]
            copies.append(
                pltpu.make_async_remote_copy(
                    src_ref=block,
                    dst_ref=block,
                    send_sem=send_sem.at[slot],
                    recv_sem=recv_sem.at[slot],
                    device_id=(peer(stage, step)[1],),
                    device_id_type=MESH,
                )
            )
            slot += 1
        for cp in copies:
            cp.start()
        for cp in copies:
            cp.wait()

    every = all_s[...].reshape(total, wide)
    emb = every[:, :width]
    own = msg_ref[:, :width]
    z = z_ref[...]
    own_row = (me * seg_here).astype(F32)
    own_pair = msg_ref[:, width : width + 128].astype(F32)
    own_pair = own_pair[:, 0:1] * 256.0 + own_pair[:, 1:2]

    scores = dot_nt(own, emb) * INV_TEMP
    column = lax.broadcasted_iota(jnp.int32, scores.shape, 1).astype(F32)
    row = lax.broadcasted_iota(jnp.int32, scores.shape, 0).astype(F32) + own_row
    masked = jnp.where(column == row, NEG, scores)
    peak = jnp.max(masked, axis=1, keepdims=True)
    log_norm = peak + jnp.log(jnp.sum(jnp.exp(masked - peak), axis=1, keepdims=True))
    weight = jnp.exp(masked - log_norm) - (column == own_pair).astype(F32)
    grad = dot_nn(weight.astype(BF16), emb)

    blk = min(total, 512)
    loss = jnp.zeros((1, 1), F32)
    for b in range(total // blk):
        part = emb[b * blk : (b + 1) * blk]
        pair = every[b * blk : (b + 1) * blk, width:].astype(F32)
        pair = pair[:, 0:1] * 256.0 + pair[:, 1:2]
        scores = dot_nt(part, emb) * INV_TEMP
        column = lax.broadcasted_iota(jnp.int32, scores.shape, 1).astype(F32)
        row = lax.broadcasted_iota(jnp.int32, scores.shape, 0).astype(F32) + float(b * blk)
        masked = jnp.where(column == row, NEG, scores)
        peak = jnp.max(masked, axis=1, keepdims=True)
        log_norm = peak + jnp.log(jnp.sum(jnp.exp(masked - peak), axis=1, keepdims=True))
        positive = jnp.sum(jnp.where(column == pair, scores, 0.0), axis=1, keepdims=True)
        loss = loss + jnp.sum(log_norm - positive, axis=0, keepdims=True)
        scores = dot_nt(part, own) * INV_TEMP
        column = lax.broadcasted_iota(jnp.int32, scores.shape, 1).astype(F32) + own_row
        row = lax.broadcasted_iota(jnp.int32, scores.shape, 0).astype(F32) + float(b * blk)
        weight = jnp.where(column == row, 0.0, jnp.exp(jnp.where(column == row, NEG, scores) - log_norm))
        weight = weight - (column == pair).astype(F32)
        grad = grad + dot_tn(weight.astype(BF16), part)
    loss_ref[...] = jnp.broadcast_to(loss * (1.0 / total), loss_ref.shape)
    grad = grad * INV_TEMP
    pooled_grad = invn_ref[:, 0:1] * (grad - z * jnp.sum(grad * z, axis=1, keepdims=True))
    gp_ref[...] = pooled_grad / cnt_ref[:, 0:1]


def contrast_call(n, emb_low, z, invn, cnt, pair_index):
    groups = axis_groups(n)
    seg_here, width = emb_low.shape
    high = (pair_index // 256).astype(BF16)[:, None]
    rest = (pair_index % 256).astype(BF16)[:, None]
    msg = jnp.concatenate([emb_low, high, rest, jnp.zeros((seg_here, 126), BF16)], axis=1)
    copies = sum(size - 1 for size in groups)
    vm = pl.BlockSpec(memory_space=pltpu.VMEM)
    return pl.pallas_call(
        functools.partial(contrast_kernel, groups),
        out_shape=(jax.ShapeDtypeStruct((8, 128), F32), jax.ShapeDtypeStruct((seg_here, width), F32)),
        in_specs=[vm] * 4,
        out_specs=[vm] * 2,
        scratch_shapes=[
            pltpu.VMEM(tuple(groups) + msg.shape, BF16),
            pltpu.SemaphoreType.DMA((copies,)),
            pltpu.SemaphoreType.DMA((copies,)),
        ],
        compiler_params=pltpu.CompilerParams(collective_id=0, has_side_effects=True, vmem_limit_bytes=56 * MIB),
        name="contrast",
    )(msg, z, invn, cnt)

def colsum(v):
    return jnp.sum(v, axis=0, keepdims=True)


def norm_back_k(grad_n, normed, inv_std):
    scale = 1.0 / grad_n.shape[-1]
    mean = jnp.sum(grad_n, axis=-1, keepdims=True) * scale
    dots = jnp.sum(grad_n * normed, axis=-1, keepdims=True) * scale
    return inv_std * (grad_n - mean - normed * dots)


def ffn_back_kernel(
    ids_ref, gp_ref, inv1_ref, inv2_ref, ag_ref, fg_ref,
    n2_hbm, wd_hbm, der_hbm, wu_hbm, n1_hbm, wp_hbm, rinv_hbm,
    gdl_hbm, gul_hbm, gal_hbm, gr1_hbm, rdo_hbm, vec_ref,
    n2_s, wd_s, der_s, wu_s, n1_s, wp_s, rinv_s, gdl_s, gul_s, gal_s, gr1_s, rdo_s, in_sem, out_sem,
):
    rows, row_len = ids_ref.shape
    width = n2_s.shape[1]
    ff = wu_s.shape[1]
    blk = 256
    whole = [(wd_hbm, wd_s), (wu_hbm, wu_s), (wp_hbm, wp_s)]
    by_row = [(n2_hbm, n2_s), (der_hbm, der_s), (n1_hbm, n1_s), (rinv_hbm, rinv_s)]
    outs = [(gdl_s, gdl_hbm), (gul_s, gul_hbm), (gal_s, gal_hbm), (gr1_s, gr1_hbm), (rdo_s, rdo_hbm)]

    def load(i, r):
        src, dst = by_row[i]
        sl = pl.ds(r * row_len, row_len)
        return pltpu.make_async_copy(src.at[sl, :], dst.at[sl, :], in_sem.at[3 + 2 * i + r])

    fixed = [pltpu.make_async_copy(src, dst, in_sem.at[i]) for i, (src, dst) in enumerate(whole)]
    load(0, 0).start()
    fixed[0].start()
    load(1, 0).start()
    fixed[1].start()
    load(2, 0).start()
    fixed[2].start()
    load(3, 0).start()
    for r in range(1, rows):
        for i in range(4):
            load(i, r).start()

    vec_ref[...] = jnp.zeros_like(vec_ref)
    ones = jnp.ones((8, row_len), BF16)
    for r in range(rows):
        rsl = slice(r * row_len, (r + 1) * row_len)
        seg = lax.broadcasted_iota(jnp.int32, (SEGS, row_len), 0)
        member = (seg == ids_ref[r : r + 1, :]).astype(BF16)
        gp = gp_ref[r * SEGS : (r + 1) * SEGS, :]
        high = gp.astype(BF16)
        rest = (gp - high.astype(F32)).astype(BF16)
        grad_y = dot_tn(member, high) + dot_tn(member, rest)
        load(0, r).wait()
        n2 = n2_s[rsl, :]
        vec_ref[0:1, :] += colsum(grad_y * n2)
        vec_ref[1:2, :] += colsum(grad_y)
        grad_r2 = norm_back_k(grad_y * fg_ref[...].reshape(1, width), n2, inv2_ref[rsl, 0:1])
        gdl = grad_r2.astype(BF16)
        gdl_s[rsl, :] = gdl
        vec_ref[2:3, :] += dot_nn(ones, gdl)[0:1]
        if r == 0:
            fixed[0].wait()
        load(1, r).wait()
        for j in range(ff // blk):
            csl = slice(j * blk, (j + 1) * blk)
            grad_act = dot_nt(gdl, wd_s[csl, :])
            gul_s[rsl, csl] = (grad_act * der_s[rsl, csl].astype(F32)).astype(BF16)
        if r == 0:
            fixed[1].wait()
        load(2, r).wait()
        for j in range(ff // width):
            vec_ref[6 + j : 7 + j, :] += dot_nn(ones, gul_s[rsl, j * width : (j + 1) * width])[0:1]
        grad_first = grad_r2 + dot_nt(gul_s[rsl, :], wu_s[...])
        n1 = n1_s[rsl, :]
        vec_ref[3:4, :] += colsum(grad_first * n1)
        vec_ref[4:5, :] += colsum(grad_first)
        grad_r1 = norm_back_k(grad_first * ag_ref[...].reshape(1, width), n1, inv1_ref[rsl, 0:1])
        gr1_s[rsl, :] = grad_r1
        gal = grad_r1.astype(BF16)
        gal_s[rsl, :] = gal
        vec_ref[5:6, :] += dot_nn(ones, gal)[0:1]
        if r == 0:
            fixed[2].wait()
        load(3, r).wait()
        grad_ctx = dot_nt(gal, wp_s[...]).astype(BF16)
        rdo_s[rsl, :] = (grad_ctx.astype(F32) * rinv_s[rsl, :]).astype(BF16)
        for i, (src, dst) in enumerate(outs):
            pltpu.make_async_copy(src.at[rsl, :], dst.at[rsl, :], out_sem.at[i]).start()
    for i, (src, dst) in enumerate(outs):
        pltpu.make_async_copy(src, dst, out_sem.at[i]).wait()


def ffn_back_call(ids, gp, inv1, inv2, ag, fg, n2, wd, der, wu, n1, wp, rinv):
    toks, width = n2.shape
    ff = wu.shape[1]
    rows = ids.shape[0]
    vm = pl.BlockSpec(memory_space=pltpu.VMEM)
    hb = pl.BlockSpec(memory_space=pl.ANY)
    sds = jax.ShapeDtypeStruct
    hbm_in = [n2, wd, der, wu, n1, wp, rinv]
    outs = [sds((toks, width), BF16), sds((toks, ff), BF16), sds((toks, width), BF16), sds((toks, width), F32), sds((toks, width), BF16)]
    return pl.pallas_call(
        ffn_back_kernel,
        out_shape=tuple(outs) + (sds((16, width), F32),),
        in_specs=[vm] * 6 + [hb] * 7,
        out_specs=[hb] * 5 + [vm],
        scratch_shapes=[pltpu.VMEM(a.shape, a.dtype) for a in hbm_in + outs]
        + [pltpu.SemaphoreType.DMA((3 + 4 * rows,)), pltpu.SemaphoreType.DMA((5,))],
        compiler_params=pltpu.CompilerParams(vmem_limit_bytes=60 * MIB),
        name="ffn_back",
    )(ids, gp, inv1, inv2, ag, fg, *hbm_in)

UNIT_ROWS = 48


def event_plan(pieces, units):
    core, axis, hop = 3.0, 6.3, 2.0
    free = {"x": 0.0, "y": 0.0, "z": 0.0}
    pending = []
    plan = []
    now = 0.0

    def advance(unit, step, at):
        first, second = ("x", "y") if unit["par"] == 0 else ("y", "x")
        size = unit["size"]
        if step == 0:
            return at + core * size
        lane, cost = ((first, axis), (second, axis / 2), ("z", axis / 2))[step - 1]
        start = max(at, free[lane])
        free[lane] = start + cost * size
        return start + cost * size + hop

    for name, cost in pieces:
        now += cost
        steps = []
        for unit in units:
            if unit["after"] == name:
                steps.append((unit["id"], 0))
                pending.append((advance(unit, 0, now), unit["id"], 1))
        pending.sort()
        while pending and pending[0][0] <= now:
            _, uid, step = pending.pop(0)
            steps.append((uid, step))
            now += 0.3
            if step < 4:
                pending.append((advance(units[uid], step, now), uid, step + 1))
                pending.sort()
        plan.append(steps)
    rest = []
    while pending:
        at, uid, step = pending.pop(0)
        now = max(now, at) + 0.3
        rest.append((uid, step))
        if step < 4:
            pending.append((advance(units[uid], step, now), uid, step + 1))
            pending.sort()
    plan.append(rest)
    return plan, now


def tail_kernel(
    depth,
    vec_ref,
    low_hbm, gul_hbm, act_hbm, gdl_hbm, ctx_hbm, gal_hbm, tok_hbm, qkv_hbm, exp_hbm, rdo_hbm, gr1_hbm, wqkv_hbm,
    tg_hbm, oq_ref, op_ref, ou_ref, od_ref, v_qb, v_vb, v_pb, v_ag, v_as, v_ub, v_db, v_fg, v_fs,
    w_s, wd_s, rc_s, rcd_s, r2_s, r2d_s, r3_s, r3d_s, rz_s, rzd_s,
    turn_s, tok_s, stream_s, gdl_s, gal_s, ctx_s, rdo_s, qg_s, exp_s, gq_s, tg_s, wq_s,
    ar0_s, ar1_s, ar2_s, br0_s, br1_s, br2_s,
    send_sem, recv_sem, asend_sem, arecv_sem, in_sem, str_sem, grp_sem, exp_sem, out_sem,
):
    toks, width = tok_s.shape
    half = width // 2
    ff = act_hbm.shape[1]
    row_len = exp_s.shape[3]
    rows = toks // row_len
    strip = width // (8 * depth)
    me = lax.axis_index("batch")
    c = lax.rem(me, 2)
    x = lax.rem(me // 2, 2)
    y = lax.rem(me // 4, 2)
    z = me // 8

    def index(zz, yy, xx, cc):
        return ((zz * 2 + yy) * 2 + xx) * 2 + cc

    core_peer = index(z, y, x, 1 - c)
    x_peer = index(z, y, 1 - x, c)
    y_peer = index(z, 1 - y, x, c)
    xy_peer = index(z, 1 - y, 1 - x, c)
    z_peers = [index(lax.rem(z + step, depth), y, x, c) for step in range(1, depth)]
    everyone = [core_peer, x_peer, y_peer, xy_peer] + z_peers

    barrier = pltpu.get_barrier_semaphore()
    for other in everyone:
        pl.semaphore_signal(barrier, inc=1, device_id=(other,), device_id_type=MESH)

    def local(src, dst, sem):
        return pltpu.make_async_copy(src, dst, sem)

    def stream(k):
        kinds = ff // width
        src = gul_hbm if k < kinds else act_hbm
        off = (k % kinds) * width
        return local(src.at[:, off : off + width], stream_s.at[k % 2], str_sem.at[k % 2])

    def group_loads(g):
        return [
            local(
                qkv_hbm.at[:, third * width + g * 2 * PAIR : third * width + (g + 1) * 2 * PAIR],
                qg_s.at[g % 2, :, third * 2 * PAIR : (third + 1) * 2 * PAIR],
                grp_sem.at[(g % 2) * 3 + third],
            )
            for third in range(3)
        ]

    def exp_load(r, p, slot):
        return local(exp_hbm.at[r * (width // PAIR) + p], exp_s.at[slot], exp_sem.at[slot])

    groups = width // (2 * PAIR)
    low_load = local(low_hbm, tok_s, in_sem.at[0])
    low_load.start()
    stream(0).start()
    stream(1).start()
    gdl_load = local(gdl_hbm, gdl_s, in_sem.at[1])
    gdl_load.start()
    ctx_load = local(ctx_hbm, ctx_s, in_sem.at[2])
    ctx_load.start()
    gal_load = local(gal_hbm, gal_s, in_sem.at[3])
    gal_load.start()
    rdo_load = local(rdo_hbm, rdo_s, in_sem.at[4])
    rdo_load.start()
    for cp in group_loads(0):
        cp.start()
    exp_load(0, 0, 0).start()
    gr1_load = local(gr1_hbm, tg_s, in_sem.at[5])
    gr1_load.start()
    wq_loads = [
        local(
            wqkv_hbm.at[:, third * width + g * 2 * PAIR : third * width + (g + 1) * 2 * PAIR],
            wq_s.at[g, :, third * 2 * PAIR : (third + 1) * 2 * PAIR],
            in_sem.at[7 + g * 3 + third],
        )
        for g in range(groups)
        for third in range(3)
    ]
    for cp in wq_loads:
        cp.start()

    def make(uid, kind, at, par, after, size):
        return {"id": uid, "kind": kind, "at": at, "par": par, "after": after, "size": size}

    units = []
    for u in range(4):
        units.append(make(u, "up", u, u % 2, "up%d" % u, 1.0))
    for j in range(3):
        units.append(make(4 + j, "down", j, (j + 1) % 2, "down%d" % (depth - 1), 4 / 3))
    units.append(make(7, "proj", 4, 0, "proj", 1.0))
    for g in range(3):
        units.append(make(8 + g, "qkv", 5 + g, (g + 1) % 2, "dqkv%d" % g, 1.0))
    pieces = [("up%d" % u, 1.8) for u in range(4)] + [("down%d" % m, 2.0) for m in range(depth)] + [("proj", 2.0)]
    for g in range(groups):
        pieces += [("attn%d%d" % (g, i), 2.0) for i in range(2 * rows)] + [("dqkv%d" % g, 2.0), ("tok%d" % g, 2.0)]
    plan, _ = event_plan(pieces, units)

    def bufs(unit):
        if unit["kind"] == "down":
            return [ref.at[unit["at"]] for ref in (wd_s, rcd_s, r2d_s, r3d_s, rzd_s)]
        return [ref.at[unit["at"]] for ref in (w_s, rc_s, r2_s, r3_s, rz_s)]

    def remote(src, dst, slot, device, ssem=send_sem, rsem=recv_sem):
        return pltpu.make_async_remote_copy(
            src_ref=src, dst_ref=dst, send_sem=ssem.at[slot], recv_sem=rsem.at[slot], device_id=(device,), device_id_type=MESH
        )

    def unit_copies(unit, step):
        w, rc, r2, r3, rz = bufs(unit)
        f, s = (x, y) if unit["par"] == 0 else (y, x)
        f_peer, s_peer = (x_peer, y_peer) if unit["par"] == 0 else (y_peer, x_peer)
        base = unit["id"] * (2 + depth)
        if step == 0:
            return [remote(w.at[1 - c], rc, base, core_peer)]
        if step == 1:
            return [remote(w.at[c, 1 - f], r2, base + 1, f_peer)]
        if step == 2:
            return [remote(w.at[c, f, 1 - s], r3, base + 2, s_peer)]
        return [
            remote(w.at[c, f, s, lax.rem(z + k, depth)], rz.at[z], base + 2 + k, z_peers[k - 1])
            for k in range(1, depth)
        ]

    def finish(unit, total):
        kind, at = unit["kind"], unit["at"]
        if kind == "down":
            per = width // 128
            for k in range(4):
                start = (k // 2) * UNIT_ROWS * per + at * 2 + k % 2
                od_ref[pl.ds(start, UNIT_ROWS, stride=per), :] = total[:, k * 128 : (k + 1) * 128]
            return
        for k in range(6):
            piece = total[(k // 3) * strip : (k // 3 + 1) * strip, (k % 3) * 128 : (k % 3 + 1) * 128]
            if kind == "up":
                ref, per, col = ou_ref, ff // 128, at * 6 + k
            elif kind == "proj":
                ref, per, col = op_ref, width // 128, k
            else:
                ref, per, col = oq_ref, 3 * width // 128, (k // 2) * (width // 128) + (at - 5) * 2 + k % 2
            ref[pl.ds(col, strip, stride=per), :] = piece

    def take(unit, step):
        w, rc, r2, r3, rz = bufs(unit)
        f, s = (x, y) if unit["par"] == 0 else (y, x)
        if step > 0:
            for cp in unit_copies(unit, step - 1):
                cp.wait_recv()
        f32 = lambda v: v.astype(F32)
        if step == 1:

            def body(i, carry):
                a, b = i // depth, lax.rem(i, depth)
                w[c, 1 - f, a, b] = (f32(w[c, 1 - f, a, b]) + f32(rc[1 - f, a, b])).astype(BF16)
                return carry

            lax.fori_loop(0, 2 * depth, body, 0)
        elif step == 2:

            def body(b, carry):
                w[c, f, 1 - s, b] = (f32(w[c, f, 1 - s, b]) + f32(rc[f, 1 - s, b]) + f32(r2[1 - s, b])).astype(BF16)
                return carry

            lax.fori_loop(0, depth, body, 0)
        elif step == 3:

            def body(k, carry):
                b = lax.rem(z + k, depth)
                w[c, f, s, b] = (f32(w[c, f, s, b]) + f32(rc[f, s, b]) + f32(r2[s, b]) + f32(r3[b])).astype(BF16)
                return carry

            lax.fori_loop(1, depth, body, 0)
        elif step == 4:
            total = f32(w[c, f, s, z]) + f32(rc[f, s, z]) + f32(r2[s, z]) + f32(r3[z])
            for k in range(1, depth):
                total = total + f32(rz[lax.rem(z + k, depth)])
            finish(unit, total)
        if step < 4:
            for cp in unit_copies(unit, step):
                cp.start()

    def vec_copies(which, stage):
        bank = ((ar0_s, ar1_s, ar2_s), (br0_s, br1_s, br2_s))[which][stage]
        base = which * (depth + 3) + (0, depth - 1, depth + 2)[stage]
        if stage == 0:
            return [remote(bank.at[z], bank.at[z], base + k, z_peers[k], asend_sem, arecv_sem) for k in range(depth - 1)]
        if stage == 1:
            mine = y * 2 + x
            return [
                remote(bank.at[mine], bank.at[mine], base + k, other, asend_sem, arecv_sem)
                for k, other in enumerate((x_peer, y_peer, xy_peer))
            ]
        return [remote(bank.at[c], bank.at[c], base, core_peer, asend_sem, arecv_sem)]

    def vec_step(which, step):
        banks = ((ar0_s, ar1_s, ar2_s), (br0_s, br1_s, br2_s))[which]
        total = None
        if step > 0:
            for cp in vec_copies(which, step - 1):
                cp.wait_recv()
            bank = banks[step - 1]
            total = bank[0]
            for k in range(1, bank.shape[0]):
                total = total + bank[k]
        if step < 3:
            if step > 0:
                banks[step][(y * 2 + x) if step == 1 else c] = total
            for cp in vec_copies(which, step):
                cp.start()
        elif which == 0:
            for k, ref in enumerate((v_fg, v_fs, v_db, v_ag, v_as, v_pb)):
                ref[...] = total[k : k + 1].reshape(width)
            v_ub[...] = jnp.concatenate([total[6 + k : 7 + k] for k in range(ff // width)], axis=1).reshape(ff)
        else:
            v_qb[...] = total[0:1].reshape(width)
            v_vb[...] = total[1:2].reshape(width)

    places = [name for name, _ in pieces]

    def after(name):
        for uid, step in plan[places.index(name)]:
            take(units[uid], step)

    def put_unit(unit, res):
        w = bufs(unit)[0]
        for d in range(8 * depth):
            cc, xx, yy, zz = d % 2, d // 2 % 2, d // 4 % 2, d // 8
            f, s = (xx, yy) if unit["par"] == 0 else (yy, xx)
            piece = res[d * strip : (d + 1) * strip]
            w[cc, f, s, zz] = jnp.concatenate([piece[:, :half], piece[:, half:]], axis=0).astype(BF16)

    ar0_s[z] = vec_ref[...]
    br0_s[z] = jnp.zeros_like(vec_ref[0:8, :])
    low_load.wait()
    turn_s[...] = jnp.transpose(tok_s[...])
    tok_load = local(tok_hbm, tok_s, in_sem.at[6])
    tok_load.start()
    kinds = ff // width
    for u in range(kinds):
        stream(u).wait()
        put_unit(units[u], dot_nn(turn_s[...], stream_s[u % 2]))
        stream(u + 2).start()
        if u == 0:
            pl.semaphore_wait(barrier, len(everyone))
            vec_step(0, 0)
        after("up%d" % u)
        if u == 2:
            vec_step(0, 1)
    gdl_load.wait()
    for m in range(depth):
        stream(kinds + m).wait()
        res = dot_tn(stream_s[m % 2], gdl_s[...])
        if m + 2 < depth:
            stream(kinds + m + 2).start()
        for i in range(8):
            cc, xx, yy = i % 2, i // 2 % 2, i // 4
            piece = res[i * 2 * UNIT_ROWS : (i + 1) * 2 * UNIT_ROWS]
            for j in range(3):
                f, s = (xx, yy) if units[4 + j]["par"] == 0 else (yy, xx)
                blk = piece[:, j * 256 : (j + 1) * 256]
                wd_s[j, cc, f, s, m] = jnp.concatenate([blk[:UNIT_ROWS], blk[UNIT_ROWS:]], axis=1).astype(BF16)
        after("down%d" % m)
        if m == 1:
            vec_step(0, 2)
    ctx_load.wait()
    gal_load.wait()
    put_unit(units[7], dot_tn(ctx_s[...], gal_s[...]))
    after("proj")
    vec_step(0, 3)
    tok_load.wait()
    turn_s[...] = jnp.transpose(tok_s[...])
    rdo_load.wait()
    lane = lax.broadcasted_iota(jnp.int32, (row_len, 2 * PAIR), 1)
    first = lax.rem(lane, PAIR) < HEAD_DIM
    ones = jnp.ones((row_len, PAIR), BF16)
    ones8 = jnp.ones((8, toks), BF16)
    scale = HEAD_DIM**-0.5
    for g in range(groups):
        for cp in group_loads(g):
            cp.wait()
        if g + 1 < groups:
            for cp in group_loads(g + 1):
                cp.start()

        def attend(i, carry):
            r, pp = i // 2, lax.rem(i, 2)
            slot = lax.rem(i, 2)
            exp_load(r, 2 * g + pp, slot).wait()

            @pl.when(i + 1 < 2 * rows)
            def _():
                exp_load((i + 1) // 2, 2 * g + lax.rem(i + 1, 2), 1 - slot).start()

            if g + 1 < groups:

                @pl.when(i + 1 == 2 * rows)
                def _():
                    exp_load(0, 2 * (g + 1), 0).start()

            rsl = pl.ds(pl.multiple_of(r * row_len, row_len), row_len)
            lanes = lambda base: pl.ds(pl.multiple_of(base + pp * PAIR, PAIR), PAIR)
            q = qg_s[g % 2, rsl, lanes(0)]
            k = qg_s[g % 2, rsl, lanes(2 * PAIR)]
            v = qg_s[g % 2, rsl, lanes(4 * PAIR)]
            do = rdo_s[rsl, lanes(g * 2 * PAIR)]
            ctx = ctx_s[rsl, lanes(g * 2 * PAIR)]
            neg = -(do.astype(F32) * ctx.astype(F32))
            lhs = jnp.concatenate([do, neg.astype(BF16)], axis=1)
            rhs = jnp.concatenate([v, ones], axis=1)
            do_t = jnp.transpose(do)
            q_t = jnp.transpose(q)
            dq, dk, dv = [], [], []
            for h in range(2):
                lh = jnp.where(first if h == 0 else ~first, lhs, jnp.zeros_like(lhs))
                e = exp_s[slot, h]
                ds = (e.astype(F32) * dot_nt(lh, rhs)).astype(BF16)
                hs = slice(h * HEAD_DIM, (h + 1) * HEAD_DIM)
                dv.append(dot_nn(do_t[hs], e))
                dk.append(dot_nn(q_t[hs], ds))
                dq.append(dot_nn(ds, k))
            gq_s[rsl, lanes(0)] = (jnp.where(first[:, :PAIR], dq[0], dq[1]) * scale).astype(BF16)
            gq_s[rsl, lanes(2 * PAIR)] = jnp.transpose((jnp.concatenate(dk, axis=0) * scale).astype(BF16))
            gq_s[rsl, lanes(4 * PAIR)] = jnp.transpose(jnp.concatenate(dv, axis=0).astype(BF16))
            for step in range(2 * rows):
                if plan[places.index("attn%d%d" % (g, step))]:

                    @pl.when(i == step)
                    def _():
                        after("attn%d%d" % (g, step))

            return carry

        lax.fori_loop(0, 2 * rows, attend, 0)
        put_unit(units[8 + g], dot_nn(turn_s[...], gq_s[...]))
        after("dqkv%d" % g)
        if g == 0:
            gr1_load.wait()
        for cp in wq_loads[3 * g : 3 * g + 3]:
            cp.wait()
        bias = dot_nn(ones8, gq_s[...])
        br0_s[z, 0:1, g * 2 * PAIR : (g + 1) * 2 * PAIR] = bias[0:1, : 2 * PAIR]
        br0_s[z, 1:2, g * 2 * PAIR : (g + 1) * 2 * PAIR] = bias[0:1, 4 * PAIR :]
        if g == groups - 1:
            vec_step(1, 0)
        tg_s[...] += dot_nt(gq_s[...], wq_s[g])
        after("tok%d" % g)
    tg_out = local(tg_s, tg_hbm, out_sem)
    tg_out.start()
    vec_step(1, 1)
    left = plan[-1]
    for k, (uid, step) in enumerate(left):
        take(units[uid], step)
        if k == len(left) // 3:
            vec_step(1, 2)
        if k == 2 * len(left) // 3:
            vec_step(1, 3)
    for step in range(4):
        for unit in units:
            for cp in unit_copies(unit, step):
                cp.wait_send()
    for which in range(2):
        for stage in range(3):
            for cp in vec_copies(which, stage):
                cp.wait_send()
    tg_out.wait()


def tail_call(n, vec, low, gul, act, gdl, ctx, gal, tok, qkv, exps, rdo, gr1, wqkv):
    depth = n // 8
    toks, width = tok.shape
    ff = act.shape[1]
    row_len = exps.shape[2]
    groups = width // (2 * PAIR)
    half = width // 2
    sds = jax.ShapeDtypeStruct
    vm = pl.BlockSpec(memory_space=pltpu.VMEM)
    hb = pl.BlockSpec(memory_space=pl.ANY)
    flat = lambda cols, rws: sds((rws // n * cols // 128, 128), F32)
    v = lambda k: sds((k,), F32)
    wide = lambda *lead: [pltpu.VMEM((8,) + lead + (UNIT_ROWS, half), BF16), pltpu.VMEM((3,) + lead + (UNIT_ROWS, 512), BF16)]
    scratch = wide(2, 2, 2, depth) + wide(2, 2, depth) + wide(2, depth) + wide(depth) + wide(depth)
    scratch += [
        pltpu.VMEM((width, toks), BF16),
        pltpu.VMEM((toks, width), BF16),
        pltpu.VMEM((2, toks, width), BF16),
        pltpu.VMEM((toks, width), BF16),
        pltpu.VMEM((toks, width), BF16),
        pltpu.VMEM((toks, width), BF16),
        pltpu.VMEM((toks, width), BF16),
        pltpu.VMEM((2, toks, 6 * PAIR), BF16),
        pltpu.VMEM((2, 2, row_len, row_len), BF16),
        pltpu.VMEM((toks, 6 * PAIR), BF16),
        pltpu.VMEM((toks, width), F32),
        pltpu.VMEM((groups, width, 6 * PAIR), BF16),
        pltpu.VMEM((depth, 16, width), F32),
        pltpu.VMEM((4, 16, width), F32),
        pltpu.VMEM((2, 16, width), F32),
        pltpu.VMEM((depth, 8, width), F32),
        pltpu.VMEM((4, 8, width), F32),
        pltpu.VMEM((2, 8, width), F32),
        pltpu.SemaphoreType.DMA((11 * (2 + depth),)),
        pltpu.SemaphoreType.DMA((11 * (2 + depth),)),
        pltpu.SemaphoreType.DMA((2 * (depth + 3),)),
        pltpu.SemaphoreType.DMA((2 * (depth + 3),)),
        pltpu.SemaphoreType.DMA((7 + 3 * groups,)),
        pltpu.SemaphoreType.DMA((2,)),
        pltpu.SemaphoreType.DMA((6,)),
        pltpu.SemaphoreType.DMA((2,)),
        pltpu.SemaphoreType.DMA,
    ]
    return pl.pallas_call(
        functools.partial(tail_kernel, depth),
        out_shape=(
            sds((toks, width), F32), flat(3 * width, width), flat(width, width), flat(ff, width), flat(width, ff),
            v(width), v(width), v(width), v(width), v(width), v(ff), v(width), v(width), v(width),
        ),
        in_specs=[vm] + [hb] * 12,
        out_specs=[hb] + [vm] * 13,
        scratch_shapes=scratch,
        compiler_params=pltpu.CompilerParams(collective_id=1, has_side_effects=True, vmem_limit_bytes=62 * MIB),
        name="weight_sums",
    )(vec, low, gul, act, gdl, ctx, gal, tok, qkv, exps, rdo, gr1, wqkv)

def norm_back(grad_out, normed, inv_std, gain):
    grad_n = grad_out * gain
    return inv_std * (
        grad_n
        - jnp.mean(grad_n, axis=-1, keepdims=True)
        - normed * jnp.mean(grad_n * normed, axis=-1, keepdims=True)
    )


def attend_back(entry):
    qkv_row, exps, rinv, ctx, grad_row = entry
    row_len = qkv_row.shape[0]
    split = qkv_row.reshape(row_len, 3, HEADS, HEAD_DIM)
    queries, key_vecs, values = split[:, 0], split[:, 1], split[:, 2]
    exps = exps.reshape(HEADS, row_len, row_len)
    scaled = (grad_row.astype(F32) * rinv).astype(BF16)
    delta = jnp.sum(scaled.astype(F32).reshape(row_len, HEADS, HEAD_DIM) * ctx.astype(F32).reshape(row_len, HEADS, HEAD_DIM), axis=-1)
    scaled = scaled.reshape(row_len, HEADS, HEAD_DIM)
    grad_probs = jnp.einsum("qhd,khd->hqk", scaled, values, preferred_element_type=F32)
    grad_values = jnp.einsum("hqk,qhd->khd", exps, scaled, preferred_element_type=F32)
    grad_scores = (exps.astype(F32) * (grad_probs - delta.T[..., None])).astype(BF16)
    grad_queries = jnp.einsum("hqk,khd->qhd", grad_scores, key_vecs, preferred_element_type=F32) * HEAD_DIM**-0.5
    grad_keys = jnp.einsum("hqk,qhd->khd", grad_scores, queries, preferred_element_type=F32) * HEAD_DIM**-0.5
    stacked = jnp.stack([grad_queries, grad_keys, grad_values], axis=1)
    return stacked.reshape(row_len, 3 * HEADS * HEAD_DIM).astype(BF16)


def per_device(
    tokens, segment_ids, pair_index, qkv_weight, query_bias, value_bias, proj_weight, proj_bias,
    attn_gain, attn_shift, up_weight, up_bias, down_weight, down_bias, ffn_gain, ffn_shift,
):
    n = lax.axis_size("batch")
    rows, row_len = segment_ids.shape
    toks, width = tokens.shape
    (exps, qkv, context, rinv, normed_one, first_low, acted, deriv, normed_two, layer_out,
     inv_one, inv_two, emb_low, z, invn, cnt) = forward_call(
        tokens, segment_ids, qkv_weight, query_bias, value_bias, proj_weight, proj_bias, attn_gain, attn_shift,
        up_weight, up_bias, down_weight, down_bias, ffn_gain, ffn_shift)
    loss, grad_seg = contrast_call(n, emb_low, z, invn, cnt, pair_index)
    if width % (8 * n) == 0 and n // 8 * 2 * UNIT_ROWS * 8 == up_weight.shape[1]:
        gdl, gul, gal, gr1, rdo, vec = ffn_back_call(
            segment_ids, grad_seg, inv_one, inv_two, attn_gain, ffn_gain,
            normed_two, down_weight, deriv, up_weight, normed_one, proj_weight, rinv)
        (tokens_grad, qkv_grad, proj_grad, up_grad, down_grad,
         d_qb, d_vb, d_pb, d_ag, d_as, d_ub, d_db, d_fg, d_fs) = tail_call(
            n, vec, first_low, gul, acted, gdl, context, gal, tokens, qkv, exps, rdo, gr1, qkv_weight)
        return (loss[0, 0], layer_out, tokens_grad, qkv_grad.reshape(-1), proj_grad.reshape(-1), up_grad.reshape(-1),
                down_grad.reshape(-1), d_qb, d_vb, d_pb, d_ag, d_as, d_ub, d_db, d_fg, d_fs)
    inv_one = inv_one[:, :1]
    inv_two = inv_two[:, :1]
    row_base = (jnp.arange(rows, dtype=jnp.int32) * SEGS)[:, None]
    local_ids = jnp.where(segment_ids >= 0, segment_ids + row_base, -1).reshape(toks)
    member = (local_ids[None, :] == jnp.arange(rows * SEGS, dtype=jnp.int32)[:, None]).astype(F32)
    grad_y = lax.dot_general(member, grad_seg, (((0,), (0,)), ((), ())), precision=lax.Precision.HIGHEST)
    ffn_gain_part = jnp.sum(grad_y * normed_two, axis=0)
    ffn_shift_part = jnp.sum(grad_y, axis=0)
    grad_r2 = norm_back(grad_y, normed_two, inv_two, ffn_gain)
    grad_down_low = grad_r2.astype(BF16)
    down_bias_part = jnp.sum(grad_down_low.astype(F32), axis=0)
    down_weight_part = dot_tn(acted, grad_down_low)
    grad_up_low = (dot_nt(grad_down_low, down_weight) * deriv.astype(F32)).astype(BF16)
    up_bias_part = jnp.sum(grad_up_low.astype(F32), axis=0)
    up_weight_part = dot_tn(first_low, grad_up_low)
    grad_first = grad_r2 + dot_nt(grad_up_low, up_weight)
    attn_gain_part = jnp.sum(grad_first * normed_one, axis=0)
    attn_shift_part = jnp.sum(grad_first, axis=0)
    grad_r1 = norm_back(grad_first, normed_one, inv_one, attn_gain)
    grad_att_low = grad_r1.astype(BF16)
    proj_bias_part = jnp.sum(grad_att_low.astype(F32), axis=0)
    proj_weight_part = dot_tn(context, grad_att_low)
    grad_context = dot_nt(grad_att_low, proj_weight).astype(BF16)
    by_row = lambda v: v.reshape(rows, row_len, -1)
    grad_qkv = lax.map(
        attend_back,
        (by_row(qkv), exps.reshape(rows, -1, 2, row_len, row_len), by_row(rinv), by_row(context), by_row(grad_context)),
    ).reshape(toks, 3 * width)
    qkv_bias_part = jnp.sum(grad_qkv.astype(F32), axis=0)
    qkv_weight_part = dot_tn(tokens, grad_qkv)
    tokens_grad = grad_r1 + dot_nt(grad_qkv, qkv_weight)
    scatter = lambda v: lax.psum_scatter(v.reshape(-1), "batch", scatter_dimension=0, tiled=True)
    sums = lax.psum(
        (qkv_bias_part[:width], qkv_bias_part[2 * width :], proj_bias_part, attn_gain_part, attn_shift_part,
         up_bias_part, down_bias_part, ffn_gain_part, ffn_shift_part),
        "batch",
    )
    return (loss[0, 0], layer_out, tokens_grad, scatter(qkv_weight_part), scatter(proj_weight_part),
            scatter(up_weight_part), scatter(down_weight_part)) + tuple(sums)


def solution(mesh):
    split, whole = P("batch"), P()
    return jax.shard_map(
        per_device,
        mesh=mesh,
        in_specs=(P("batch", None), P("batch", None), split) + (whole,) * 13,
        out_specs=(whole, P("batch", None), P("batch", None)) + (split,) * 4 + (whole,) * 9,
        check_vma=False,
    )
```

```python
import functools
import jax
import jax.numpy as jnp
from jax import lax
from jax.experimental import pallas as pl
from jax.experimental.pallas import tpu as pltpu
from jax.sharding import PartitionSpec as P

F32 = jnp.float32
BF16 = jnp.bfloat16
HEADS = 12
HEAD_DIM = 64
SEGS = 8
PAIR = 2 * HEAD_DIM
LN_EPS = 1e-12
NORM_EPS = 1e-06
MIB = 2**20


def dot_nn(a, b):
    return lax.dot_general(a, b, (((1,), (0,)), ((), ())), preferred_element_type=F32)


def dot_nt(a, b):
    return lax.dot_general(a, b, (((1,), (1,)), ((), ())), preferred_element_type=F32)


def dot_tn(a, b):
    return lax.dot_general(a, b, (((0,), (0,)), ((), ())), preferred_element_type=F32)


def gelu_parts(pre):
    half = 0.5 * pre
    cdf = 0.5 + 0.5 * lax.erf(pre * 0.7071067811865476)
    pdf = jnp.exp(-half * pre) * 0.3989422804014327
    return pre * cdf, cdf + pre * pdf


def normalize(resid):
    width = resid.shape[-1]
    average = jnp.sum(resid, axis=-1, keepdims=True) * (1.0 / width)
    centred = resid - average
    variance = jnp.sum(centred * centred, axis=-1, keepdims=True) * (1.0 / width)
    inv_std = lax.rsqrt(variance + LN_EPS)
    return centred * inv_std, inv_std


def forward_kernel(
    ids_ref, qb_ref, vb_ref, pb_ref, ag_ref, as_ref, ub_ref, db_ref, fg_ref, fs_ref,
    tok_hbm, wqkv_hbm, wp_hbm, wu_hbm, wd_hbm,
    exp_hbm, qkv_hbm, ctx_hbm, rinv_hbm, n1_hbm, low_hbm, act_hbm, der_hbm, n2_hbm, out_hbm,
    stat_ref, z_ref, invn_ref, cnt_ref,
    tok_s, wqkv_s, wp_s, wu_s, wd_s, qkv_s, ctx_s, rinv_s, bias_s, exp_s,
    n1_s, low_s, act_s, der_s, n2_s, out_s, in_sem, out_sem, exp_sem,
):
    rows, row_len = ids_ref.shape
    toks, width = tok_s.shape
    pairs = width // PAIR
    ff = wu_s.shape[1]
    qb, vb, pb, ag, ash, db, fg, fs = (
        ref[...].reshape(1, width) for ref in (qb_ref, vb_ref, pb_ref, ag_ref, as_ref, db_ref, fg_ref, fs_ref)
    )
    ub = ub_ref[...].reshape(1, ff)

    loads = [
        pltpu.make_async_copy(src, dst, in_sem.at[i])
        for i, (src, dst) in enumerate(
            [(tok_hbm, tok_s), (wqkv_hbm, wqkv_s), (wp_hbm, wp_s), (wu_hbm, wu_s), (wd_hbm, wd_s)]
        )
    ]
    for cp in loads:
        cp.start()
    loads[0].wait()
    loads[1].wait()

    tok = tok_s[...]
    blk = 256
    for j in range(3 * width // blk):
        piece = dot_nn(tok, wqkv_s[:, j * blk : (j + 1) * blk])
        third, off = divmod(j * blk, width)
        if third == 0:
            piece = piece + qb[:, off : off + blk]
        elif third == 2:
            piece = piece + vb[:, off : off + blk]
        qkv_s[:, j * blk : (j + 1) * blk] = piece.astype(BF16)
    qkv_out = pltpu.make_async_copy(qkv_s, qkv_hbm, out_sem.at[0])
    qkv_out.start()

    lane = lax.broadcasted_iota(jnp.int32, (row_len, PAIR), 1)
    first = lane < HEAD_DIM
    ones = jnp.ones((row_len, PAIR), BF16)

    for r in range(rows):
        ids_row = ids_ref[r : r + 1, :].astype(F32)
        ids_col = jnp.transpose(jnp.broadcast_to(ids_row, (128, row_len)))
        for c in range(row_len // 128):
            bias_s[r, :, c * 128 : (c + 1) * 128] = jnp.where(
                ids_col == ids_row[:, c * 128 : (c + 1) * 128], 0.0, -1e9
            )

    def attend(it, carry):
        r = it // pairs
        p = it % pairs
        rsl = pl.ds(pl.multiple_of(r * row_len, row_len), row_len)
        col = lambda third: pl.ds(pl.multiple_of(third * width + p * PAIR, PAIR), PAIR)
        q = qkv_s[rsl, col(0)] * jnp.asarray(HEAD_DIM**-0.5, BF16)
        k = qkv_s[rsl, col(1)]
        v = jnp.concatenate([qkv_s[rsl, col(2)], ones], axis=1)
        slot = lax.rem(it, 2)

        @pl.when(it >= 2)
        def _():
            pltpu.make_async_copy(exp_s.at[slot], exp_hbm.at[it], exp_sem.at[slot]).wait()

        parts = []
        for h in range(2):
            qh = jnp.where(first if h == 0 else ~first, q, jnp.zeros_like(q))
            s = dot_nt(qh, k) + bias_s[r]
            e = jnp.exp(s - jnp.max(s, axis=1, keepdims=True)).astype(BF16)
            exp_s[slot, h] = e
            oe = dot_nn(e, v)
            rinv = 1.0 / oe[:, PAIR:]
            parts.append((oe[:, :PAIR] * rinv, rinv))
        ctx_s[rsl, pl.ds(pl.multiple_of(p * PAIR, PAIR), PAIR)] = jnp.where(
            first, parts[0][0], parts[1][0]
        ).astype(BF16)
        rinv_s[rsl, pl.ds(pl.multiple_of(p * PAIR, PAIR), PAIR)] = jnp.where(
            first, parts[0][1], parts[1][1]
        ).astype(BF16)
        pltpu.make_async_copy(exp_s.at[slot], exp_hbm.at[it], exp_sem.at[slot]).start()
        return carry

    lax.fori_loop(0, rows * pairs, attend, 0)
    ctx_out = pltpu.make_async_copy(ctx_s, ctx_hbm, out_sem.at[1])
    ctx_out.start()
    rinv_out = pltpu.make_async_copy(rinv_s, rinv_hbm, out_sem.at[2])
    rinv_out.start()
    for cp in loads[2:]:
        cp.wait()

    outs = [(n1_s, n1_hbm), (low_s, low_hbm), (act_s, act_hbm), (der_s, der_hbm), (n2_s, n2_hbm), (out_s, out_hbm)]

    def ffn(r, carry):
        rsl = pl.ds(pl.multiple_of(r * row_len, row_len), row_len)
        resid = tok_s[rsl, :].astype(F32) + (dot_nn(ctx_s[rsl, :], wp_s[...]) + pb)
        normed, inv_std = normalize(resid)
        n1_s[rsl, :] = normed.astype(BF16)
        first_norm = normed * ag + ash
        low = first_norm.astype(BF16)
        low_s[rsl, :] = low
        for j in range(ff // blk):
            pre = dot_nn(low, wu_s[:, j * blk : (j + 1) * blk]) + ub[:, j * blk : (j + 1) * blk]
            act, der = gelu_parts(pre)
            act_s[rsl, j * blk : (j + 1) * blk] = act.astype(BF16)
            der_s[rsl, j * blk : (j + 1) * blk] = der.astype(BF16)
        down = dot_nn(act_s[rsl, :], wd_s[...]) + db
        normed2, inv_std2 = normalize(first_norm + down)
        n2_s[rsl, :] = normed2.astype(BF16)
        stat_ref[rsl, :] = jnp.where(lane == 0, inv_std, inv_std2)
        y = normed2 * fg + fs
        high = y.astype(BF16)
        out_s[rsl, :] = high
        rest = (y - high.astype(F32)).astype(BF16)
        seg = lax.broadcasted_iota(jnp.int32, (SEGS, row_len), 0)
        member = (seg == ids_ref[pl.ds(r, 1), :]).astype(F32)
        count = jnp.sum(member, axis=1, keepdims=True)
        member = member.astype(BF16)
        pooled = (dot_nn(member, high) + dot_nn(member, rest)) / count
        inv_norm = lax.rsqrt(jnp.sum(pooled * pooled, axis=1, keepdims=True) + NORM_EPS)
        z = pooled * inv_norm
        ssl = pl.ds(pl.multiple_of(r * SEGS, SEGS), SEGS)
        z_ref[ssl, :] = z
        invn_ref[ssl, :] = jnp.broadcast_to(inv_norm, (SEGS, 128))
        cnt_ref[ssl, :] = jnp.broadcast_to(count, (SEGS, 128))
        for i, (src, dst) in enumerate(outs):
            pltpu.make_async_copy(src.at[rsl, :], dst.at[rsl, :], out_sem.at[3 + i]).start()
        return carry

    lax.fori_loop(0, rows, ffn, 0)
    for i, (src, dst) in enumerate(outs):
        pltpu.make_async_copy(src, dst, out_sem.at[3 + i]).wait()
    qkv_out.wait()
    ctx_out.wait()
    rinv_out.wait()
    for slot in range(2):
        pltpu.make_async_copy(exp_s.at[slot], exp_hbm.at[0], exp_sem.at[slot]).wait()


def forward_call(tokens, ids, wqkv, qb, vb, wp, pb, ag, ash, wu, ub, wd, db, fg, fs):
    toks, width = tokens.shape
    rows, row_len = ids.shape
    ff = wu.shape[1]
    pairs = width // PAIR
    segs = rows * SEGS
    sds = jax.ShapeDtypeStruct
    vm = pl.BlockSpec(memory_space=pltpu.VMEM)
    hb = pl.BlockSpec(memory_space=pl.ANY)
    return pl.pallas_call(
        forward_kernel,
        out_shape=(
            sds((rows * pairs, 2, row_len, row_len), BF16),
            sds((toks, 3 * width), BF16),
            sds((toks, width), BF16),
            sds((toks, width), BF16),
            sds((toks, width), BF16),
            sds((toks, width), BF16),
            sds((toks, ff), BF16),
            sds((toks, ff), BF16),
            sds((toks, width), BF16),
            sds((toks, width), BF16),
            sds((toks, 128), F32),
            sds((segs, width), F32),
            sds((segs, 128), F32),
            sds((segs, 128), F32),
        ),
        in_specs=[vm] * 10 + [hb] * 5,
        out_specs=[hb] * 10 + [vm] * 4,
        scratch_shapes=[
            pltpu.VMEM((toks, width), BF16),
            pltpu.VMEM(wqkv.shape, BF16),
            pltpu.VMEM(wp.shape, BF16),
            pltpu.VMEM(wu.shape, BF16),
            pltpu.VMEM(wd.shape, BF16),
            pltpu.VMEM((toks, 3 * width), BF16),
            pltpu.VMEM((toks, width), BF16),
            pltpu.VMEM((toks, width), BF16),
            pltpu.VMEM((rows, row_len, row_len), F32),
            pltpu.VMEM((2, 2, row_len, row_len), BF16),
            pltpu.VMEM((toks, width), BF16),
            pltpu.VMEM((toks, width), BF16),
            pltpu.VMEM((toks, ff), BF16),
            pltpu.VMEM((toks, ff), BF16),
            pltpu.VMEM((toks, width), BF16),
            pltpu.VMEM((toks, width), BF16),
            pltpu.SemaphoreType.DMA((5,)),
            pltpu.SemaphoreType.DMA((9,)),
            pltpu.SemaphoreType.DMA((2,)),
        ],
        compiler_params=pltpu.CompilerParams(vmem_limit_bytes=60 * MIB),
        name="forward",
    )(ids, qb, vb, pb, ag, ash, ub, db, fg, fs, tokens, wqkv, wp, wu, wd)

MESH = pl.DeviceIdType.MESH
INV_TEMP = 100.0
NEG = -1000000000.0


def axis_groups(n):
    groups = []
    rest = n // 2
    while rest > 1:
        size = 4 if rest % 4 == 0 else (2 if rest % 2 == 0 else rest)
        groups.append(size)
        rest //= size
    return groups + [2]


def digits_of(me, groups):
    digits = []
    for size in reversed(groups):
        digits.append(lax.rem(me, size))
        me = me // size
    return digits[::-1]


def index_of(digits, groups):
    me = 0
    for digit, size in zip(digits, groups):
        me = me * size + digit
    return me


def contrast_math(every, msg, me, z, invn, cnt):
    total, wide = every.shape
    seg_here, width = z.shape
    emb = every[:, :width]
    own = msg[:, :width]
    own_row = (me * seg_here).astype(F32)
    own_pair = msg[:, width : width + 128].astype(F32)
    own_pair = own_pair[:, 0:1] * 256.0 + own_pair[:, 1:2]

    scores = dot_nt(own, emb) * INV_TEMP
    column = lax.broadcasted_iota(jnp.int32, scores.shape, 1).astype(F32)
    row = lax.broadcasted_iota(jnp.int32, scores.shape, 0).astype(F32) + own_row
    masked = jnp.where(column == row, NEG, scores)
    peak = jnp.max(masked, axis=1, keepdims=True)
    log_norm = peak + jnp.log(jnp.sum(jnp.exp(masked - peak), axis=1, keepdims=True))
    weight = jnp.exp(masked - log_norm) - (column == own_pair).astype(F32)
    grad = dot_nn(weight.astype(BF16), emb)

    blk = min(total, 512)
    loss = jnp.zeros((1, 1), F32)
    for b in range(total // blk):
        part = emb[b * blk : (b + 1) * blk]
        pair = every[b * blk : (b + 1) * blk, width:].astype(F32)
        pair = pair[:, 0:1] * 256.0 + pair[:, 1:2]
        scores = dot_nt(part, emb) * INV_TEMP
        column = lax.broadcasted_iota(jnp.int32, scores.shape, 1).astype(F32)
        row = lax.broadcasted_iota(jnp.int32, scores.shape, 0).astype(F32) + float(b * blk)
        masked = jnp.where(column == row, NEG, scores)
        peak = jnp.max(masked, axis=1, keepdims=True)
        log_norm = peak + jnp.log(jnp.sum(jnp.exp(masked - peak), axis=1, keepdims=True))
        positive = jnp.sum(jnp.where(column == pair, scores, 0.0), axis=1, keepdims=True)
        loss = loss + jnp.sum(log_norm - positive, axis=0, keepdims=True)
        scores = dot_nt(part, own) * INV_TEMP
        column = lax.broadcasted_iota(jnp.int32, scores.shape, 1).astype(F32) + own_row
        row = lax.broadcasted_iota(jnp.int32, scores.shape, 0).astype(F32) + float(b * blk)
        weight = jnp.where(column == row, 0.0, jnp.exp(jnp.where(column == row, NEG, scores) - log_norm))
        weight = weight - (column == pair).astype(F32)
        grad = grad + dot_tn(weight.astype(BF16), part)
    grad = grad * INV_TEMP
    pooled_grad = invn * (grad - z * jnp.sum(grad * z, axis=1, keepdims=True))
    return loss * (1.0 / total), pooled_grad / cnt


def contrast_kernel(groups, msg_ref, z_ref, invn_ref, cnt_ref, loss_ref, gp_ref, all_s, send_sem, recv_sem):
    n = 1
    for size in groups:
        n *= size
    me = lax.axis_index("batch")
    mine = digits_of(me, groups)
    seg_here, wide = msg_ref.shape
    width = z_ref.shape[1]
    total = n * seg_here
    stages = len(groups)

    def peer(stage, step):
        other = lax.rem(mine[stage] + step, groups[stage])
        return other, index_of(mine[:stage] + [other] + mine[stage + 1 :], groups)

    barrier = pltpu.get_barrier_semaphore()
    hops = 0
    for stage in range(stages):
        for step in range(1, groups[stage]):
            pl.semaphore_signal(barrier, inc=1, device_id=(peer(stage, step)[1],), device_id_type=MESH)
            hops += 1
    all_s[tuple(mine)] = msg_ref[...]
    pl.semaphore_wait(barrier, hops)

    slot = 0
    for stage in range(stages):
        copies = []
        for step in range(1, groups[stage]):
            block = all_s.at[(slice(None),) * stage + tuple(mine[stage:])]
            copies.append(
                pltpu.make_async_remote_copy(
                    src_ref=block,
                    dst_ref=block,
                    send_sem=send_sem.at[slot],
                    recv_sem=recv_sem.at[slot],
                    device_id=(peer(stage, step)[1],),
                    device_id_type=MESH,
                )
            )
            slot += 1
        for cp in copies:
            cp.start()
        for cp in copies:
            cp.wait()

    loss, grad = contrast_math(
        all_s[...].reshape(total, wide), msg_ref[...], me, z_ref[...], invn_ref[:, 0:1], cnt_ref[:, 0:1]
    )
    loss_ref[...] = jnp.broadcast_to(loss, loss_ref.shape)
    gp_ref[...] = grad


def contrast_call(n, emb_low, z, invn, cnt, pair_index):
    groups = axis_groups(n)
    seg_here, width = emb_low.shape
    high = (pair_index // 256).astype(BF16)[:, None]
    rest = (pair_index % 256).astype(BF16)[:, None]
    msg = jnp.concatenate([emb_low, high, rest, jnp.zeros((seg_here, 126), BF16)], axis=1)
    copies = sum(size - 1 for size in groups)
    vm = pl.BlockSpec(memory_space=pltpu.VMEM)
    return pl.pallas_call(
        functools.partial(contrast_kernel, groups),
        out_shape=(jax.ShapeDtypeStruct((8, 128), F32), jax.ShapeDtypeStruct((seg_here, width), F32)),
        in_specs=[vm] * 4,
        out_specs=[vm] * 2,
        scratch_shapes=[
            pltpu.VMEM(tuple(groups) + msg.shape, BF16),
            pltpu.SemaphoreType.DMA((copies,)),
            pltpu.SemaphoreType.DMA((copies,)),
        ],
        compiler_params=pltpu.CompilerParams(collective_id=0, has_side_effects=True, vmem_limit_bytes=56 * MIB),
        name="contrast",
    )(msg, z, invn, cnt)

UNIT_ROWS = 48


def event_plan(pieces, units):
    core, axis, hop, own = 2.2, 6.3, 2.0, 0.3
    free = {"x": 0.0, "y": 0.0, "z": 0.0}
    pending = []
    plan = []
    now = 0.0

    def advance(unit, step, at):
        size = unit["size"]
        if step == 0:
            return at + core * size
        if step == 1:
            lane, cost = unit["first"], axis
        elif unit["z_last"]:
            lane, cost = (unit["second"], axis / 2) if step == 2 else ("z", axis / 2)
        else:
            lane, cost = ("z", axis) if step == 2 else (unit["second"], axis / 8)
        start = max(at, free[lane])
        free[lane] = start + cost * size
        return start + cost * size + hop

    def serve(entry, steps):
        nonlocal now
        at, uid, step = entry
        now = max(now, at) + own
        steps.append((uid, step))
        if step < 4:
            pending.append((advance(units[uid], step, now), uid, step + 1))
            pending.sort()

    for name, cost in pieces:
        now += cost
        steps = []
        for unit in units:
            if unit["after"] == name:
                steps.append((unit["id"], 0))
                pending.append((advance(unit, 0, now), unit["id"], 1))
        pending.sort()
        while pending and pending[0][0] <= now:
            serve(pending.pop(0), steps)
        plan.append(steps)
    steps = []
    while pending:
        serve(pending.pop(0), steps)
    plan.append(steps)
    return plan, now


def unit_list(depth, groups, orders):
    names = (
        [("down", j, "down%d" % (depth - 1), 4 / 3) for j in range(3)]
        + [("up", u, "up%d" % u, 1.0) for u in range(4)]
        + [("proj", 4, "proj", 1.0)]
        + [("qkv", 5 + g, "dqkv%d" % g, 1.0) for g in range(groups)]
    )
    units = []
    for uid, ((kind, at, after, size), order) in enumerate(zip(names, orders)):
        units.append(
            {
                "id": uid, "kind": kind, "at": at, "after": after, "size": size, "z_last": order[2] == "z",
                "first": order[0], "second": order[1] if order[2] == "z" else order[2],
            }
        )
    return units


def piece_list(depth, groups, rows):
    pieces = [("down%d" % m, 1.5) for m in range(depth)]
    for j in range(4):
        pieces += [("up%d" % j, 2.6), ("first%d" % j, 1.6)]
    pieces += [("norm%d" % r, 1.5) for r in range(rows)] + [("proj", 1.5)]
    for g in range(groups):
        pieces += [("attn%d%d" % (g, i), 1.6) for i in range(2 * rows)] + [("dqkv%d" % g, 1.5), ("tok%d" % g, 1.6)]
    return pieces


ORDERS = ("xyz", "yxz", "xyz", "yxz", "xyz", "yxz", "xyz", "yxz", "xyz", "yxz", "xyz")


def colsum(v):
    return jnp.sum(v, axis=0, keepdims=True)


def norm_back_k(grad_n, normed, inv_std):
    scale = 1.0 / grad_n.shape[-1]
    mean = jnp.sum(grad_n, axis=-1, keepdims=True) * scale
    dots = jnp.sum(grad_n * normed, axis=-1, keepdims=True) * scale
    return inv_std * (grad_n - mean - normed * dots)


def backward_kernel(
    depth,
    ids_ref, pair_ref, z_ref, invn_ref, cnt_ref, ag_ref, fg_ref,
    low_hbm, tok_hbm, n2_hbm, stat_hbm, act_hbm, der_hbm, wd_hbm, wu_hbm, n1_hbm, wp_hbm, rinv_hbm, ctx_hbm,
    qkv_hbm, exp_hbm, wqkv_hbm,
    tg_hbm, loss_ref, oq_ref, op_ref, ou_ref, od_ref, v_qb, v_vb, v_pb, v_ag, v_as, v_ub, v_db, v_fg, v_fs,
    w_s, wd_s, rc_s, rcd_s, r2_s, r2d_s, q_s, qd_s,
    all_s, low_t, tok_t, tok_s, stream_s, g_s, ctx_s, rdo_s, qg_s, exp_s, gq_s, tg_s, wst_s, wp_s, stat_s,
    ar0_s, ar1_s, ar2_s, br0_s, br1_s, br2_s,
    send_sem, recv_sem, gsend_sem, grecv_sem, asend_sem, arecv_sem, in_sem, str_sem, wst_sem, grp_sem, exp_sem, out_sem,
):
    toks, width = tok_s.shape
    half = width // 2
    ff = act_hbm.shape[1]
    kinds = ff // width
    row_len = exp_s.shape[3]
    rows = toks // row_len
    strip = width // (8 * depth)
    groups = width // (2 * PAIR)
    seg_here = z_ref.shape[0]
    me = lax.axis_index("batch")
    c = lax.rem(me, 2)
    x = lax.rem(me // 2, 2)
    y = lax.rem(me // 4, 2)
    z = me // 8
    xy = y * 2 + x

    def index(zz, yy, xx, cc):
        return ((zz * 2 + yy) * 2 + xx) * 2 + cc

    core_peer = index(z, y, x, 1 - c)
    x_peer = index(z, y, 1 - x, c)
    y_peer = index(z, 1 - y, x, c)
    xy_peer = index(z, 1 - y, 1 - x, c)
    z_peers = [index(lax.rem(z + step, depth), y, x, c) for step in range(1, depth)]
    everyone = [core_peer, x_peer, y_peer, xy_peer] + z_peers

    barrier = pltpu.get_barrier_semaphore()
    for other in everyone:
        pl.semaphore_signal(barrier, inc=1, device_id=(other,), device_id_type=MESH)

    local = pltpu.make_async_copy

    def stream(k):
        src = act_hbm if k < depth else der_hbm
        off = (k % depth if k < depth else k - depth) * width
        return local(src.at[:, off : off + width], stream_s.at[k % 2], str_sem.at[k % 2])

    def ffn_weights(j):
        at = (j % 2) * 2
        return [
            local(wd_hbm.at[j * width : (j + 1) * width, :], wst_s.at[at], wst_sem.at[at]),
            local(wu_hbm.at[:, j * width : (j + 1) * width], wst_s.at[at + 1], wst_sem.at[at + 1]),
        ]

    def group_loads(g):
        return [
            local(
                qkv_hbm.at[:, third * width + g * 2 * PAIR : third * width + (g + 1) * 2 * PAIR],
                qg_s.at[g % 2, :, third * 2 * PAIR : (third + 1) * 2 * PAIR],
                grp_sem.at[(g % 2) * 3 + third],
            )
            for third in range(3)
        ]

    def weight_loads(g):
        return [
            local(
                wqkv_hbm.at[:, third * width + g * 2 * PAIR : third * width + (g + 1) * 2 * PAIR],
                wst_s.at[g, :, third * 2 * PAIR : (third + 1) * 2 * PAIR],
                wst_sem.at[4 + g * 3 + third],
            )
            for third in range(3)
        ]

    def exp_load(r, p, slot):
        return local(exp_hbm.at[r * (width // PAIR) + p], exp_s.at[slot], exp_sem.at[slot])

    low_load = local(low_hbm, tok_s, in_sem.at[0])
    tok_load = local(tok_hbm, tok_s, in_sem.at[1])
    n2_load = local(n2_hbm, gq_s, in_sem.at[2])
    stat_load = local(stat_hbm, stat_s, in_sem.at[3])
    n1_load = local(n1_hbm, qg_s.at[1], in_sem.at[4])
    rinv_load = local(rinv_hbm, tok_s, in_sem.at[5])
    wp_load = local(wp_hbm, wp_s, in_sem.at[6])
    ctx_load = local(ctx_hbm, ctx_s, in_sem.at[7])
    low_load.start()
    n2_load.start()
    stat_load.start()
    stream(0).start()
    stream(1).start()
    for j in range(2):
        for cp in ffn_weights(j):
            cp.start()
    n1_load.start()
    wp_load.start()
    ctx_load.start()
    for cp in group_loads(0):
        cp.start()
    exp_load(0, 0, 0).start()

    def remote(src, dst, slot, device, ssem=send_sem, rsem=recv_sem):
        return pltpu.make_async_remote_copy(
            src_ref=src, dst_ref=dst, send_sem=ssem.at[slot], recv_sem=rsem.at[slot], device_id=(device,), device_id_type=MESH
        )

    pair_row = jnp.broadcast_to(pair_ref[...].reshape(1, seg_here), (seg_here, seg_here))
    here = lax.broadcasted_iota(jnp.int32, (seg_here, seg_here), 0) == lax.broadcasted_iota(
        jnp.int32, (seg_here, seg_here), 1
    )
    as_column = lambda v: jnp.sum(jnp.where(here, v.astype(F32), 0.0), axis=1, keepdims=True)
    lane = lax.broadcasted_iota(jnp.int32, (seg_here, 128), 1)
    tag = jnp.where(lane == 0, as_column(pair_row // 256), 0.0) + jnp.where(lane == 1, as_column(pair_row % 256), 0.0)
    msg = jnp.concatenate([z_ref[...].astype(BF16), tag.astype(BF16)], axis=1)
    all_s[z, xy, c] = msg

    def gather(stage):
        if stage == 0:
            ref, others = all_s.at[z, xy, c], z_peers
        elif stage == 1:
            ref, others = all_s.at[:, xy, c], [x_peer, y_peer, xy_peer]
        else:
            ref, others = all_s.at[:, :, c], [core_peer]
        base = (0, depth - 1, depth + 2)[stage]
        return [remote(ref, ref, base + k, other, gsend_sem, grecv_sem) for k, other in enumerate(others)]

    pl.semaphore_wait(barrier, len(everyone))
    for cp in gather(0):
        cp.start()
    low_load.wait()
    low_t[...] = jnp.transpose(tok_s[...])
    tok_load.start()
    for cp in gather(0):
        cp.wait_recv()
    for cp in gather(1):
        cp.start()
    tok_load.wait()
    tok_t[...] = jnp.transpose(tok_s[...])
    rinv_load.start()
    for cp in gather(1):
        cp.wait_recv()
    for cp in gather(2):
        cp.start()
    br0_s[z] = jnp.zeros(br0_s.shape[1:], F32)
    ar0_s[z] = jnp.zeros(ar0_s.shape[1:], F32)
    for cp in gather(2):
        cp.wait_recv()
    loss, grad_seg = contrast_math(
        all_s[...].reshape(8 * depth * seg_here, msg.shape[1]), msg, me, z_ref[...], invn_ref[:, 0:1], cnt_ref[:, 0:1]
    )
    loss_ref[...] = jnp.broadcast_to(loss, loss_ref.shape)

    units = unit_list(depth, groups, ORDERS)
    pieces = piece_list(depth, groups, rows)
    plan, _ = event_plan(pieces, units)
    places = [name for name, _ in pieces]

    def bufs(unit):
        if unit["kind"] == "down":
            return [ref.at[unit["at"]] for ref in (wd_s, rcd_s, r2d_s, qd_s)]
        return [ref.at[unit["at"]] for ref in (w_s, rc_s, r2_s, q_s)]

    def unit_copies(unit, step):
        w, rc, r2, q = bufs(unit)
        f, s = (x, y) if unit["first"] == "x" else (y, x)
        f_peer, s_peer = (x_peer, y_peer) if unit["first"] == "x" else (y_peer, x_peer)
        base = unit["id"] * (2 + depth)
        if step == 0:
            return [remote(w.at[1 - c], rc, base, core_peer)]
        if step == 1:
            return [remote(w.at[c, 1 - f], r2, base + 1, f_peer)]
        if unit["z_last"]:
            if step == 2:
                return [remote(w.at[c, f, 1 - s], q.at[0], base + 2, s_peer)]
            return [
                remote(w.at[c, f, s, lax.rem(z + k, depth)], q.at[1, z], base + 2 + k, z_peers[k - 1])
                for k in range(1, depth)
            ]
        if step == 2:
            return [
                remote(w.at[c, f, :, lax.rem(z + k, depth)], q.at[:, z], base + 2 + k, z_peers[k - 1])
                for k in range(1, depth)
            ]
        return [remote(w.at[c, f, 1 - s, z], q.at[0, z], base + 2, s_peer)]

    def finish(unit, total):
        kind, at = unit["kind"], unit["at"]
        if kind == "down":
            per = width // 128
            for k in range(4):
                start = (k // 2) * UNIT_ROWS * per + at * 2 + k % 2
                od_ref[pl.ds(start, UNIT_ROWS, stride=per), :] = total[:, k * 128 : (k + 1) * 128]
            return
        for k in range(6):
            piece = total[(k // 3) * strip : (k // 3 + 1) * strip, (k % 3) * 128 : (k % 3 + 1) * 128]
            if kind == "up":
                ref, per, col = ou_ref, ff // 128, at * 6 + k
            elif kind == "proj":
                ref, per, col = op_ref, width // 128, k
            else:
                ref, per, col = oq_ref, 3 * width // 128, (k // 2) * (width // 128) + (at - 5) * 2 + k % 2
            ref[pl.ds(col, strip, stride=per), :] = piece

    def take(unit, step):
        w, rc, r2, q = bufs(unit)
        f, s = (x, y) if unit["first"] == "x" else (y, x)
        z_last = unit["z_last"]
        if step > 0:
            for cp in unit_copies(unit, step - 1):
                cp.wait_recv()
        f32 = lambda v: v.astype(F32)
        two = lambda a, b: f32(w[c, f, a, b]) + f32(rc[f, a, b]) + f32(r2[a, b])
        if step == 1:

            def body(i, carry):
                a, b = i // depth, lax.rem(i, depth)
                w[c, 1 - f, a, b] = (f32(w[c, 1 - f, a, b]) + f32(rc[1 - f, a, b])).astype(BF16)
                return carry

            lax.fori_loop(0, 2 * depth, body, 0)
        elif step == 2 and z_last:

            def body(b, carry):
                w[c, f, 1 - s, b] = two(1 - s, b).astype(BF16)
                return carry

            lax.fori_loop(0, depth, body, 0)
        elif step == 3 and z_last:

            def body(k, carry):
                b = lax.rem(z + k, depth)
                w[c, f, s, b] = (two(s, b) + f32(q[0, b])).astype(BF16)
                return carry

            lax.fori_loop(1, depth, body, 0)
        elif step == 2:

            def body(k, carry):
                b = lax.rem(z + 1 + k // 2, depth)
                a = lax.rem(k, 2)
                w[c, f, a, b] = two(a, b).astype(BF16)
                return carry

            lax.fori_loop(0, 2 * (depth - 1), body, 0)
        elif step == 3:
            total = two(1 - s, z)
            for k in range(1, depth):
                total = total + f32(q[1 - s, lax.rem(z + k, depth)])
            w[c, f, 1 - s, z] = total.astype(BF16)
        elif step == 4:
            total = two(s, z) + f32(q[0, z])
            for k in range(1, depth):
                total = total + f32(q[1 if z_last else s, lax.rem(z + k, depth)])
            finish(unit, total)
        if step < 4:
            for cp in unit_copies(unit, step):
                cp.start()

    def after(name):
        for uid, step in plan[places.index(name)]:
            take(units[uid], step)

    def vec_copies(which, stage):
        bank = ((ar0_s, ar1_s, ar2_s), (br0_s, br1_s, br2_s))[which][stage]
        base = which * (depth + 3) + (0, depth - 1, depth + 2)[stage]
        slot, others = ((z, z_peers), (xy, [x_peer, y_peer, xy_peer]), (c, [core_peer]))[stage]
        return [
            remote(bank.at[slot], bank.at[slot], base + k, other, asend_sem, arecv_sem) for k, other in enumerate(others)
        ]

    def vec_step(which, step):
        banks = ((ar0_s, ar1_s, ar2_s), (br0_s, br1_s, br2_s))[which]
        total = None
        if step > 0:
            for cp in vec_copies(which, step - 1):
                cp.wait_recv()
            bank = banks[step - 1]
            total = bank[0]
            for k in range(1, bank.shape[0]):
                total = total + bank[k]
        if step < 3:
            if step > 0:
                banks[step][xy if step == 1 else c] = total
            for cp in vec_copies(which, step):
                cp.start()
        elif which == 0:
            for k, ref in enumerate((v_fg, v_fs, v_db, v_ag, v_as, v_pb)):
                ref[...] = total[k : k + 1].reshape(width)
            v_ub[...] = jnp.concatenate([total[6 + k : 7 + k] for k in range(kinds)], axis=1).reshape(ff)
        else:
            v_qb[...] = total[0:1].reshape(width)
            v_vb[...] = total[1:2].reshape(width)

    def put_unit(unit, res):
        w = bufs(unit)[0]
        for d in range(8 * depth):
            cc, xx, yy, zz = d % 2, d // 2 % 2, d // 4 % 2, d // 8
            f, s = (xx, yy) if unit["first"] == "x" else (yy, xx)
            piece = res[d * strip : (d + 1) * strip]
            w[cc, f, s, zz] = jnp.concatenate([piece[:, :half], piece[:, half:]], axis=0).astype(BF16)

    n2_load.wait()
    stat_load.wait()
    ones_row = jnp.ones((8, row_len), BF16)
    ones8 = jnp.ones((8, toks), BF16)
    for r in range(rows):
        rsl = slice(r * row_len, (r + 1) * row_len)
        seg = lax.broadcasted_iota(jnp.int32, (SEGS, row_len), 0)
        member = (seg == ids_ref[r : r + 1, :]).astype(BF16)
        gp = grad_seg[r * SEGS : (r + 1) * SEGS, :]
        high = gp.astype(BF16)
        rest = (gp - high.astype(F32)).astype(BF16)
        grad_y = dot_tn(member, high) + dot_tn(member, rest)
        n2 = gq_s[rsl, :].astype(F32)
        ar0_s[z, 0:1, :] += colsum(grad_y * n2)
        ar0_s[z, 1:2, :] += colsum(grad_y)
        grad_r2 = norm_back_k(grad_y * fg_ref[...].reshape(1, width), n2, stat_s[rsl, 1:2])
        gdl = grad_r2.astype(BF16)
        tg_s[rsl, :] = grad_r2
        g_s[rsl, :] = gdl
        ar0_s[z, 2:3, :] += dot_nn(ones_row, gdl)[0:1]

    for m in range(depth):
        stream(m).wait()
        res = dot_tn(stream_s[m % 2], g_s[...])
        stream(m + 2).start()
        for i in range(8):
            cc, xx, yy = i % 2, i // 2 % 2, i // 4
            piece = res[i * 2 * UNIT_ROWS : (i + 1) * 2 * UNIT_ROWS]
            for j in range(3):
                f, s = (xx, yy) if units[j]["first"] == "x" else (yy, xx)
                blk = piece[:, j * 256 : (j + 1) * 256]
                wd_s[j, cc, f, s, m] = jnp.concatenate([blk[:UNIT_ROWS], blk[UNIT_ROWS:]], axis=1).astype(BF16)
        after("down%d" % m)

    for j in range(kinds):
        at = (j % 2) * 2
        loads = ffn_weights(j)
        loads[0].wait()
        stream(depth + j).wait()
        for b in range(3):
            bsl = slice(b * 256, (b + 1) * 256)
            grad_act = dot_nt(g_s[...], wst_s[at, bsl, :])
            gq_s[:, bsl] = (grad_act * stream_s[(depth + j) % 2, :, bsl].astype(F32)).astype(BF16)
        if j + 2 < kinds:
            stream(depth + j + 2).start()
        ar0_s[z, 6 + j : 7 + j, :] = dot_nn(ones8, gq_s[...])[0:1]
        put_unit(units[3 + j], dot_nn(low_t[...], gq_s[...]))
        after("up%d" % j)
        loads[1].wait()
        for b in range(3):
            bsl = slice(b * 256, (b + 1) * 256)
            tg_s[:, bsl] += dot_nt(gq_s[...], wst_s[at + 1, bsl, :])
        if j + 2 < kinds:
            for cp in ffn_weights(j + 2):
                cp.start()
        after("first%d" % j)

    for g in range(groups):
        for cp in weight_loads(g):
            cp.start()
    n1_load.wait()
    wp_load.wait()
    rinv_load.wait()
    for r in range(rows):
        rsl = slice(r * row_len, (r + 1) * row_len)
        grad_first = tg_s[rsl, :]
        n1 = qg_s[1, rsl, :].astype(F32)
        ar0_s[z, 3:4, :] += colsum(grad_first * n1)
        ar0_s[z, 4:5, :] += colsum(grad_first)
        grad_r1 = norm_back_k(grad_first * ag_ref[...].reshape(1, width), n1, stat_s[rsl, 0:1])
        tg_s[rsl, :] = grad_r1
        gal = grad_r1.astype(BF16)
        g_s[rsl, :] = gal
        ar0_s[z, 5:6, :] += dot_nn(ones_row, gal)[0:1]
        grad_ctx = dot_nt(gal, wp_s[...]).astype(BF16)
        rdo_s[rsl, :] = (grad_ctx.astype(F32) * tok_s[rsl, :].astype(F32)).astype(BF16)
        after("norm%d" % r)
    vec_step(0, 0)
    ctx_load.wait()
    put_unit(units[7], dot_tn(ctx_s[...], g_s[...]))
    after("proj")

    lane = lax.broadcasted_iota(jnp.int32, (row_len, 2 * PAIR), 1)
    first = lax.rem(lane, PAIR) < HEAD_DIM
    ones = jnp.ones((row_len, PAIR), BF16)
    scale = HEAD_DIM**-0.5
    for g in range(groups):
        for cp in group_loads(g):
            cp.wait()
        if g + 1 < groups:
            for cp in group_loads(g + 1):
                cp.start()

        def attend(i, carry):
            r, pp = i // 2, lax.rem(i, 2)
            slot = lax.rem(i, 2)
            exp_load(r, 2 * g + pp, slot).wait()

            @pl.when(i + 1 < 2 * rows)
            def _():
                exp_load((i + 1) // 2, 2 * g + lax.rem(i + 1, 2), 1 - slot).start()

            if g + 1 < groups:

                @pl.when(i + 1 == 2 * rows)
                def _():
                    exp_load(0, 2 * (g + 1), 0).start()

            rsl = pl.ds(pl.multiple_of(r * row_len, row_len), row_len)
            lanes = lambda base: pl.ds(pl.multiple_of(base + pp * PAIR, PAIR), PAIR)
            q = qg_s[g % 2, rsl, lanes(0)]
            k = qg_s[g % 2, rsl, lanes(2 * PAIR)]
            v = qg_s[g % 2, rsl, lanes(4 * PAIR)]
            do = rdo_s[rsl, lanes(g * 2 * PAIR)]
            ctx = ctx_s[rsl, lanes(g * 2 * PAIR)]
            neg = -(do.astype(F32) * ctx.astype(F32))
            lhs = jnp.concatenate([do, neg.astype(BF16)], axis=1)
            rhs = jnp.concatenate([v, ones], axis=1)
            do_t = jnp.transpose(do)
            q_t = jnp.transpose(q)
            dq, dk, dv = [], [], []
            for h in range(2):
                lh = jnp.where(first if h == 0 else ~first, lhs, jnp.zeros_like(lhs))
                e = exp_s[slot, h]
                ds = (e.astype(F32) * dot_nt(lh, rhs)).astype(BF16)
                hs = slice(h * HEAD_DIM, (h + 1) * HEAD_DIM)
                dv.append(dot_nn(do_t[hs], e))
                dk.append(dot_nn(q_t[hs], ds))
                dq.append(dot_nn(ds, k))
            gq_s[rsl, lanes(0)] = (jnp.where(first[:, :PAIR], dq[0], dq[1]) * scale).astype(BF16)
            gq_s[rsl, lanes(2 * PAIR)] = jnp.transpose((jnp.concatenate(dk, axis=0) * scale).astype(BF16))
            gq_s[rsl, lanes(4 * PAIR)] = jnp.transpose(jnp.concatenate(dv, axis=0).astype(BF16))
            for step in range(2 * rows):
                if plan[places.index("attn%d%d" % (g, step))]:

                    @pl.when(i == step)
                    def _():
                        after("attn%d%d" % (g, step))

            return carry

        lax.fori_loop(0, 2 * rows, attend, 0)
        put_unit(units[8 + g], dot_nn(tok_t[...], gq_s[...]))
        after("dqkv%d" % g)
        bias = dot_nn(ones8, gq_s[...])
        br0_s[z, 0:1, g * 2 * PAIR : (g + 1) * 2 * PAIR] = bias[0:1, : 2 * PAIR]
        br0_s[z, 1:2, g * 2 * PAIR : (g + 1) * 2 * PAIR] = bias[0:1, 4 * PAIR :]
        if g == groups - 1:
            vec_step(1, 0)
        for cp in weight_loads(g):
            cp.wait()
        for b in range(3):
            bsl = slice(b * 256, (b + 1) * 256)
            tg_s[:, bsl] += dot_nt(gq_s[...], wst_s[g, bsl, :])
        vec_step(0, g + 1)
        after("tok%d" % g)
    tg_out = local(tg_s, tg_hbm, out_sem)
    tg_out.start()
    left = plan[-1]
    marks = {len(left) * (k + 1) // 4: k + 1 for k in range(3)}
    for k, (uid, step) in enumerate(left):
        if k in marks:
            vec_step(1, marks[k])
        take(units[uid], step)
    for stage in range(3):
        for cp in gather(stage):
            cp.wait_send()
    for step in range(4):
        for unit in units:
            for cp in unit_copies(unit, step):
                cp.wait_send()
    for which in range(2):
        for stage in range(3):
            for cp in vec_copies(which, stage):
                cp.wait_send()
    tg_out.wait()


def backward_call(n, ids, pair, zed, invn, cnt, ag, fg, low, tok, n2, stat, act, der, wd, wu, n1, wp, rinv, ctx, qkv, exps, wqkv):
    depth = n // 8
    toks, width = tok.shape
    ff = act.shape[1]
    row_len = exps.shape[2]
    groups = width // (2 * PAIR)
    half = width // 2
    segs = zed.shape[0]
    sds = jax.ShapeDtypeStruct
    vm = pl.BlockSpec(memory_space=pltpu.VMEM)
    hb = pl.BlockSpec(memory_space=pl.ANY)
    flat = lambda cols, rws: sds((rws // n * cols // 128, 128), F32)
    v = lambda k: sds((k,), F32)
    wide = lambda *lead: [pltpu.VMEM((8,) + lead + (UNIT_ROWS, half), BF16), pltpu.VMEM((3,) + lead + (UNIT_ROWS, 512), BF16)]
    big = pltpu.VMEM((toks, width), BF16)
    turned = pltpu.VMEM((width, toks), BF16)
    sem = lambda k: pltpu.SemaphoreType.DMA((k,))
    scratch = wide(2, 2, 2, depth) + wide(2, 2, depth) + wide(2, depth) + wide(2, depth)
    scratch += [
        pltpu.VMEM((depth, 4, 2, segs, width + 128), BF16),
        turned,
        turned,
        big,
        pltpu.VMEM((2, toks, width), BF16),
        big,
        big,
        big,
        pltpu.VMEM((2, toks, 6 * PAIR), BF16),
        pltpu.VMEM((2, 2, row_len, row_len), BF16),
        big,
        pltpu.VMEM((toks, width), F32),
        pltpu.VMEM((4, width, width), BF16),
        pltpu.VMEM((width, width), BF16),
        pltpu.VMEM((toks, 128), F32),
        pltpu.VMEM((depth, 16, width), F32),
        pltpu.VMEM((4, 16, width), F32),
        pltpu.VMEM((2, 16, width), F32),
        pltpu.VMEM((depth, 8, width), F32),
        pltpu.VMEM((4, 8, width), F32),
        pltpu.VMEM((2, 8, width), F32),
        sem(11 * (2 + depth)),
        sem(11 * (2 + depth)),
        sem(depth + 3),
        sem(depth + 3),
        sem(2 * (depth + 3)),
        sem(2 * (depth + 3)),
        sem(8),
        sem(2),
        sem(4 + 3 * groups),
        sem(6),
        sem(2),
        pltpu.SemaphoreType.DMA,
    ]
    return pl.pallas_call(
        functools.partial(backward_kernel, depth),
        out_shape=(
            sds((toks, width), F32), sds((8, 128), F32),
            flat(3 * width, width), flat(width, width), flat(ff, width), flat(width, ff),
            v(width), v(width), v(width), v(width), v(width), v(ff), v(width), v(width), v(width),
        ),
        in_specs=[vm] * 7 + [hb] * 15,
        out_specs=[hb] + [vm] * 14,
        scratch_shapes=scratch,
        compiler_params=pltpu.CompilerParams(collective_id=1, has_side_effects=True, vmem_limit_bytes=63 * MIB),
        name="backward",
    )(ids, pair, zed, invn, cnt, ag, fg, low, tok, n2, stat, act, der, wd, wu, n1, wp, rinv, ctx, qkv, exps, wqkv)


def deliver_kernel(big_ref, loss_ref, *refs):
    count = (len(refs) - 4) // 2
    big_out, loss_out = refs[count : count + 2]
    held, sems = refs[-2:]
    parts = sems.shape[0] // 2
    step = held.shape[0] // parts
    loads, stores = [], []
    for k in range(parts):
        rsl = slice(k * step, (k + 1) * step)
        loads.append(pltpu.make_async_copy(big_ref.at[rsl], held.at[rsl], sems.at[k]))
        stores.append(pltpu.make_async_copy(held.at[rsl], big_out.at[rsl], sems.at[parts + k]))
    for cp in loads:
        cp.start()
    for i in range(count):
        refs[count + 2 + i][...] = refs[i][...]
    loss_out[0] = loss_ref[0, 0]
    for load, store in zip(loads, stores):
        load.wait()
        store.start()
    for cp in stores:
        cp.wait()


def deliver_call(arrays):
    hb = pl.BlockSpec(memory_space=pl.ANY)
    vm = pl.BlockSpec(memory_space=pltpu.VMEM)
    big, loss, *rest = arrays
    same = [jax.ShapeDtypeStruct(a.shape, a.dtype) for a in rest]
    return pl.pallas_call(
        deliver_kernel,
        out_shape=tuple([jax.ShapeDtypeStruct(big.shape, big.dtype), jax.ShapeDtypeStruct((1,), F32)] + same),
        in_specs=[hb] + [vm] * (len(rest) + 1),
        out_specs=[hb, pl.BlockSpec(memory_space=pltpu.SMEM)] + [vm] * len(rest),
        scratch_shapes=[pltpu.VMEM(big.shape, big.dtype), pltpu.SemaphoreType.DMA((16,))],
        name="deliver",
    )(*arrays)

def norm_back(grad_out, normed, inv_std, gain):
    grad_n = grad_out * gain
    return inv_std * (
        grad_n
        - jnp.mean(grad_n, axis=-1, keepdims=True)
        - normed * jnp.mean(grad_n * normed, axis=-1, keepdims=True)
    )


def attend_back(entry):
    qkv_row, exps, rinv, ctx, grad_row = entry
    row_len = qkv_row.shape[0]
    split = qkv_row.reshape(row_len, 3, HEADS, HEAD_DIM)
    queries, key_vecs, values = split[:, 0], split[:, 1], split[:, 2]
    exps = exps.reshape(HEADS, row_len, row_len)
    scaled = (grad_row.astype(F32) * rinv.astype(F32)).astype(BF16)
    delta = jnp.sum(scaled.astype(F32).reshape(row_len, HEADS, HEAD_DIM) * ctx.astype(F32).reshape(row_len, HEADS, HEAD_DIM), axis=-1)
    scaled = scaled.reshape(row_len, HEADS, HEAD_DIM)
    grad_probs = jnp.einsum("qhd,khd->hqk", scaled, values, preferred_element_type=F32)
    grad_values = jnp.einsum("hqk,qhd->khd", exps, scaled, preferred_element_type=F32)
    grad_scores = (exps.astype(F32) * (grad_probs - delta.T[..., None])).astype(BF16)
    grad_queries = jnp.einsum("hqk,khd->qhd", grad_scores, key_vecs, preferred_element_type=F32) * HEAD_DIM**-0.5
    grad_keys = jnp.einsum("hqk,qhd->khd", grad_scores, queries, preferred_element_type=F32) * HEAD_DIM**-0.5
    stacked = jnp.stack([grad_queries, grad_keys, grad_values], axis=1)
    return stacked.reshape(row_len, 3 * HEADS * HEAD_DIM).astype(BF16)


def per_device(
    tokens, segment_ids, pair_index, qkv_weight, query_bias, value_bias, proj_weight, proj_bias,
    attn_gain, attn_shift, up_weight, up_bias, down_weight, down_bias, ffn_gain, ffn_shift,
):
    n = lax.axis_size("batch")
    rows, row_len = segment_ids.shape
    toks, width = tokens.shape
    (exps, qkv, context, rinv, normed_one, first_low, acted, deriv, normed_two, layer_out, stat, z, invn, cnt) = forward_call(
        tokens, segment_ids, qkv_weight, query_bias, value_bias, proj_weight, proj_bias, attn_gain, attn_shift,
        up_weight, up_bias, down_weight, down_bias, ffn_gain, ffn_shift)
    if width % (8 * n) == 0 and n // 8 * 2 * UNIT_ROWS * 8 == up_weight.shape[1]:
        grads = deliver_call(backward_call(
            n, segment_ids, pair_index, z, invn, cnt, attn_gain, ffn_gain, first_low, tokens, normed_two, stat, acted,
            deriv, down_weight, up_weight, normed_one, proj_weight, rinv, context, qkv, exps, qkv_weight))
        return (grads[1].reshape(()), layer_out, grads[0]) + tuple(v.reshape(-1) for v in grads[2:])
    loss, grad_seg = contrast_call(n, z.astype(BF16), z, invn, cnt, pair_index)
    inv_one = stat[:, :1]
    inv_two = stat[:, 1:2]
    normed_one = normed_one.astype(F32)
    normed_two = normed_two.astype(F32)
    row_base = (jnp.arange(rows, dtype=jnp.int32) * SEGS)[:, None]
    local_ids = jnp.where(segment_ids >= 0, segment_ids + row_base, -1).reshape(toks)
    member = (local_ids[None, :] == jnp.arange(rows * SEGS, dtype=jnp.int32)[:, None]).astype(F32)
    grad_y = lax.dot_general(member, grad_seg, (((0,), (0,)), ((), ())), precision=lax.Precision.HIGHEST)
    ffn_gain_part = jnp.sum(grad_y * normed_two, axis=0)
    ffn_shift_part = jnp.sum(grad_y, axis=0)
    grad_r2 = norm_back(grad_y, normed_two, inv_two, ffn_gain)
    grad_down_low = grad_r2.astype(BF16)
    down_bias_part = jnp.sum(grad_down_low.astype(F32), axis=0)
    down_weight_part = dot_tn(acted, grad_down_low)
    grad_up_low = (dot_nt(grad_down_low, down_weight) * deriv.astype(F32)).astype(BF16)
    up_bias_part = jnp.sum(grad_up_low.astype(F32), axis=0)
    up_weight_part = dot_tn(first_low, grad_up_low)
    grad_first = grad_r2 + dot_nt(grad_up_low, up_weight)
    attn_gain_part = jnp.sum(grad_first * normed_one, axis=0)
    attn_shift_part = jnp.sum(grad_first, axis=0)
    grad_r1 = norm_back(grad_first, normed_one, inv_one, attn_gain)
    grad_att_low = grad_r1.astype(BF16)
    proj_bias_part = jnp.sum(grad_att_low.astype(F32), axis=0)
    proj_weight_part = dot_tn(context, grad_att_low)
    grad_context = dot_nt(grad_att_low, proj_weight).astype(BF16)
    by_row = lambda v: v.reshape(rows, row_len, -1)
    grad_qkv = lax.map(
        attend_back,
        (by_row(qkv), exps.reshape(rows, -1, 2, row_len, row_len), by_row(rinv), by_row(context), by_row(grad_context)),
    ).reshape(toks, 3 * width)
    qkv_bias_part = jnp.sum(grad_qkv.astype(F32), axis=0)
    qkv_weight_part = dot_tn(tokens, grad_qkv)
    tokens_grad = grad_r1 + dot_nt(grad_qkv, qkv_weight)
    scatter = lambda v: lax.psum_scatter(v.reshape(-1), "batch", scatter_dimension=0, tiled=True)
    sums = lax.psum(
        (qkv_bias_part[:width], qkv_bias_part[2 * width :], proj_bias_part, attn_gain_part, attn_shift_part,
         up_bias_part, down_bias_part, ffn_gain_part, ffn_shift_part),
        "batch",
    )
    return (loss[0, 0], layer_out, tokens_grad, scatter(qkv_weight_part), scatter(proj_weight_part),
            scatter(up_weight_part), scatter(down_weight_part)) + tuple(sums)


def solution(mesh):
    split, whole = P("batch"), P()
    return jax.shard_map(
        per_device,
        mesh=mesh,
        in_specs=(P("batch", None), P("batch", None), split) + (whole,) * 13,
        out_specs=(whole, P("batch", None), P("batch", None)) + (split,) * 4 + (whole,) * 9,
        check_vma=False,
    )
```

```python
import functools
import jax
import jax.numpy as jnp
from jax import lax
from jax.experimental import pallas as pl
from jax.experimental.pallas import tpu as pltpu
from jax.sharding import PartitionSpec as P

F32 = jnp.float32
BF16 = jnp.bfloat16
HEADS = 12
HEAD_DIM = 64
SEGS = 8
PAIR = 2 * HEAD_DIM
LN_EPS = 1e-12
NORM_EPS = 1e-06
MIB = 2**20


def dot_nn(a, b):
    return lax.dot_general(a, b, (((1,), (0,)), ((), ())), preferred_element_type=F32)


def dot_nt(a, b):
    return lax.dot_general(a, b, (((1,), (1,)), ((), ())), preferred_element_type=F32)


def dot_tn(a, b):
    return lax.dot_general(a, b, (((0,), (0,)), ((), ())), preferred_element_type=F32)


def gelu_parts(pre):
    half = 0.5 * pre
    cdf = 0.5 + 0.5 * lax.erf(pre * 0.7071067811865476)
    pdf = jnp.exp(-half * pre) * 0.3989422804014327
    return pre * cdf, cdf + pre * pdf


def normalize(resid):
    width = resid.shape[-1]
    average = jnp.sum(resid, axis=-1, keepdims=True) * (1.0 / width)
    centred = resid - average
    variance = jnp.sum(centred * centred, axis=-1, keepdims=True) * (1.0 / width)
    inv_std = lax.rsqrt(variance + LN_EPS)
    return centred * inv_std, inv_std


def forward_kernel(
    ids_ref, qb_ref, vb_ref, pb_ref, ag_ref, as_ref, ub_ref, db_ref, fg_ref, fs_ref,
    tok_hbm, wqkv_hbm, wp_hbm, wu_hbm, wd_hbm,
    exp_hbm, qkv_hbm, ctx_hbm, rinv_hbm, n1_hbm, low_hbm, act_hbm, der_hbm, n2_hbm, out_hbm,
    stat_ref, z_ref, invn_ref, cnt_ref,
    tok_s, wqkv_s, wp_s, wu_s, wd_s, qkv_s, ctx_s, rinv_s, bias_s, exp_s,
    n1_s, low_s, act_s, der_s, n2_s, out_s, in_sem, out_sem, exp_sem,
):
    rows, row_len = ids_ref.shape
    toks, width = tok_s.shape
    pairs = width // PAIR
    ff = wu_s.shape[1]
    qb, vb, pb, ag, ash, db, fg, fs = (
        ref[...].reshape(1, width) for ref in (qb_ref, vb_ref, pb_ref, ag_ref, as_ref, db_ref, fg_ref, fs_ref)
    )
    ub = ub_ref[...].reshape(1, ff)

    thirds = [
        (wqkv_hbm.at[:, k * width : (k + 1) * width], wqkv_s.at[:, k * width : (k + 1) * width]) for k in range(3)
    ]
    loads = [
        pltpu.make_async_copy(src, dst, in_sem.at[i])
        for i, (src, dst) in enumerate([(tok_hbm, tok_s)] + thirds + [(wp_hbm, wp_s), (wu_hbm, wu_s), (wd_hbm, wd_s)])
    ]
    for cp in loads:
        cp.start()
    loads[0].wait()

    tok = tok_s[...]
    blk = 256
    for j in range(3 * width // blk):
        third, off = divmod(j * blk, width)
        if off == 0:
            loads[1 + third].wait()
        piece = dot_nn(tok, wqkv_s[:, j * blk : (j + 1) * blk])
        if third == 0:
            piece = piece + qb[:, off : off + blk]
        elif third == 2:
            piece = piece + vb[:, off : off + blk]
        qkv_s[:, j * blk : (j + 1) * blk] = piece.astype(BF16)
    qkv_out = pltpu.make_async_copy(qkv_s, qkv_hbm, out_sem.at[0])
    qkv_out.start()

    lane = lax.broadcasted_iota(jnp.int32, (row_len, PAIR), 1)
    first = lane < HEAD_DIM
    ones = jnp.ones((row_len, PAIR), BF16)

    for r in range(rows):
        ids_row = ids_ref[r : r + 1, :].astype(F32)
        ids_col = jnp.transpose(jnp.broadcast_to(ids_row, (128, row_len)))
        for c in range(row_len // 128):
            bias_s[r, :, c * 128 : (c + 1) * 128] = jnp.where(
                ids_col == ids_row[:, c * 128 : (c + 1) * 128], 0.0, -1e9
            )

    def exp_store(it, slot):
        return pltpu.make_async_copy(exp_s.at[slot], exp_hbm.at[pl.ds(2 * it, 2)], exp_sem.at[slot])

    def attend(it, carry):
        r = it // (pairs // 2)
        g = lax.rem(it, pairs // 2)
        rsl = pl.ds(pl.multiple_of(r * row_len, row_len), row_len)
        slot = lax.rem(it, 2)

        @pl.when(it >= 2)
        def _():
            exp_store(it - 2, slot).wait()

        for pp in range(2):
            col = lambda base: pl.ds(pl.multiple_of(base + (2 * g + pp) * PAIR, PAIR), PAIR)
            q = qkv_s[rsl, col(0)] * jnp.asarray(HEAD_DIM**-0.5, BF16)
            k = qkv_s[rsl, col(width)]
            v = jnp.concatenate([qkv_s[rsl, col(2 * width)], ones], axis=1)
            parts = []
            for h in range(2):
                qh = jnp.where(first if h == 0 else ~first, q, jnp.zeros_like(q))
                s = dot_nt(qh, k) + bias_s[r]
                e = jnp.exp(s - jnp.max(s, axis=1, keepdims=True)).astype(BF16)
                exp_s[slot, pp, h] = e
                oe = dot_nn(e, v)
                rinv = 1.0 / oe[:, PAIR:]
                parts.append((oe[:, :PAIR] * rinv, rinv))
            ctx_s[rsl, col(0)] = jnp.where(first, parts[0][0], parts[1][0]).astype(BF16)
            rinv_s[rsl, col(0)] = jnp.where(first, parts[0][1], parts[1][1]).astype(BF16)
        exp_store(it, slot).start()
        return carry

    lax.fori_loop(0, rows * pairs // 2, attend, 0)
    ctx_out = pltpu.make_async_copy(ctx_s, ctx_hbm, out_sem.at[1])
    ctx_out.start()
    rinv_out = pltpu.make_async_copy(rinv_s, rinv_hbm, out_sem.at[2])
    rinv_out.start()
    for cp in loads[4:]:
        cp.wait()

    outs = [(n1_s, n1_hbm), (low_s, low_hbm), (act_s, act_hbm), (der_s, der_hbm), (n2_s, n2_hbm), (out_s, out_hbm)]

    def store(i, rsl, csl=slice(None)):
        src, dst = outs[i]
        pltpu.make_async_copy(src.at[rsl, csl], dst.at[rsl, csl], out_sem.at[3 + i]).start()

    def ffn(r, carry):
        rsl = pl.ds(pl.multiple_of(r * row_len, row_len), row_len)
        resid = tok_s[rsl, :].astype(F32) + (dot_nn(ctx_s[rsl, :], wp_s[...]) + pb)
        normed, inv_std = normalize(resid)
        n1_s[rsl, :] = normed.astype(BF16)
        first_norm = normed * ag + ash
        low = first_norm.astype(BF16)
        low_s[rsl, :] = low
        store(0, rsl)
        store(1, rsl)
        for j in range(ff // blk):
            pre = dot_nn(low, wu_s[:, j * blk : (j + 1) * blk]) + ub[:, j * blk : (j + 1) * blk]
            act, der = gelu_parts(pre)
            act_s[rsl, j * blk : (j + 1) * blk] = act.astype(BF16)
            der_s[rsl, j * blk : (j + 1) * blk] = der.astype(BF16)
            if (j + 1) * blk % width == 0:
                store(2, rsl, slice((j + 1) * blk - width, (j + 1) * blk))
                store(3, rsl, slice((j + 1) * blk - width, (j + 1) * blk))
        down = dot_nn(act_s[rsl, :], wd_s[...]) + db
        normed2, inv_std2 = normalize(first_norm + down)
        n2_s[rsl, :] = normed2.astype(BF16)
        stat_ref[rsl, :] = jnp.where(lane == 0, inv_std, inv_std2)
        y = normed2 * fg + fs
        high = y.astype(BF16)
        out_s[rsl, :] = high
        rest = (y - high.astype(F32)).astype(BF16)
        seg = lax.broadcasted_iota(jnp.int32, (SEGS, row_len), 0)
        member = (seg == ids_ref[pl.ds(r, 1), :]).astype(F32)
        count = jnp.sum(member, axis=1, keepdims=True)
        member = member.astype(BF16)
        pooled = (dot_nn(member, high) + dot_nn(member, rest)) / count
        inv_norm = lax.rsqrt(jnp.sum(pooled * pooled, axis=1, keepdims=True) + NORM_EPS)
        z = pooled * inv_norm
        ssl = pl.ds(pl.multiple_of(r * SEGS, SEGS), SEGS)
        z_ref[ssl, :] = z
        invn_ref[ssl, :] = jnp.broadcast_to(inv_norm, (SEGS, 128))
        cnt_ref[ssl, :] = jnp.broadcast_to(count, (SEGS, 128))
        store(4, rsl)
        store(5, rsl)
        return carry

    lax.fori_loop(0, rows, ffn, 0)
    for i, (src, dst) in enumerate(outs):
        pltpu.make_async_copy(src, dst, out_sem.at[3 + i]).wait()
    qkv_out.wait()
    ctx_out.wait()
    rinv_out.wait()
    for slot in range(2):
        exp_store(slot, slot).wait()


def forward_call(tokens, ids, wqkv, qb, vb, wp, pb, ag, ash, wu, ub, wd, db, fg, fs):
    toks, width = tokens.shape
    rows, row_len = ids.shape
    ff = wu.shape[1]
    pairs = width // PAIR
    segs = rows * SEGS
    sds = jax.ShapeDtypeStruct
    vm = pl.BlockSpec(memory_space=pltpu.VMEM)
    hb = pl.BlockSpec(memory_space=pl.ANY)
    return pl.pallas_call(
        forward_kernel,
        out_shape=(
            sds((rows * pairs, 2, row_len, row_len), BF16),
            sds((toks, 3 * width), BF16),
            sds((toks, width), BF16),
            sds((toks, width), BF16),
            sds((toks, width), BF16),
            sds((toks, width), BF16),
            sds((toks, ff), BF16),
            sds((toks, ff), BF16),
            sds((toks, width), BF16),
            sds((toks, width), BF16),
            sds((toks, 128), F32),
            sds((segs, width), F32),
            sds((segs, 128), F32),
            sds((segs, 128), F32),
        ),
        in_specs=[vm] * 10 + [hb] * 5,
        out_specs=[hb] * 10 + [vm] * 4,
        scratch_shapes=[
            pltpu.VMEM((toks, width), BF16),
            pltpu.VMEM(wqkv.shape, BF16),
            pltpu.VMEM(wp.shape, BF16),
            pltpu.VMEM(wu.shape, BF16),
            pltpu.VMEM(wd.shape, BF16),
            pltpu.VMEM((toks, 3 * width), BF16),
            pltpu.VMEM((toks, width), BF16),
            pltpu.VMEM((toks, width), BF16),
            pltpu.VMEM((rows, row_len, row_len), F32),
            pltpu.VMEM((2, 2, 2, row_len, row_len), BF16),
            pltpu.VMEM((toks, width), BF16),
            pltpu.VMEM((toks, width), BF16),
            pltpu.VMEM((toks, ff), BF16),
            pltpu.VMEM((toks, ff), BF16),
            pltpu.VMEM((toks, width), BF16),
            pltpu.VMEM((toks, width), BF16),
            pltpu.SemaphoreType.DMA((7,)),
            pltpu.SemaphoreType.DMA((9,)),
            pltpu.SemaphoreType.DMA((2,)),
        ],
        compiler_params=pltpu.CompilerParams(vmem_limit_bytes=60 * MIB),
        name="forward",
    )(ids, qb, vb, pb, ag, ash, ub, db, fg, fs, tokens, wqkv, wp, wu, wd)

MESH = pl.DeviceIdType.MESH
INV_TEMP = 100.0
NEG = -1000000000.0


def axis_groups(n):
    groups = []
    rest = n // 2
    while rest > 1:
        size = 4 if rest % 4 == 0 else (2 if rest % 2 == 0 else rest)
        groups.append(size)
        rest //= size
    return groups + [2]


def digits_of(me, groups):
    digits = []
    for size in reversed(groups):
        digits.append(lax.rem(me, size))
        me = me // size
    return digits[::-1]


def index_of(digits, groups):
    me = 0
    for digit, size in zip(digits, groups):
        me = me * size + digit
    return me


def contrast_math(every, msg, me, z, invn, cnt):
    total, wide = every.shape
    seg_here, width = z.shape
    emb = every[:, :width]
    own = msg[:, :width]
    own_row = (me * seg_here).astype(F32)
    own_pair = msg[:, width : width + 128].astype(F32)
    own_pair = own_pair[:, 0:1] * 256.0 + own_pair[:, 1:2]

    scores = dot_nt(own, emb) * INV_TEMP
    column = lax.broadcasted_iota(jnp.int32, scores.shape, 1).astype(F32)
    row = lax.broadcasted_iota(jnp.int32, scores.shape, 0).astype(F32) + own_row
    masked = jnp.where(column == row, NEG, scores)
    peak = jnp.max(masked, axis=1, keepdims=True)
    log_norm = peak + jnp.log(jnp.sum(jnp.exp(masked - peak), axis=1, keepdims=True))
    weight = jnp.exp(masked - log_norm) - (column == own_pair).astype(F32)
    grad = dot_nn(weight.astype(BF16), emb)

    blk = min(total, 512)
    loss = jnp.zeros((1, 1), F32)
    for b in range(total // blk):
        part = emb[b * blk : (b + 1) * blk]
        pair = every[b * blk : (b + 1) * blk, width:].astype(F32)
        pair = pair[:, 0:1] * 256.0 + pair[:, 1:2]
        scores = dot_nt(part, emb) * INV_TEMP
        column = lax.broadcasted_iota(jnp.int32, scores.shape, 1).astype(F32)
        row = lax.broadcasted_iota(jnp.int32, scores.shape, 0).astype(F32) + float(b * blk)
        masked = jnp.where(column == row, NEG, scores)
        peak = jnp.max(masked, axis=1, keepdims=True)
        log_norm = peak + jnp.log(jnp.sum(jnp.exp(masked - peak), axis=1, keepdims=True))
        positive = jnp.sum(jnp.where(column == pair, scores, 0.0), axis=1, keepdims=True)
        loss = loss + jnp.sum(log_norm - positive, axis=0, keepdims=True)
        scores = dot_nt(part, own) * INV_TEMP
        column = lax.broadcasted_iota(jnp.int32, scores.shape, 1).astype(F32) + own_row
        row = lax.broadcasted_iota(jnp.int32, scores.shape, 0).astype(F32) + float(b * blk)
        weight = jnp.where(column == row, 0.0, jnp.exp(jnp.where(column == row, NEG, scores) - log_norm))
        weight = weight - (column == pair).astype(F32)
        grad = grad + dot_tn(weight.astype(BF16), part)
    grad = grad * INV_TEMP
    pooled_grad = invn * (grad - z * jnp.sum(grad * z, axis=1, keepdims=True))
    return loss * (1.0 / total), pooled_grad / cnt


def contrast_kernel(groups, msg_ref, z_ref, invn_ref, cnt_ref, loss_ref, gp_ref, all_s, send_sem, recv_sem):
    n = 1
    for size in groups:
        n *= size
    me = lax.axis_index("batch")
    mine = digits_of(me, groups)
    seg_here, wide = msg_ref.shape
    width = z_ref.shape[1]
    total = n * seg_here
    stages = len(groups)

    def peer(stage, step):
        other = lax.rem(mine[stage] + step, groups[stage])
        return other, index_of(mine[:stage] + [other] + mine[stage + 1 :], groups)

    barrier = pltpu.get_barrier_semaphore()
    hops = 0
    for stage in range(stages):
        for step in range(1, groups[stage]):
            pl.semaphore_signal(barrier, inc=1, device_id=(peer(stage, step)[1],), device_id_type=MESH)
            hops += 1
    all_s[tuple(mine)] = msg_ref[...]
    pl.semaphore_wait(barrier, hops)

    slot = 0
    for stage in range(stages):
        copies = []
        for step in range(1, groups[stage]):
            block = all_s.at[(slice(None),) * stage + tuple(mine[stage:])]
            copies.append(
                pltpu.make_async_remote_copy(
                    src_ref=block,
                    dst_ref=block,
                    send_sem=send_sem.at[slot],
                    recv_sem=recv_sem.at[slot],
                    device_id=(peer(stage, step)[1],),
                    device_id_type=MESH,
                )
            )
            slot += 1
        for cp in copies:
            cp.start()
        for cp in copies:
            cp.wait()

    loss, grad = contrast_math(
        all_s[...].reshape(total, wide), msg_ref[...], me, z_ref[...], invn_ref[:, 0:1], cnt_ref[:, 0:1]
    )
    loss_ref[...] = jnp.broadcast_to(loss, loss_ref.shape)
    gp_ref[...] = grad


def contrast_call(n, emb_low, z, invn, cnt, pair_index):
    groups = axis_groups(n)
    seg_here, width = emb_low.shape
    high = (pair_index // 256).astype(BF16)[:, None]
    rest = (pair_index % 256).astype(BF16)[:, None]
    msg = jnp.concatenate([emb_low, high, rest, jnp.zeros((seg_here, 126), BF16)], axis=1)
    copies = sum(size - 1 for size in groups)
    vm = pl.BlockSpec(memory_space=pltpu.VMEM)
    return pl.pallas_call(
        functools.partial(contrast_kernel, groups),
        out_shape=(jax.ShapeDtypeStruct((8, 128), F32), jax.ShapeDtypeStruct((seg_here, width), F32)),
        in_specs=[vm] * 4,
        out_specs=[vm] * 2,
        scratch_shapes=[
            pltpu.VMEM(tuple(groups) + msg.shape, BF16),
            pltpu.SemaphoreType.DMA((copies,)),
            pltpu.SemaphoreType.DMA((copies,)),
        ],
        compiler_params=pltpu.CompilerParams(collective_id=0, has_side_effects=True, vmem_limit_bytes=56 * MIB),
        name="contrast",
    )(msg, z, invn, cnt)

UNIT_ROWS = 48


def event_plan(pieces, units):
    core, axis, hop, own = 2.4, 6.4, 1.8, 0.1
    free = {"x": 0.0, "y": 0.0, "z": 0.0}
    pending = []
    plan = []
    now = 0.0

    def advance(unit, step, at):
        size = unit["size"]
        if step == 0:
            return at + core * size
        if step == 1 and unit["flat"]:
            free["x"] = free["y"] = max(at, free["x"], free["y"]) + axis * size
            return free["x"] + hop
        if step == 1:
            lane, cost = unit["first"], axis
        elif unit["flat"]:
            lane, cost = "z", axis / 2
        elif unit["z_last"]:
            lane, cost = (unit["second"], axis / 2) if step == 2 else ("z", axis / 2)
        else:
            lane, cost = ("z", axis) if step == 2 else (unit["second"], axis / 8)
        start = max(at, free[lane])
        free[lane] = start + cost * size
        return start + cost * size + hop

    def serve(entry, steps):
        nonlocal now
        at, uid, step = entry
        now = max(now, at) + own
        steps.append((uid, step))
        if step < last_step(units[uid]):
            pending.append((advance(units[uid], step, now), uid, step + 1))
            pending.sort()

    for name, cost in pieces:
        now += cost
        steps = []
        for unit in units:
            if unit["after"] == name:
                steps.append((unit["id"], 0))
                pending.append((advance(unit, 0, now), unit["id"], 1))
        pending.sort()
        while pending and pending[0][0] <= now:
            serve(pending.pop(0), steps)
        plan.append(steps)
    steps = []
    while pending:
        serve(pending.pop(0), steps)
    plan.append(steps)
    return plan, now


def last_step(unit):
    return 3 if unit["flat"] else 4


def unit_list(depth, groups, orders):
    names = (
        [("down", j, "down%d" % (depth - 1), 4 / 3) for j in range(3)]
        + [("up", u, "up%d" % u, 1.0) for u in range(4)]
        + [("proj", 4, "proj", 1.0)]
        + [("qkv", 5 + g, "dqkv%d" % g, 1.0) for g in range(groups)]
    )
    units = []
    for uid, ((kind, at, after, size), order) in enumerate(zip(names, orders)):
        units.append(
            {
                "id": uid, "kind": kind, "at": at, "after": after, "size": size, "z_last": order[-1] == "z", "flat": len(order) == 2,
                "first": order[0][0], "second": order[1] if order[-1] == "z" else order[2],
            }
        )
    return units


def piece_list(depth, groups, rows):
    pieces = []
    for j in range(4):
        pieces += [("up%d" % j, 3.0), ("first%d" % j, 1.7)]
        if j == 0:
            pieces += [("down%d" % m, 1.6) for m in range(depth)]
    pieces += [("norm%d" % r, 2.0) for r in range(rows)] + [("proj", 1.5)]
    for g in range(groups):
        pieces += [("attn%d%d" % (g, i), 1.6) for i in range(2 * rows)] + [("dqkv%d" % g, 1.5)]
    return pieces + [("tok%d" % g, 2.0) for g in range(groups)]


ORDERS = ("yzx", "xyz", "yxz", "pz", "xzy", "yxz", "xzy", "yxz", "xyz", "pz", "pz")


def colsum(v):
    return jnp.sum(v, axis=0, keepdims=True)


def norm_back_k(grad_n, normed, inv_std):
    scale = 1.0 / grad_n.shape[-1]
    mean = jnp.sum(grad_n, axis=-1, keepdims=True) * scale
    dots = jnp.sum(grad_n * normed, axis=-1, keepdims=True) * scale
    return inv_std * (grad_n - mean - normed * dots)


def backward_kernel(
    depth,
    ids_ref, pair_ref, z_ref, invn_ref, cnt_ref, ag_ref, fg_ref,
    low_hbm, tok_hbm, n2_hbm, stat_hbm, act_hbm, der_hbm, wd_hbm, wu_hbm, n1_hbm, wp_hbm, rinv_hbm, ctx_hbm,
    qkv_hbm, exp_hbm, wqkv_hbm,
    tg_hbm, loss_ref, oq_ref, op_ref, ou_ref, od_ref, v_qb, v_vb, v_pb, v_ag, v_as, v_ub, v_db, v_fg, v_fs,
    w_s, wd_s, rc_s, rcd_s, r2_s, r2d_s, q_s, qd_s,
    all_s, low_t, tok_t, tok_s, stream_s, g_s, ctx_s, rdo_s, qg_s, exp_s, gq_s, tg_s, wst_s, wp_s, stat_s,
    ar0_s, ar1_s, ar2_s, br0_s, br1_s, br2_s,
    send_sem, recv_sem, gsend_sem, grecv_sem, asend_sem, arecv_sem, in_sem, str_sem, wst_sem, grp_sem, exp_sem, out_sem,
):
    toks, width = tok_s.shape
    half = width // 2
    ff = act_hbm.shape[1]
    kinds = ff // width
    row_len = exp_s.shape[3]
    rows = toks // row_len
    strip = width // (8 * depth)
    groups = width // (2 * PAIR)
    seg_here = z_ref.shape[0]
    me = lax.axis_index("batch")
    c = lax.rem(me, 2)
    x = lax.rem(me // 2, 2)
    y = lax.rem(me // 4, 2)
    z = me // 8
    xy = y * 2 + x

    def index(zz, yy, xx, cc):
        return ((zz * 2 + yy) * 2 + xx) * 2 + cc

    core_peer = index(z, y, x, 1 - c)
    x_peer = index(z, y, 1 - x, c)
    y_peer = index(z, 1 - y, x, c)
    xy_peer = index(z, 1 - y, 1 - x, c)
    z_peers = [index(lax.rem(z + step, depth), y, x, c) for step in range(1, depth)]
    everyone = [core_peer, x_peer, y_peer, xy_peer] + z_peers

    barrier = pltpu.get_barrier_semaphore()
    for other in everyone:
        pl.semaphore_signal(barrier, inc=1, device_id=(other,), device_id_type=MESH)

    local = pltpu.make_async_copy

    def stream(k):
        src = act_hbm if 1 <= k <= depth else der_hbm
        off = (0 if k == 0 else k - 1 if k <= depth else k - depth) * width
        return local(src.at[:, off : off + width], stream_s.at[k % 2], str_sem.at[k % 2])

    def ffn_weights(j):
        at = (j % 2) * 2
        return [
            local(wd_hbm.at[j * width : (j + 1) * width, :], wst_s.at[at], wst_sem.at[at]),
            local(wu_hbm.at[:, j * width : (j + 1) * width], wst_s.at[at + 1], wst_sem.at[at + 1]),
        ]

    def group_loads(g):
        return [
            local(
                qkv_hbm.at[:, third * width + g * 2 * PAIR : third * width + (g + 1) * 2 * PAIR],
                qg_s.at[g % 2, :, third * 2 * PAIR : (third + 1) * 2 * PAIR],
                grp_sem.at[(g % 2) * 3 + third],
            )
            for third in range(3)
        ]

    def weight_loads(g):
        return [
            local(
                wqkv_hbm.at[:, third * width + g * 2 * PAIR : third * width + (g + 1) * 2 * PAIR],
                wst_s.at[g, :, third * 2 * PAIR : (third + 1) * 2 * PAIR],
                wst_sem.at[4 + g * 3 + third],
            )
            for third in range(3)
        ]

    def exp_load(r, p, slot):
        return local(exp_hbm.at[r * (width // PAIR) + p], exp_s.at[slot], exp_sem.at[slot])

    low_load = local(low_hbm, tok_s, in_sem.at[0])
    tok_load = local(tok_hbm, tok_s, in_sem.at[1])
    n2_load = local(n2_hbm, gq_s, in_sem.at[2])
    stat_load = local(stat_hbm, stat_s, in_sem.at[3])
    n1_load = local(n1_hbm, qg_s.at[1], in_sem.at[4])
    rinv_load = local(rinv_hbm, tok_s, in_sem.at[5])
    wp_load = local(wp_hbm, wp_s, in_sem.at[6])
    ctx_load = local(ctx_hbm, ctx_s, in_sem.at[7])
    low_load.start()
    n2_load.start()
    stat_load.start()
    stream(0).start()
    stream(1).start()
    for j in range(2):
        for cp in ffn_weights(j):
            cp.start()
    n1_load.start()
    wp_load.start()
    ctx_load.start()
    for cp in group_loads(0):
        cp.start()
    exp_load(0, 0, 0).start()

    def remote(src, dst, slot, device, ssem=send_sem, rsem=recv_sem):
        return pltpu.make_async_remote_copy(
            src_ref=src, dst_ref=dst, send_sem=ssem.at[slot], recv_sem=rsem.at[slot], device_id=(device,), device_id_type=MESH
        )

    pair_row = jnp.broadcast_to(pair_ref[...].reshape(1, seg_here), (seg_here, seg_here))
    here = lax.broadcasted_iota(jnp.int32, (seg_here, seg_here), 0) == lax.broadcasted_iota(
        jnp.int32, (seg_here, seg_here), 1
    )
    as_column = lambda v: jnp.sum(jnp.where(here, v.astype(F32), 0.0), axis=1, keepdims=True)
    lane = lax.broadcasted_iota(jnp.int32, (seg_here, 128), 1)
    tag = jnp.where(lane == 0, as_column(pair_row // 256), 0.0) + jnp.where(lane == 1, as_column(pair_row % 256), 0.0)
    msg = jnp.concatenate([z_ref[...].astype(BF16), tag.astype(BF16)], axis=1)
    all_s[z, xy, c] = msg

    def gather(stage):
        if stage == 0:
            ref, others = all_s.at[z, xy, c], z_peers
        elif stage == 1:
            ref, others = all_s.at[:, xy, c], [x_peer, y_peer, xy_peer]
        else:
            ref, others = all_s.at[:, :, c], [core_peer]
        base = (0, depth - 1, depth + 2)[stage]
        return [remote(ref, ref, base + k, other, gsend_sem, grecv_sem) for k, other in enumerate(others)]

    pl.semaphore_wait(barrier, len(everyone))
    for cp in gather(0):
        cp.start()
    low_load.wait()
    low_t[...] = jnp.transpose(tok_s[...])
    tok_load.start()
    for cp in gather(0):
        cp.wait_recv()
    for cp in gather(1):
        cp.start()
    tok_load.wait()
    tok_t[...] = jnp.transpose(tok_s[...])
    rinv_load.start()
    for cp in gather(1):
        cp.wait_recv()
    for cp in gather(2):
        cp.start()
    br0_s[z] = jnp.zeros(br0_s.shape[1:], F32)
    ar0_s[z] = jnp.zeros(ar0_s.shape[1:], F32)
    for cp in gather(2):
        cp.wait_recv()
    loss, grad_seg = contrast_math(
        all_s[...].reshape(8 * depth * seg_here, msg.shape[1]), msg, me, z_ref[...], invn_ref[:, 0:1], cnt_ref[:, 0:1]
    )
    loss_ref[...] = jnp.broadcast_to(loss, loss_ref.shape)

    units = unit_list(depth, groups, ORDERS)
    pieces = piece_list(depth, groups, rows)
    plan, _ = event_plan(pieces, units)
    places = [name for name, _ in pieces]

    def bufs(unit):
        if unit["kind"] == "down":
            return [ref.at[unit["at"]] for ref in (wd_s, rcd_s, r2d_s, qd_s)]
        return [ref.at[unit["at"]] for ref in (w_s, rc_s, r2_s, q_s)]

    def unit_copies(unit, step):
        w, rc, r2, q = bufs(unit)
        f, s = (y, x) if unit["first"] == "y" else (x, y)
        f_peer, s_peer = (y_peer, x_peer) if unit["first"] == "y" else (x_peer, y_peer)
        base = unit["id"] * (3 + depth)
        if step == 0:
            return [remote(w.at[1 - c], rc, base, core_peer)]
        if unit["flat"] and step == 1:
            return [
                remote(w.at[c, 1 - x, y], r2.at[0], base + 1, x_peer),
                remote(w.at[c, x, 1 - y], r2.at[1], base + 2, y_peer),
                remote(w.at[c, 1 - x, 1 - y], q.at[0], base + 2 + depth, xy_peer),
            ]
        if unit["flat"]:
            return [
                remote(w.at[c, x, y, lax.rem(z + k, depth)], q.at[1, z], base + 2 + k, z_peers[k - 1])
                for k in range(1, depth)
            ]
        if step == 1:
            return [remote(w.at[c, 1 - f], r2, base + 1, f_peer)]
        if unit["z_last"]:
            if step == 2:
                return [remote(w.at[c, f, 1 - s], q.at[0], base + 2, s_peer)]
            return [
                remote(w.at[c, f, s, lax.rem(z + k, depth)], q.at[1, z], base + 2 + k, z_peers[k - 1])
                for k in range(1, depth)
            ]
        if step == 2:
            return [
                remote(w.at[c, f, :, lax.rem(z + k, depth)], q.at[:, z], base + 2 + k, z_peers[k - 1])
                for k in range(1, depth)
            ]
        return [remote(w.at[c, f, 1 - s, z], q.at[0, z], base + 2, s_peer)]

    def finish(unit, total):
        kind, at = unit["kind"], unit["at"]
        if kind == "down":
            per = width // 128
            for k in range(4):
                start = (k // 2) * UNIT_ROWS * per + at * 2 + k % 2
                od_ref[pl.ds(start, UNIT_ROWS, stride=per), :] = total[:, k * 128 : (k + 1) * 128]
            return
        for k in range(6):
            piece = total[(k // 3) * strip : (k // 3 + 1) * strip, (k % 3) * 128 : (k % 3 + 1) * 128]
            if kind == "up":
                ref, per, col = ou_ref, ff // 128, at * 6 + k
            elif kind == "proj":
                ref, per, col = op_ref, width // 128, k
            else:
                ref, per, col = oq_ref, 3 * width // 128, (k // 2) * (width // 128) + (at - 5) * 2 + k % 2
            ref[pl.ds(col, strip, stride=per), :] = piece

    def take(unit, step):
        w, rc, r2, q = bufs(unit)
        f, s = (y, x) if unit["first"] == "y" else (x, y)
        z_last = unit["z_last"]
        if step > 0:
            for cp in unit_copies(unit, step - 1):
                cp.wait_recv()
        f32 = lambda v: v.astype(F32)
        two = lambda a, b: f32(w[c, f, a, b]) + f32(rc[f, a, b]) + f32(r2[a, b])
        four = lambda b: f32(w[c, x, y, b]) + f32(rc[x, y, b]) + f32(r2[0, b]) + f32(r2[1, b]) + f32(q[0, b])
        if step == 1 and unit["flat"]:

            def body(i, carry):
                b = lax.rem(i, depth)
                k = 1 + i // depth
                a1, a2 = lax.rem(x + k % 2, 2), lax.rem(y + k // 2, 2)
                w[c, a1, a2, b] = (f32(w[c, a1, a2, b]) + f32(rc[a1, a2, b])).astype(BF16)
                return carry

            lax.fori_loop(0, 3 * depth, body, 0)
        elif unit["flat"] and step == 2:

            def body(k, carry):
                b = lax.rem(z + k, depth)
                w[c, x, y, b] = four(b).astype(BF16)
                return carry

            lax.fori_loop(1, depth, body, 0)
        elif unit["flat"] and step == 3:
            total = four(z)
            for k in range(1, depth):
                total = total + f32(q[1, lax.rem(z + k, depth)])
            finish(unit, total)
        elif step == 1:

            def body(i, carry):
                a, b = i // depth, lax.rem(i, depth)
                w[c, 1 - f, a, b] = (f32(w[c, 1 - f, a, b]) + f32(rc[1 - f, a, b])).astype(BF16)
                return carry

            lax.fori_loop(0, 2 * depth, body, 0)
        elif step == 2 and z_last:

            def body(b, carry):
                w[c, f, 1 - s, b] = two(1 - s, b).astype(BF16)
                return carry

            lax.fori_loop(0, depth, body, 0)
        elif step == 3 and z_last:

            def body(k, carry):
                b = lax.rem(z + k, depth)
                w[c, f, s, b] = (two(s, b) + f32(q[0, b])).astype(BF16)
                return carry

            lax.fori_loop(1, depth, body, 0)
        elif step == 2:

            def body(k, carry):
                b = lax.rem(z + 1 + k // 2, depth)
                a = lax.rem(k, 2)
                w[c, f, a, b] = two(a, b).astype(BF16)
                return carry

            lax.fori_loop(0, 2 * (depth - 1), body, 0)
        elif step == 3:
            total = two(1 - s, z)
            for k in range(1, depth):
                total = total + f32(q[1 - s, lax.rem(z + k, depth)])
            w[c, f, 1 - s, z] = total.astype(BF16)
        elif step == 4:
            total = two(s, z) + f32(q[0, z])
            for k in range(1, depth):
                total = total + f32(q[1 if z_last else s, lax.rem(z + k, depth)])
            finish(unit, total)
        if step < last_step(unit):
            for cp in unit_copies(unit, step):
                cp.start()

    def after(name):
        for uid, step in plan[places.index(name)]:
            take(units[uid], step)

    def vec_copies(which, stage):
        bank = ((ar0_s, ar1_s, ar2_s), (br0_s, br1_s, br2_s))[which][stage]
        base = which * (depth + 3) + (0, depth - 1, depth + 2)[stage]
        slot, others = ((z, z_peers), (xy, [x_peer, y_peer, xy_peer]), (c, [core_peer]))[stage]
        return [
            remote(bank.at[slot], bank.at[slot], base + k, other, asend_sem, arecv_sem) for k, other in enumerate(others)
        ]

    def vec_step(which, step):
        banks = ((ar0_s, ar1_s, ar2_s), (br0_s, br1_s, br2_s))[which]
        total = None
        if step > 0:
            for cp in vec_copies(which, step - 1):
                cp.wait_recv()
            bank = banks[step - 1]
            total = bank[0]
            for k in range(1, bank.shape[0]):
                total = total + bank[k]
        if step < 3:
            if step > 0:
                banks[step][xy if step == 1 else c] = total
            for cp in vec_copies(which, step):
                cp.start()
        elif which == 0:
            for k, ref in enumerate((v_fg, v_fs, v_db, v_ag, v_as, v_pb)):
                ref[...] = total[k : k + 1].reshape(width)
            v_ub[...] = jnp.concatenate([total[6 + k : 7 + k] for k in range(kinds)], axis=1).reshape(ff)
        else:
            v_qb[...] = total[0:1].reshape(width)
            v_vb[...] = total[1:2].reshape(width)

    def put_unit(unit, res):
        w = bufs(unit)[0]
        for d in range(8 * depth):
            cc, xx, yy, zz = d % 2, d // 2 % 2, d // 4 % 2, d // 8
            f, s = (yy, xx) if unit["first"] == "y" else (xx, yy)
            piece = res[d * strip : (d + 1) * strip]
            w[cc, f, s, zz] = jnp.concatenate([piece[:, :half], piece[:, half:]], axis=0).astype(BF16)

    n2_load.wait()
    stat_load.wait()
    for r in range(rows):
        rsl = slice(r * row_len, (r + 1) * row_len)
        seg = lax.broadcasted_iota(jnp.int32, (SEGS, row_len), 0)
        member = (seg == ids_ref[r : r + 1, :]).astype(BF16)
        gp = grad_seg[r * SEGS : (r + 1) * SEGS, :]
        high = gp.astype(BF16)
        rest = (gp - high.astype(F32)).astype(BF16)
        grad_y = dot_tn(member, high) + dot_tn(member, rest)
        n2 = gq_s[rsl, :].astype(F32)
        ar0_s[z, 0:1, :] += colsum(grad_y * n2)
        ar0_s[z, 1:2, :] += colsum(grad_y)
        grad_r2 = norm_back_k(grad_y * fg_ref[...].reshape(1, width), n2, stat_s[rsl, 1:2])
        gdl = grad_r2.astype(BF16)
        tg_s[rsl, :] = grad_r2
        g_s[rsl, :] = gdl
        ar0_s[z, 2:3, :] += colsum(gdl.astype(F32))

    for j in range(kinds):
        at_stream = 0 if j == 0 else depth + j
        at = (j % 2) * 2
        loads = ffn_weights(j)
        loads[0].wait()
        stream(at_stream).wait()
        for b in range(3):
            bsl = slice(b * 256, (b + 1) * 256)
            grad_act = dot_nt(g_s[...], wst_s[at, bsl, :])
            gul = (grad_act * stream_s[at_stream % 2, :, bsl].astype(F32)).astype(BF16)
            gq_s[:, bsl] = gul
            ar0_s[z, 6 + j : 7 + j, bsl] = colsum(gul.astype(F32))
        if j == 0:
            stream(2).start()
        elif j + 2 < kinds:
            stream(depth + j + 2).start()
        put_unit(units[3 + j], dot_nn(low_t[...], gq_s[...]))
        after("up%d" % j)
        loads[1].wait()
        for b in range(3):
            bsl = slice(b * 256, (b + 1) * 256)
            tg_s[:, bsl] += dot_nt(gq_s[...], wst_s[at + 1, bsl, :])
        if j + 2 < kinds:
            for cp in ffn_weights(j + 2):
                cp.start()
        after("first%d" % j)
        for m in range(depth if j == 0 else 0):
            stream(1 + m).wait()
            res = dot_tn(stream_s[(1 + m) % 2], g_s[...])
            stream(3 + m).start()
            for i in range(8):
                cc, xx, yy = i % 2, i // 2 % 2, i // 4
                piece = res[i * 2 * UNIT_ROWS : (i + 1) * 2 * UNIT_ROWS]
                for j in range(3):
                    f, s = (yy, xx) if units[j]["first"] == "y" else (xx, yy)
                    blk = piece[:, j * 256 : (j + 1) * 256]
                    wd_s[j, cc, f, s, m] = jnp.concatenate([blk[:UNIT_ROWS], blk[UNIT_ROWS:]], axis=1).astype(BF16)
            after("down%d" % m)

    for g in range(groups):
        for cp in weight_loads(g):
            cp.start()
    n1_load.wait()
    wp_load.wait()
    rinv_load.wait()
    for r in range(rows):
        rsl = slice(r * row_len, (r + 1) * row_len)
        grad_first = tg_s[rsl, :]
        n1 = qg_s[1, rsl, :].astype(F32)
        ar0_s[z, 3:4, :] += colsum(grad_first * n1)
        ar0_s[z, 4:5, :] += colsum(grad_first)
        grad_r1 = norm_back_k(grad_first * ag_ref[...].reshape(1, width), n1, stat_s[rsl, 0:1])
        tg_s[rsl, :] = grad_r1
        gal = grad_r1.astype(BF16)
        g_s[rsl, :] = gal
        ar0_s[z, 5:6, :] += colsum(gal.astype(F32))
        grad_ctx = dot_nt(gal, wp_s[...]).astype(BF16)
        rdo_s[rsl, :] = (grad_ctx.astype(F32) * tok_s[rsl, :].astype(F32)).astype(BF16)
        after("norm%d" % r)
    vec_step(0, 0)
    ctx_load.wait()
    put_unit(units[7], dot_tn(ctx_s[...], g_s[...]))
    after("proj")

    lane = lax.broadcasted_iota(jnp.int32, (row_len, 2 * PAIR), 1)
    first = lax.rem(lane, PAIR) < HEAD_DIM
    ones = jnp.ones((row_len, PAIR), BF16)
    scale = HEAD_DIM**-0.5
    grads = [stream_s.at[0], stream_s.at[1], gq_s]
    qcols = lambda g, pp: pl.ds(pl.multiple_of((2 * g + pp) * PAIR, PAIR), PAIR)
    for g in range(groups):
        for cp in group_loads(g):
            cp.wait()
        if g + 1 < groups:
            for cp in group_loads(g + 1):
                cp.start()

        def attend(i, carry):
            r, pp = i // 2, lax.rem(i, 2)
            slot = lax.rem(i, 2)
            exp_load(r, 2 * g + pp, slot).wait()

            @pl.when(i + 1 < 2 * rows)
            def _():
                exp_load((i + 1) // 2, 2 * g + lax.rem(i + 1, 2), 1 - slot).start()

            if g + 1 < groups:

                @pl.when(i + 1 == 2 * rows)
                def _():
                    exp_load(0, 2 * (g + 1), 0).start()

            rsl = pl.ds(pl.multiple_of(r * row_len, row_len), row_len)
            lanes = lambda base: pl.ds(pl.multiple_of(base + pp * PAIR, PAIR), PAIR)
            q = qg_s[g % 2, rsl, lanes(0)]
            k = qg_s[g % 2, rsl, lanes(2 * PAIR)]
            v = qg_s[g % 2, rsl, lanes(4 * PAIR)]
            do = rdo_s[rsl, lanes(g * 2 * PAIR)]
            ctx = ctx_s[rsl, lanes(g * 2 * PAIR)]
            neg = -(do.astype(F32) * ctx.astype(F32))
            lhs = jnp.concatenate([do, neg.astype(BF16)], axis=1)
            rhs = jnp.concatenate([v, ones], axis=1)
            do_t = jnp.transpose(do)
            q_t = jnp.transpose(q)
            dq, dk, dv = [], [], []
            for h in range(2):
                lh = jnp.where(first if h == 0 else ~first, lhs, jnp.zeros_like(lhs))
                e = exp_s[slot, h]
                ds = (e.astype(F32) * dot_nt(lh, rhs)).astype(BF16)
                hs = slice(h * HEAD_DIM, (h + 1) * HEAD_DIM)
                dv.append(dot_nn(do_t[hs], e))
                dk.append(dot_nn(q_t[hs], ds))
                dq.append(dot_nn(ds, k))
            dq = (jnp.where(first[:, :PAIR], dq[0], dq[1]) * scale).astype(BF16)
            dk = jnp.transpose((jnp.concatenate(dk, axis=0) * scale).astype(BF16))
            dv = jnp.transpose(jnp.concatenate(dv, axis=0).astype(BF16))
            grads[g][rsl, lanes(0)] = dq
            grads[g][rsl, lanes(2 * PAIR)] = dk
            grads[g][rsl, lanes(4 * PAIR)] = dv
            br0_s[z, 0:1, qcols(g, pp)] += colsum(dq.astype(F32))
            br0_s[z, 1:2, qcols(g, pp)] += colsum(dv.astype(F32))
            for step in range(2 * rows):
                if plan[places.index("attn%d%d" % (g, step))]:

                    @pl.when(i == step)
                    def _():
                        after("attn%d%d" % (g, step))

            return carry

        lax.fori_loop(0, 2 * rows, attend, 0)
        put_unit(units[8 + g], dot_nn(tok_t[...], grads[g][...]))
        after("dqkv%d" % g)
        vec_step(0, g + 1)
    vec_step(1, 0)
    for g in range(groups):
        for cp in weight_loads(g):
            cp.wait()
        for b in range(3):
            bsl = slice(b * 256, (b + 1) * 256)
            tg_s[:, bsl] += dot_nt(grads[g][...], wst_s[g, bsl, :])
        after("tok%d" % g)
    tg_out = local(tg_s, tg_hbm, out_sem)
    tg_out.start()
    left = plan[-1]
    marks = {len(left) * (k + 1) // 4: k + 1 for k in range(3)}
    for k, (uid, step) in enumerate(left):
        if k in marks:
            vec_step(1, marks[k])
        take(units[uid], step)
    for stage in range(3):
        for cp in gather(stage):
            cp.wait_send()
    for step in range(4):
        for unit in units:
            if step < last_step(unit):
                for cp in unit_copies(unit, step):
                    cp.wait_send()
    for which in range(2):
        for stage in range(3):
            for cp in vec_copies(which, stage):
                cp.wait_send()
    tg_out.wait()


def backward_call(n, ids, pair, zed, invn, cnt, ag, fg, low, tok, n2, stat, act, der, wd, wu, n1, wp, rinv, ctx, qkv, exps, wqkv):
    depth = n // 8
    toks, width = tok.shape
    ff = act.shape[1]
    row_len = exps.shape[2]
    groups = width // (2 * PAIR)
    half = width // 2
    segs = zed.shape[0]
    sds = jax.ShapeDtypeStruct
    vm = pl.BlockSpec(memory_space=pltpu.VMEM)
    hb = pl.BlockSpec(memory_space=pl.ANY)
    flat = lambda cols, rws: sds((rws // n * cols // 128, 128), F32)
    v = lambda k: sds((k,), F32)
    wide = lambda *lead: [pltpu.VMEM((8,) + lead + (UNIT_ROWS, half), BF16), pltpu.VMEM((3,) + lead + (UNIT_ROWS, 512), BF16)]
    big = pltpu.VMEM((toks, width), BF16)
    turned = pltpu.VMEM((width, toks), BF16)
    sem = lambda k: pltpu.SemaphoreType.DMA((k,))
    scratch = wide(2, 2, 2, depth) + wide(2, 2, depth) + wide(2, depth) + wide(2, depth)
    scratch += [
        pltpu.VMEM((depth, 4, 2, segs, width + 128), BF16),
        turned,
        turned,
        big,
        pltpu.VMEM((2, toks, width), BF16),
        big,
        big,
        big,
        pltpu.VMEM((2, toks, 6 * PAIR), BF16),
        pltpu.VMEM((2, 2, row_len, row_len), BF16),
        big,
        pltpu.VMEM((toks, width), F32),
        pltpu.VMEM((4, width, width), BF16),
        pltpu.VMEM((width, width), BF16),
        pltpu.VMEM((toks, 128), F32),
        pltpu.VMEM((depth, 16, width), F32),
        pltpu.VMEM((4, 16, width), F32),
        pltpu.VMEM((2, 16, width), F32),
        pltpu.VMEM((depth, 8, width), F32),
        pltpu.VMEM((4, 8, width), F32),
        pltpu.VMEM((2, 8, width), F32),
        sem(11 * (3 + depth)),
        sem(11 * (3 + depth)),
        sem(depth + 3),
        sem(depth + 3),
        sem(2 * (depth + 3)),
        sem(2 * (depth + 3)),
        sem(8),
        sem(2),
        sem(4 + 3 * groups),
        sem(6),
        sem(2),
        pltpu.SemaphoreType.DMA,
    ]
    return pl.pallas_call(
        functools.partial(backward_kernel, depth),
        out_shape=(
            sds((toks, width), F32), sds((8, 128), F32),
            flat(3 * width, width), flat(width, width), flat(ff, width), flat(width, ff),
            v(width), v(width), v(width), v(width), v(width), v(ff), v(width), v(width), v(width),
        ),
        in_specs=[vm] * 7 + [hb] * 15,
        out_specs=[hb] + [vm] * 14,
        scratch_shapes=scratch,
        compiler_params=pltpu.CompilerParams(collective_id=1, has_side_effects=True, vmem_limit_bytes=63 * MIB),
        name="backward",
    )(ids, pair, zed, invn, cnt, ag, fg, low, tok, n2, stat, act, der, wd, wu, n1, wp, rinv, ctx, qkv, exps, wqkv)


def deliver_kernel(big_ref, loss_ref, *refs):
    count = (len(refs) - 4) // 2
    big_out, loss_out = refs[count : count + 2]
    held, sems = refs[-2:]
    parts = sems.shape[0] // 2
    step = held.shape[0] // parts
    loads, stores = [], []
    for k in range(parts):
        rsl = slice(k * step, (k + 1) * step)
        loads.append(pltpu.make_async_copy(big_ref.at[rsl], held.at[rsl], sems.at[k]))
        stores.append(pltpu.make_async_copy(held.at[rsl], big_out.at[rsl], sems.at[parts + k]))
    for cp in loads:
        cp.start()
    for i in range(count):
        refs[count + 2 + i][...] = refs[i][...]
    loss_out[0] = loss_ref[0, 0]
    for load, store in zip(loads, stores):
        load.wait()
        store.start()
    for cp in stores:
        cp.wait()


def deliver_call(arrays):
    hb = pl.BlockSpec(memory_space=pl.ANY)
    vm = pl.BlockSpec(memory_space=pltpu.VMEM)
    big, loss, *rest = arrays
    same = [jax.ShapeDtypeStruct(a.shape, a.dtype) for a in rest]
    return pl.pallas_call(
        deliver_kernel,
        out_shape=tuple([jax.ShapeDtypeStruct(big.shape, big.dtype), jax.ShapeDtypeStruct((1,), F32)] + same),
        in_specs=[hb] + [vm] * (len(rest) + 1),
        out_specs=[hb, pl.BlockSpec(memory_space=pltpu.SMEM)] + [vm] * len(rest),
        scratch_shapes=[pltpu.VMEM(big.shape, big.dtype), pltpu.SemaphoreType.DMA((16,))],
        name="deliver",
    )(*arrays)

def norm_back(grad_out, normed, inv_std, gain):
    grad_n = grad_out * gain
    return inv_std * (
        grad_n
        - jnp.mean(grad_n, axis=-1, keepdims=True)
        - normed * jnp.mean(grad_n * normed, axis=-1, keepdims=True)
    )


def attend_back(entry):
    qkv_row, exps, rinv, ctx, grad_row = entry
    row_len = qkv_row.shape[0]
    split = qkv_row.reshape(row_len, 3, HEADS, HEAD_DIM)
    queries, key_vecs, values = split[:, 0], split[:, 1], split[:, 2]
    exps = exps.reshape(HEADS, row_len, row_len)
    scaled = (grad_row.astype(F32) * rinv.astype(F32)).astype(BF16)
    delta = jnp.sum(scaled.astype(F32).reshape(row_len, HEADS, HEAD_DIM) * ctx.astype(F32).reshape(row_len, HEADS, HEAD_DIM), axis=-1)
    scaled = scaled.reshape(row_len, HEADS, HEAD_DIM)
    grad_probs = jnp.einsum("qhd,khd->hqk", scaled, values, preferred_element_type=F32)
    grad_values = jnp.einsum("hqk,qhd->khd", exps, scaled, preferred_element_type=F32)
    grad_scores = (exps.astype(F32) * (grad_probs - delta.T[..., None])).astype(BF16)
    grad_queries = jnp.einsum("hqk,khd->qhd", grad_scores, key_vecs, preferred_element_type=F32) * HEAD_DIM**-0.5
    grad_keys = jnp.einsum("hqk,qhd->khd", grad_scores, queries, preferred_element_type=F32) * HEAD_DIM**-0.5
    stacked = jnp.stack([grad_queries, grad_keys, grad_values], axis=1)
    return stacked.reshape(row_len, 3 * HEADS * HEAD_DIM).astype(BF16)


def per_device(
    tokens, segment_ids, pair_index, qkv_weight, query_bias, value_bias, proj_weight, proj_bias,
    attn_gain, attn_shift, up_weight, up_bias, down_weight, down_bias, ffn_gain, ffn_shift,
):
    n = lax.axis_size("batch")
    rows, row_len = segment_ids.shape
    toks, width = tokens.shape
    (exps, qkv, context, rinv, normed_one, first_low, acted, deriv, normed_two, layer_out, stat, z, invn, cnt) = forward_call(
        tokens, segment_ids, qkv_weight, query_bias, value_bias, proj_weight, proj_bias, attn_gain, attn_shift,
        up_weight, up_bias, down_weight, down_bias, ffn_gain, ffn_shift)
    if width % (8 * n) == 0 and n // 8 * 2 * UNIT_ROWS * 8 == up_weight.shape[1]:
        grads = deliver_call(backward_call(
            n, segment_ids, pair_index, z, invn, cnt, attn_gain, ffn_gain, first_low, tokens, normed_two, stat, acted,
            deriv, down_weight, up_weight, normed_one, proj_weight, rinv, context, qkv, exps, qkv_weight))
        return (grads[1].reshape(()), layer_out, grads[0]) + tuple(v.reshape(-1) for v in grads[2:])
    loss, grad_seg = contrast_call(n, z.astype(BF16), z, invn, cnt, pair_index)
    inv_one = stat[:, :1]
    inv_two = stat[:, 1:2]
    normed_one = normed_one.astype(F32)
    normed_two = normed_two.astype(F32)
    row_base = (jnp.arange(rows, dtype=jnp.int32) * SEGS)[:, None]
    local_ids = jnp.where(segment_ids >= 0, segment_ids + row_base, -1).reshape(toks)
    member = (local_ids[None, :] == jnp.arange(rows * SEGS, dtype=jnp.int32)[:, None]).astype(F32)
    grad_y = lax.dot_general(member, grad_seg, (((0,), (0,)), ((), ())), precision=lax.Precision.HIGHEST)
    ffn_gain_part = jnp.sum(grad_y * normed_two, axis=0)
    ffn_shift_part = jnp.sum(grad_y, axis=0)
    grad_r2 = norm_back(grad_y, normed_two, inv_two, ffn_gain)
    grad_down_low = grad_r2.astype(BF16)
    down_bias_part = jnp.sum(grad_down_low.astype(F32), axis=0)
    down_weight_part = dot_tn(acted, grad_down_low)
    grad_up_low = (dot_nt(grad_down_low, down_weight) * deriv.astype(F32)).astype(BF16)
    up_bias_part = jnp.sum(grad_up_low.astype(F32), axis=0)
    up_weight_part = dot_tn(first_low, grad_up_low)
    grad_first = grad_r2 + dot_nt(grad_up_low, up_weight)
    attn_gain_part = jnp.sum(grad_first * normed_one, axis=0)
    attn_shift_part = jnp.sum(grad_first, axis=0)
    grad_r1 = norm_back(grad_first, normed_one, inv_one, attn_gain)
    grad_att_low = grad_r1.astype(BF16)
    proj_bias_part = jnp.sum(grad_att_low.astype(F32), axis=0)
    proj_weight_part = dot_tn(context, grad_att_low)
    grad_context = dot_nt(grad_att_low, proj_weight).astype(BF16)
    by_row = lambda v: v.reshape(rows, row_len, -1)
    grad_qkv = lax.map(
        attend_back,
        (by_row(qkv), exps.reshape(rows, -1, 2, row_len, row_len), by_row(rinv), by_row(context), by_row(grad_context)),
    ).reshape(toks, 3 * width)
    qkv_bias_part = jnp.sum(grad_qkv.astype(F32), axis=0)
    qkv_weight_part = dot_tn(tokens, grad_qkv)
    tokens_grad = grad_r1 + dot_nt(grad_qkv, qkv_weight)
    scatter = lambda v: lax.psum_scatter(v.reshape(-1), "batch", scatter_dimension=0, tiled=True)
    sums = lax.psum(
        (qkv_bias_part[:width], qkv_bias_part[2 * width :], proj_bias_part, attn_gain_part, attn_shift_part,
         up_bias_part, down_bias_part, ffn_gain_part, ffn_shift_part),
        "batch",
    )
    return (loss[0, 0], layer_out, tokens_grad, scatter(qkv_weight_part), scatter(proj_weight_part),
            scatter(up_weight_part), scatter(down_weight_part)) + tuple(sums)


def solution(mesh):
    split, whole = P("batch"), P()
    return jax.shard_map(
        per_device,
        mesh=mesh,
        in_specs=(P("batch", None), P("batch", None), split) + (whole,) * 13,
        out_specs=(whole, P("batch", None), P("batch", None)) + (split,) * 4 + (whole,) * 9,
        check_vma=False,
    )
```

```python
import functools
import jax
import jax.numpy as jnp
from jax import lax
from jax.experimental import pallas as pl
from jax.experimental.pallas import tpu as pltpu
from jax.sharding import PartitionSpec as P

F32 = jnp.float32
BF16 = jnp.bfloat16
HEADS = 12
HEAD_DIM = 64
SEGS = 8
PAIR = 2 * HEAD_DIM
LN_EPS = 1e-12
NORM_EPS = 1e-06
MIB = 2**20


def dot_nn(a, b):
    return lax.dot_general(a, b, (((1,), (0,)), ((), ())), preferred_element_type=F32)


def dot_nt(a, b):
    return lax.dot_general(a, b, (((1,), (1,)), ((), ())), preferred_element_type=F32)


def dot_tn(a, b):
    return lax.dot_general(a, b, (((0,), (0,)), ((), ())), preferred_element_type=F32)


def gelu_parts(pre):
    half = 0.5 * pre
    cdf = 0.5 + 0.5 * lax.erf(pre * 0.7071067811865476)
    pdf = jnp.exp(-half * pre) * 0.3989422804014327
    return pre * cdf, cdf + pre * pdf


def normalize(resid):
    width = resid.shape[-1]
    average = jnp.sum(resid, axis=-1, keepdims=True) * (1.0 / width)
    centred = resid - average
    variance = jnp.sum(centred * centred, axis=-1, keepdims=True) * (1.0 / width)
    inv_std = lax.rsqrt(variance + LN_EPS)
    return centred * inv_std, inv_std


def forward_kernel(
    ids_ref, qb_ref, vb_ref, pb_ref, ag_ref, as_ref, ub_ref, db_ref, fg_ref, fs_ref,
    tok_hbm, wqkv_hbm, wp_hbm, wu_hbm, wd_hbm,
    exp_hbm, qkv_hbm, ctx_hbm, rinv_hbm, n1_hbm, low_hbm, act_hbm, der_hbm, n2_hbm, out_hbm,
    stat_ref, z_ref, invn_ref, cnt_ref,
    tok_s, wqkv_s, wp_s, wu_s, wd_s, qkv_s, ctx_s, rinv_s, bias_s, exp_s,
    n1_s, low_s, act_s, der_s, n2_s, out_s, in_sem, out_sem, exp_sem,
):
    rows, row_len = ids_ref.shape
    toks, width = tok_s.shape
    pairs = width // PAIR
    ff = wu_s.shape[1]
    qb, vb, pb, ag, ash, db, fg, fs = (
        ref[...].reshape(1, width) for ref in (qb_ref, vb_ref, pb_ref, ag_ref, as_ref, db_ref, fg_ref, fs_ref)
    )
    ub = ub_ref[...].reshape(1, ff)

    thirds = [
        (wqkv_hbm.at[:, k * width : (k + 1) * width], wqkv_s.at[:, k * width : (k + 1) * width]) for k in range(3)
    ]
    loads = [
        pltpu.make_async_copy(src, dst, in_sem.at[i])
        for i, (src, dst) in enumerate([(tok_hbm, tok_s)] + thirds + [(wp_hbm, wp_s), (wu_hbm, wu_s), (wd_hbm, wd_s)])
    ]
    for cp in loads:
        cp.start()
    loads[0].wait()

    tok = tok_s[...]
    blk = 256
    for j in range(3 * width // blk):
        third, off = divmod(j * blk, width)
        if off == 0:
            loads[1 + third].wait()
        piece = dot_nn(tok, wqkv_s[:, j * blk : (j + 1) * blk])
        if third == 0:
            piece = piece + qb[:, off : off + blk]
        elif third == 2:
            piece = piece + vb[:, off : off + blk]
        qkv_s[:, j * blk : (j + 1) * blk] = piece.astype(BF16)
    qkv_out = pltpu.make_async_copy(qkv_s, qkv_hbm, out_sem.at[0])
    qkv_out.start()

    lane = lax.broadcasted_iota(jnp.int32, (row_len, PAIR), 1)
    first = lane < HEAD_DIM
    ones = jnp.ones((row_len, PAIR), BF16)

    for r in range(rows):
        ids_row = ids_ref[r : r + 1, :].astype(F32)
        ids_col = jnp.transpose(jnp.broadcast_to(ids_row, (128, row_len)))
        for c in range(row_len // 128):
            bias_s[r, :, c * 128 : (c + 1) * 128] = jnp.where(
                ids_col == ids_row[:, c * 128 : (c + 1) * 128], 0.0, -1e9
            )

    def exp_store(it, slot):
        return pltpu.make_async_copy(exp_s.at[slot], exp_hbm.at[pl.ds(2 * it, 2)], exp_sem.at[slot])

    def attend(it, carry):
        r = it // (pairs // 2)
        g = lax.rem(it, pairs // 2)
        rsl = pl.ds(pl.multiple_of(r * row_len, row_len), row_len)
        slot = lax.rem(it, 2)

        @pl.when(it >= 2)
        def _():
            exp_store(it - 2, slot).wait()

        for pp in range(2):
            col = lambda base: pl.ds(pl.multiple_of(base + (2 * g + pp) * PAIR, PAIR), PAIR)
            q = qkv_s[rsl, col(0)] * jnp.asarray(HEAD_DIM**-0.5, BF16)
            k = qkv_s[rsl, col(width)]
            v = jnp.concatenate([qkv_s[rsl, col(2 * width)], ones], axis=1)
            parts = []
            for h in range(2):
                qh = jnp.where(first if h == 0 else ~first, q, jnp.zeros_like(q))
                halves = []
                for t in range(2):
                    ts = slice(t * (row_len // 2), (t + 1) * (row_len // 2))
                    s = dot_nt(qh[ts], k) + bias_s[r, ts]
                    e = jnp.exp(s - jnp.max(s, axis=1, keepdims=True)).astype(BF16)
                    exp_s[slot, pp, h, ts] = e
                    halves.append(dot_nn(e, v))
                oe = jnp.concatenate(halves, axis=0)
                rinv = 1.0 / oe[:, PAIR:]
                parts.append((oe[:, :PAIR] * rinv, rinv))
            ctx_s[rsl, col(0)] = jnp.where(first, parts[0][0], parts[1][0]).astype(BF16)
            rinv_s[rsl, col(0)] = jnp.where(first, parts[0][1], parts[1][1]).astype(BF16)
        exp_store(it, slot).start()
        return carry

    lax.fori_loop(0, rows * pairs // 2, attend, 0)
    ctx_out = pltpu.make_async_copy(ctx_s, ctx_hbm, out_sem.at[1])
    ctx_out.start()
    rinv_out = pltpu.make_async_copy(rinv_s, rinv_hbm, out_sem.at[2])
    rinv_out.start()
    for cp in loads[4:]:
        cp.wait()

    outs = [(n1_s, n1_hbm), (low_s, low_hbm), (act_s, act_hbm), (der_s, der_hbm), (n2_s, n2_hbm), (out_s, out_hbm)]

    def store(i, rsl, csl=slice(None)):
        src, dst = outs[i]
        pltpu.make_async_copy(src.at[rsl, csl], dst.at[rsl, csl], out_sem.at[3 + i]).start()

    def ffn(r, carry):
        rsl = pl.ds(pl.multiple_of(r * row_len, row_len), row_len)
        resid = tok_s[rsl, :].astype(F32) + (dot_nn(ctx_s[rsl, :], wp_s[...]) + pb)
        normed, inv_std = normalize(resid)
        n1_s[rsl, :] = normed.astype(BF16)
        first_norm = normed * ag + ash
        low = first_norm.astype(BF16)
        low_s[rsl, :] = low
        store(0, rsl)
        store(1, rsl)
        for j in range(ff // blk):
            pre = dot_nn(low, wu_s[:, j * blk : (j + 1) * blk]) + ub[:, j * blk : (j + 1) * blk]
            act, der = gelu_parts(pre)
            act_s[rsl, j * blk : (j + 1) * blk] = act.astype(BF16)
            der_s[rsl, j * blk : (j + 1) * blk] = der.astype(BF16)
            if (j + 1) * blk % width == 0:
                store(2, rsl, slice((j + 1) * blk - width, (j + 1) * blk))
                store(3, rsl, slice((j + 1) * blk - width, (j + 1) * blk))
        down = dot_nn(act_s[rsl, :], wd_s[...]) + db
        normed2, inv_std2 = normalize(first_norm + down)
        n2_s[rsl, :] = normed2.astype(BF16)
        stat_ref[rsl, :] = jnp.where(lane == 0, inv_std, inv_std2)
        y = normed2 * fg + fs
        high = y.astype(BF16)
        out_s[rsl, :] = high
        rest = (y - high.astype(F32)).astype(BF16)
        seg = lax.broadcasted_iota(jnp.int32, (SEGS, row_len), 0)
        member = (seg == ids_ref[pl.ds(r, 1), :]).astype(F32)
        count = jnp.sum(member, axis=1, keepdims=True)
        member = member.astype(BF16)
        pooled = (dot_nn(member, high) + dot_nn(member, rest)) / count
        inv_norm = lax.rsqrt(jnp.sum(pooled * pooled, axis=1, keepdims=True) + NORM_EPS)
        z = pooled * inv_norm
        ssl = pl.ds(pl.multiple_of(r * SEGS, SEGS), SEGS)
        z_ref[ssl, :] = z
        invn_ref[ssl, :] = jnp.broadcast_to(inv_norm, (SEGS, 128))
        cnt_ref[ssl, :] = jnp.broadcast_to(count, (SEGS, 128))
        store(4, rsl)
        store(5, rsl)
        return carry

    lax.fori_loop(0, rows, ffn, 0)
    for i, (src, dst) in enumerate(outs):
        pltpu.make_async_copy(src, dst, out_sem.at[3 + i]).wait()
    qkv_out.wait()
    ctx_out.wait()
    rinv_out.wait()
    for slot in range(2):
        exp_store(slot, slot).wait()


def forward_call(tokens, ids, wqkv, qb, vb, wp, pb, ag, ash, wu, ub, wd, db, fg, fs):
    toks, width = tokens.shape
    rows, row_len = ids.shape
    ff = wu.shape[1]
    pairs = width // PAIR
    segs = rows * SEGS
    sds = jax.ShapeDtypeStruct
    vm = pl.BlockSpec(memory_space=pltpu.VMEM)
    hb = pl.BlockSpec(memory_space=pl.ANY)
    return pl.pallas_call(
        forward_kernel,
        out_shape=(
            sds((rows * pairs, 2, row_len, row_len), BF16),
            sds((toks, 3 * width), BF16),
            sds((toks, width), BF16),
            sds((toks, width), BF16),
            sds((toks, width), BF16),
            sds((toks, width), BF16),
            sds((toks, ff), BF16),
            sds((toks, ff), BF16),
            sds((toks, width), BF16),
            sds((toks, width), BF16),
            sds((toks, 128), F32),
            sds((segs, width), F32),
            sds((segs, 128), F32),
            sds((segs, 128), F32),
        ),
        in_specs=[vm] * 10 + [hb] * 5,
        out_specs=[hb] * 10 + [vm] * 4,
        scratch_shapes=[
            pltpu.VMEM((toks, width), BF16),
            pltpu.VMEM(wqkv.shape, BF16),
            pltpu.VMEM(wp.shape, BF16),
            pltpu.VMEM(wu.shape, BF16),
            pltpu.VMEM(wd.shape, BF16),
            pltpu.VMEM((toks, 3 * width), BF16),
            pltpu.VMEM((toks, width), BF16),
            pltpu.VMEM((toks, width), BF16),
            pltpu.VMEM((rows, row_len, row_len), F32),
            pltpu.VMEM((2, 2, 2, row_len, row_len), BF16),
            pltpu.VMEM((toks, width), BF16),
            pltpu.VMEM((toks, width), BF16),
            pltpu.VMEM((toks, ff), BF16),
            pltpu.VMEM((toks, ff), BF16),
            pltpu.VMEM((toks, width), BF16),
            pltpu.VMEM((toks, width), BF16),
            pltpu.SemaphoreType.DMA((7,)),
            pltpu.SemaphoreType.DMA((9,)),
            pltpu.SemaphoreType.DMA((2,)),
        ],
        compiler_params=pltpu.CompilerParams(vmem_limit_bytes=60 * MIB),
        name="forward",
    )(ids, qb, vb, pb, ag, ash, ub, db, fg, fs, tokens, wqkv, wp, wu, wd)

MESH = pl.DeviceIdType.MESH
INV_TEMP = 100.0
NEG = -1000000000.0


def axis_groups(n):
    groups = []
    rest = n // 2
    while rest > 1:
        size = 4 if rest % 4 == 0 else (2 if rest % 2 == 0 else rest)
        groups.append(size)
        rest //= size
    return groups + [2]


def digits_of(me, groups):
    digits = []
    for size in reversed(groups):
        digits.append(lax.rem(me, size))
        me = me // size
    return digits[::-1]


def index_of(digits, groups):
    me = 0
    for digit, size in zip(digits, groups):
        me = me * size + digit
    return me


def contrast_math(every, msg, me, z, invn, cnt):
    total, wide = every.shape
    seg_here, width = z.shape
    emb = every[:, :width]
    own = msg[:, :width]
    own_row = (me * seg_here).astype(F32)
    own_pair = msg[:, width : width + 128].astype(F32)
    own_pair = own_pair[:, 0:1] * 256.0 + own_pair[:, 1:2]

    scores = dot_nt(own, emb) * INV_TEMP
    column = lax.broadcasted_iota(jnp.int32, scores.shape, 1).astype(F32)
    row = lax.broadcasted_iota(jnp.int32, scores.shape, 0).astype(F32) + own_row
    masked = jnp.where(column == row, NEG, scores)
    peak = jnp.max(masked, axis=1, keepdims=True)
    log_norm = peak + jnp.log(jnp.sum(jnp.exp(masked - peak), axis=1, keepdims=True))
    weight = jnp.exp(masked - log_norm) - (column == own_pair).astype(F32)
    grad = dot_nn(weight.astype(BF16), emb)

    blk = min(total, 512)
    loss = jnp.zeros((1, 1), F32)
    for b in range(total // blk):
        part = emb[b * blk : (b + 1) * blk]
        pair = every[b * blk : (b + 1) * blk, width:].astype(F32)
        pair = pair[:, 0:1] * 256.0 + pair[:, 1:2]
        scores = dot_nt(part, emb) * INV_TEMP
        column = lax.broadcasted_iota(jnp.int32, scores.shape, 1).astype(F32)
        row = lax.broadcasted_iota(jnp.int32, scores.shape, 0).astype(F32) + float(b * blk)
        masked = jnp.where(column == row, NEG, scores)
        peak = jnp.max(masked, axis=1, keepdims=True)
        log_norm = peak + jnp.log(jnp.sum(jnp.exp(masked - peak), axis=1, keepdims=True))
        positive = jnp.sum(jnp.where(column == pair, scores, 0.0), axis=1, keepdims=True)
        loss = loss + jnp.sum(log_norm - positive, axis=0, keepdims=True)
        scores = dot_nt(part, own) * INV_TEMP
        column = lax.broadcasted_iota(jnp.int32, scores.shape, 1).astype(F32) + own_row
        row = lax.broadcasted_iota(jnp.int32, scores.shape, 0).astype(F32) + float(b * blk)
        weight = jnp.where(column == row, 0.0, jnp.exp(jnp.where(column == row, NEG, scores) - log_norm))
        weight = weight - (column == pair).astype(F32)
        grad = grad + dot_tn(weight.astype(BF16), part)
    grad = grad * INV_TEMP
    pooled_grad = invn * (grad - z * jnp.sum(grad * z, axis=1, keepdims=True))
    return loss * (1.0 / total), pooled_grad / cnt


def contrast_kernel(groups, msg_ref, z_ref, invn_ref, cnt_ref, loss_ref, gp_ref, all_s, send_sem, recv_sem):
    n = 1
    for size in groups:
        n *= size
    me = lax.axis_index("batch")
    mine = digits_of(me, groups)
    seg_here, wide = msg_ref.shape
    width = z_ref.shape[1]
    total = n * seg_here
    stages = len(groups)

    def peer(stage, step):
        other = lax.rem(mine[stage] + step, groups[stage])
        return other, index_of(mine[:stage] + [other] + mine[stage + 1 :], groups)

    barrier = pltpu.get_barrier_semaphore()
    hops = 0
    for stage in range(stages):
        for step in range(1, groups[stage]):
            pl.semaphore_signal(barrier, inc=1, device_id=(peer(stage, step)[1],), device_id_type=MESH)
            hops += 1
    all_s[tuple(mine)] = msg_ref[...]
    pl.semaphore_wait(barrier, hops)

    slot = 0
    for stage in range(stages):
        copies = []
        for step in range(1, groups[stage]):
            block = all_s.at[(slice(None),) * stage + tuple(mine[stage:])]
            copies.append(
                pltpu.make_async_remote_copy(
                    src_ref=block,
                    dst_ref=block,
                    send_sem=send_sem.at[slot],
                    recv_sem=recv_sem.at[slot],
                    device_id=(peer(stage, step)[1],),
                    device_id_type=MESH,
                )
            )
            slot += 1
        for cp in copies:
            cp.start()
        for cp in copies:
            cp.wait()

    loss, grad = contrast_math(
        all_s[...].reshape(total, wide), msg_ref[...], me, z_ref[...], invn_ref[:, 0:1], cnt_ref[:, 0:1]
    )
    loss_ref[...] = jnp.broadcast_to(loss, loss_ref.shape)
    gp_ref[...] = grad


def contrast_call(n, emb_low, z, invn, cnt, pair_index):
    groups = axis_groups(n)
    seg_here, width = emb_low.shape
    high = (pair_index // 256).astype(BF16)[:, None]
    rest = (pair_index % 256).astype(BF16)[:, None]
    msg = jnp.concatenate([emb_low, high, rest, jnp.zeros((seg_here, 126), BF16)], axis=1)
    copies = sum(size - 1 for size in groups)
    vm = pl.BlockSpec(memory_space=pltpu.VMEM)
    return pl.pallas_call(
        functools.partial(contrast_kernel, groups),
        out_shape=(jax.ShapeDtypeStruct((8, 128), F32), jax.ShapeDtypeStruct((seg_here, width), F32)),
        in_specs=[vm] * 4,
        out_specs=[vm] * 2,
        scratch_shapes=[
            pltpu.VMEM(tuple(groups) + msg.shape, BF16),
            pltpu.SemaphoreType.DMA((copies,)),
            pltpu.SemaphoreType.DMA((copies,)),
        ],
        compiler_params=pltpu.CompilerParams(collective_id=0, has_side_effects=True, vmem_limit_bytes=56 * MIB),
        name="contrast",
    )(msg, z, invn, cnt)

UNIT_ROWS = 48


def event_plan(pieces, units):
    core, axis, hop, own = 2.4, 6.8, 2.8, 0.1
    free = {"x": 0.0, "y": 0.0, "z": 0.0}
    pending = []
    plan = []
    now = 0.0

    def advance(unit, step, at):
        size = unit["size"]
        if step == 0:
            return at + core * size
        if step == 1 and unit["flat"]:
            free["x"] = free["y"] = max(at, free["x"], free["y"]) + axis * size
            return free["x"] + hop
        if step == 1:
            lane, cost = unit["first"], axis
        elif unit["flat"]:
            lane, cost = "z", axis / 2
        elif unit["z_last"]:
            lane, cost = (unit["second"], axis / 2) if step == 2 else ("z", axis / 2)
        else:
            lane, cost = ("z", axis) if step == 2 else (unit["second"], axis / 8)
        start = max(at, free[lane])
        free[lane] = start + cost * size
        return start + cost * size + hop

    def serve(entry, steps):
        nonlocal now
        at, uid, step = entry
        now = max(now, at) + own
        steps.append((uid, step))
        if step < last_step(units[uid]):
            pending.append((advance(units[uid], step, now), uid, step + 1))
            pending.sort()

    for name, cost in pieces:
        now += cost
        steps = []
        for unit in units:
            if unit["after"] == name:
                steps.append((unit["id"], 0))
                pending.append((advance(unit, 0, now), unit["id"], 1))
        pending.sort()
        while pending and pending[0][0] <= now:
            serve(pending.pop(0), steps)
        plan.append(steps)
    steps = []
    while pending:
        serve(pending.pop(0), steps)
    plan.append(steps)
    return plan, now


def last_step(unit):
    return 3 if unit["flat"] else 4


def unit_list(depth, groups, orders):
    names = (
        [("down", j, "down%d" % (depth - 1), 4 / 3) for j in range(3)]
        + [("up", u, "up%d" % u, 1.0) for u in range(4)]
        + [("proj", 4, "proj", 1.0)]
        + [("qkv", 5 + g, "dqkv%d" % g, 1.0) for g in range(groups)]
    )
    units = []
    for uid, ((kind, at, after, size), order) in enumerate(zip(names, orders)):
        units.append(
            {
                "id": uid, "kind": kind, "at": at, "after": after, "size": size, "z_last": order[-1] == "z", "flat": len(order) == 2,
                "first": order[0][0], "second": order[1] if order[-1] == "z" else order[2],
            }
        )
    return units


def piece_list(depth, groups, rows):
    pieces = []
    for j in range(4):
        pieces += [("up%d" % j, 3.0), ("first%d" % j, 1.7)]
        if j == DOWN_AFTER:
            pieces += [("down%d" % m, 1.6) for m in range(depth)]
    pieces += [("norm%d" % r, 2.0) for r in range(rows)] + [("proj", 1.5)]
    for g in range(groups):
        pieces += [("attn%d%d" % (g, i), 1.6) for i in range(2 * rows)] + [("dqkv%d" % g, 1.5)]
    return pieces + [("tok%d" % g, 2.0) for g in range(groups)]


DOWN_AFTER = 0
ORDERS = ("yzx", "xyz", "yxz", "pz", "xzy", "yxz", "xzy", "yxz", "xyz", "pz", "pz")


def colsum(v):
    return jnp.sum(v, axis=0, keepdims=True)


def norm_back_k(grad_n, normed, inv_std):
    scale = 1.0 / grad_n.shape[-1]
    mean = jnp.sum(grad_n, axis=-1, keepdims=True) * scale
    dots = jnp.sum(grad_n * normed, axis=-1, keepdims=True) * scale
    return inv_std * (grad_n - mean - normed * dots)


def backward_kernel(
    depth,
    ids_ref, pair_ref, z_ref, invn_ref, cnt_ref, ag_ref, fg_ref,
    low_hbm, tok_hbm, n2_hbm, stat_hbm, act_hbm, der_hbm, wd_hbm, wu_hbm, n1_hbm, wp_hbm, rinv_hbm, ctx_hbm,
    qkv_hbm, exp_hbm, wqkv_hbm,
    tg_hbm, loss_ref, oq_ref, op_ref, ou_ref, od_ref, v_qb, v_vb, v_pb, v_ag, v_as, v_ub, v_db, v_fg, v_fs,
    w_s, wd_s, rc_s, rcd_s, r2_s, r2d_s, q_s, qd_s,
    all_s, low_t, tok_t, tok_s, stream_s, g_s, ctx_s, rdo_s, qg_s, exp_s, gq_s, tg_s, wst_s, wp_s, stat_s,
    ar0_s, ar1_s, ar2_s, br0_s, br1_s, br2_s,
    send_sem, recv_sem, gsend_sem, grecv_sem, asend_sem, arecv_sem, in_sem, str_sem, wst_sem, grp_sem, exp_sem, out_sem,
):
    toks, width = tok_s.shape
    half = width // 2
    ff = act_hbm.shape[1]
    kinds = ff // width
    row_len = exp_s.shape[3]
    rows = toks // row_len
    strip = width // (8 * depth)
    groups = width // (2 * PAIR)
    seg_here = z_ref.shape[0]
    me = lax.axis_index("batch")
    c = lax.rem(me, 2)
    x = lax.rem(me // 2, 2)
    y = lax.rem(me // 4, 2)
    z = me // 8
    xy = y * 2 + x

    def index(zz, yy, xx, cc):
        return ((zz * 2 + yy) * 2 + xx) * 2 + cc

    core_peer = index(z, y, x, 1 - c)
    x_peer = index(z, y, 1 - x, c)
    y_peer = index(z, 1 - y, x, c)
    xy_peer = index(z, 1 - y, 1 - x, c)
    z_peers = [index(lax.rem(z + step, depth), y, x, c) for step in range(1, depth)]
    everyone = [core_peer, x_peer, y_peer, xy_peer] + z_peers

    barrier = pltpu.get_barrier_semaphore()
    for other in everyone:
        pl.semaphore_signal(barrier, inc=1, device_id=(other,), device_id_type=MESH)

    local = pltpu.make_async_copy

    items = []
    for j in range(kinds):
        items.append(("der", j))
        if j == DOWN_AFTER:
            items += [("act", m) for m in range(depth)]

    def stream(k):
        name, off = items[k]
        src = der_hbm if name == "der" else act_hbm
        return local(src.at[:, off * width : (off + 1) * width], stream_s.at[k % 2], str_sem.at[k % 2])

    def stream_next(k):
        if k + 2 < len(items):
            stream(k + 2).start()

    def ffn_weights(j):
        at = (j % 2) * 2
        return [
            local(wd_hbm.at[j * width : (j + 1) * width, :], wst_s.at[at], wst_sem.at[at]),
            local(wu_hbm.at[:, j * width : (j + 1) * width], wst_s.at[at + 1], wst_sem.at[at + 1]),
        ]

    def group_loads(g):
        return [
            local(
                qkv_hbm.at[:, third * width + g * 2 * PAIR : third * width + (g + 1) * 2 * PAIR],
                qg_s.at[g % 2, :, third * 2 * PAIR : (third + 1) * 2 * PAIR],
                grp_sem.at[(g % 2) * 3 + third],
            )
            for third in range(3)
        ]

    def weight_loads(g):
        return [
            local(
                wqkv_hbm.at[:, third * width + g * 2 * PAIR : third * width + (g + 1) * 2 * PAIR],
                wst_s.at[g, :, third * 2 * PAIR : (third + 1) * 2 * PAIR],
                wst_sem.at[4 + g * 3 + third],
            )
            for third in range(3)
        ]

    def exp_load(r, p, slot):
        return local(exp_hbm.at[r * (width // PAIR) + p], exp_s.at[slot], exp_sem.at[slot])

    low_load = local(low_hbm, tok_s, in_sem.at[0])
    tok_load = local(tok_hbm, tok_s, in_sem.at[1])
    n2_load = local(n2_hbm, gq_s, in_sem.at[2])
    stat_load = local(stat_hbm, stat_s, in_sem.at[3])
    n1_load = local(n1_hbm, qg_s.at[1], in_sem.at[4])
    rinv_load = local(rinv_hbm, tok_s, in_sem.at[5])
    wp_load = local(wp_hbm, wp_s, in_sem.at[6])
    ctx_load = local(ctx_hbm, ctx_s, in_sem.at[7])
    low_load.start()
    n2_load.start()
    stat_load.start()
    stream(0).start()
    stream(1).start()
    for j in range(2):
        for cp in ffn_weights(j):
            cp.start()
    n1_load.start()
    wp_load.start()
    ctx_load.start()
    for cp in group_loads(0):
        cp.start()
    exp_load(0, 0, 0).start()

    def remote(src, dst, slot, device, ssem=send_sem, rsem=recv_sem):
        return pltpu.make_async_remote_copy(
            src_ref=src, dst_ref=dst, send_sem=ssem.at[slot], recv_sem=rsem.at[slot], device_id=(device,), device_id_type=MESH
        )

    pair_row = jnp.broadcast_to(pair_ref[...].reshape(1, seg_here), (seg_here, seg_here))
    here = lax.broadcasted_iota(jnp.int32, (seg_here, seg_here), 0) == lax.broadcasted_iota(
        jnp.int32, (seg_here, seg_here), 1
    )
    as_column = lambda v: jnp.sum(jnp.where(here, v.astype(F32), 0.0), axis=1, keepdims=True)
    lane = lax.broadcasted_iota(jnp.int32, (seg_here, 128), 1)
    tag = jnp.where(lane == 0, as_column(pair_row // 256), 0.0) + jnp.where(lane == 1, as_column(pair_row % 256), 0.0)
    msg = jnp.concatenate([z_ref[...].astype(BF16), tag.astype(BF16)], axis=1)
    all_s[z, xy, c] = msg

    def gather(stage):
        if stage == 0:
            ref, others = all_s.at[z, xy, c], z_peers
        elif stage == 1:
            ref, others = all_s.at[:, xy, c], [x_peer, y_peer, xy_peer]
        else:
            ref, others = all_s.at[:, :, c], [core_peer]
        base = (0, depth - 1, depth + 2)[stage]
        return [remote(ref, ref, base + k, other, gsend_sem, grecv_sem) for k, other in enumerate(others)]

    pl.semaphore_wait(barrier, len(everyone))
    for cp in gather(0):
        cp.start()
    low_load.wait()
    low_t[...] = jnp.transpose(tok_s[...])
    tok_load.start()
    for cp in gather(0):
        cp.wait_recv()
    for cp in gather(1):
        cp.start()
    for cp in gather(1):
        cp.wait_recv()
    for cp in gather(2):
        cp.start()
    tok_load.wait()
    tok_t[...] = jnp.transpose(tok_s[...])
    rinv_load.start()
    br0_s[z] = jnp.zeros(br0_s.shape[1:], F32)
    ar0_s[z] = jnp.zeros(ar0_s.shape[1:], F32)
    for cp in gather(2):
        cp.wait_recv()
    loss, grad_seg = contrast_math(
        all_s[...].reshape(8 * depth * seg_here, msg.shape[1]), msg, me, z_ref[...], invn_ref[:, 0:1], cnt_ref[:, 0:1]
    )
    loss_ref[...] = jnp.broadcast_to(loss, loss_ref.shape)

    units = unit_list(depth, groups, ORDERS)
    pieces = piece_list(depth, groups, rows)
    plan, _ = event_plan(pieces, units)
    places = [name for name, _ in pieces]

    def bufs(unit):
        if unit["kind"] == "down":
            return [ref.at[unit["at"]] for ref in (wd_s, rcd_s, r2d_s, qd_s)]
        return [ref.at[unit["at"]] for ref in (w_s, rc_s, r2_s, q_s)]

    def unit_copies(unit, step):
        w, rc, r2, q = bufs(unit)
        f, s = (y, x) if unit["first"] == "y" else (x, y)
        f_peer, s_peer = (y_peer, x_peer) if unit["first"] == "y" else (x_peer, y_peer)
        base = unit["id"] * (3 + depth)
        if step == 0:
            return [remote(w.at[1 - c], rc, base, core_peer)]
        if unit["flat"] and step == 1:
            return [
                remote(w.at[c, 1 - x, y], r2.at[0], base + 1, x_peer),
                remote(w.at[c, x, 1 - y], r2.at[1], base + 2, y_peer),
                remote(w.at[c, 1 - x, 1 - y], q.at[0], base + 2 + depth, xy_peer),
            ]
        if unit["flat"]:
            return [
                remote(w.at[c, x, y, lax.rem(z + k, depth)], q.at[1, z], base + 2 + k, z_peers[k - 1])
                for k in range(1, depth)
            ]
        if step == 1:
            return [remote(w.at[c, 1 - f], r2, base + 1, f_peer)]
        if unit["z_last"]:
            if step == 2:
                return [remote(w.at[c, f, 1 - s], q.at[0], base + 2, s_peer)]
            return [
                remote(w.at[c, f, s, lax.rem(z + k, depth)], q.at[1, z], base + 2 + k, z_peers[k - 1])
                for k in range(1, depth)
            ]
        if step == 2:
            return [
                remote(w.at[c, f, :, lax.rem(z + k, depth)], q.at[:, z], base + 2 + k, z_peers[k - 1])
                for k in range(1, depth)
            ]
        return [remote(w.at[c, f, 1 - s, z], q.at[0, z], base + 2, s_peer)]

    def finish(unit, total):
        kind, at = unit["kind"], unit["at"]
        if kind == "down":
            per = width // 128
            for k in range(4):
                start = (k // 2) * UNIT_ROWS * per + at * 2 + k % 2
                od_ref[pl.ds(start, UNIT_ROWS, stride=per), :] = total[:, k * 128 : (k + 1) * 128]
            return
        for k in range(6):
            piece = total[(k // 3) * strip : (k // 3 + 1) * strip, (k % 3) * 128 : (k % 3 + 1) * 128]
            if kind == "up":
                ref, per, col = ou_ref, ff // 128, at * 6 + k
            elif kind == "proj":
                ref, per, col = op_ref, width // 128, k
            else:
                ref, per, col = oq_ref, 3 * width // 128, (k // 2) * (width // 128) + (at - 5) * 2 + k % 2
            ref[pl.ds(col, strip, stride=per), :] = piece

    def take(unit, step):
        w, rc, r2, q = bufs(unit)
        f, s = (y, x) if unit["first"] == "y" else (x, y)
        z_last = unit["z_last"]
        if step > 0:
            for cp in unit_copies(unit, step - 1):
                cp.wait_recv()
        f32 = lambda v: v.astype(F32)
        two = lambda a, b: f32(w[c, f, a, b]) + f32(rc[f, a, b]) + f32(r2[a, b])
        four = lambda b: f32(w[c, x, y, b]) + f32(rc[x, y, b]) + f32(r2[0, b]) + f32(r2[1, b]) + f32(q[0, b])
        if step == 1 and unit["flat"]:

            def body(i, carry):
                b = lax.rem(i, depth)
                k = 1 + i // depth
                a1, a2 = lax.rem(x + k % 2, 2), lax.rem(y + k // 2, 2)
                w[c, a1, a2, b] = (f32(w[c, a1, a2, b]) + f32(rc[a1, a2, b])).astype(BF16)
                return carry

            lax.fori_loop(0, 3 * depth, body, 0)
        elif unit["flat"] and step == 2:

            def body(k, carry):
                b = lax.rem(z + k, depth)
                w[c, x, y, b] = four(b).astype(BF16)
                return carry

            lax.fori_loop(1, depth, body, 0)
        elif unit["flat"] and step == 3:
            total = four(z)
            for k in range(1, depth):
                total = total + f32(q[1, lax.rem(z + k, depth)])
            finish(unit, total)
        elif step == 1:

            def body(i, carry):
                a, b = i // depth, lax.rem(i, depth)
                w[c, 1 - f, a, b] = (f32(w[c, 1 - f, a, b]) + f32(rc[1 - f, a, b])).astype(BF16)
                return carry

            lax.fori_loop(0, 2 * depth, body, 0)
        elif step == 2 and z_last:

            def body(b, carry):
                w[c, f, 1 - s, b] = two(1 - s, b).astype(BF16)
                return carry

            lax.fori_loop(0, depth, body, 0)
        elif step == 3 and z_last:

            def body(k, carry):
                b = lax.rem(z + k, depth)
                w[c, f, s, b] = (two(s, b) + f32(q[0, b])).astype(BF16)
                return carry

            lax.fori_loop(1, depth, body, 0)
        elif step == 2:

            def body(k, carry):
                b = lax.rem(z + 1 + k // 2, depth)
                a = lax.rem(k, 2)
                w[c, f, a, b] = two(a, b).astype(BF16)
                return carry

            lax.fori_loop(0, 2 * (depth - 1), body, 0)
        elif step == 3:
            total = two(1 - s, z)
            for k in range(1, depth):
                total = total + f32(q[1 - s, lax.rem(z + k, depth)])
            w[c, f, 1 - s, z] = total.astype(BF16)
        elif step == 4:
            total = two(s, z) + f32(q[0, z])
            for k in range(1, depth):
                total = total + f32(q[1 if z_last else s, lax.rem(z + k, depth)])
            finish(unit, total)
        if step < last_step(unit):
            for cp in unit_copies(unit, step):
                cp.start()

    def after(name):
        for uid, step in plan[places.index(name)]:
            take(units[uid], step)

    def vec_copies(which, stage):
        bank = ((ar0_s, ar1_s, ar2_s), (br0_s, br1_s, br2_s))[which][stage]
        base = which * (depth + 3) + (0, depth - 1, depth + 2)[stage]
        slot, others = ((z, z_peers), (xy, [x_peer, y_peer, xy_peer]), (c, [core_peer]))[stage]
        return [
            remote(bank.at[slot], bank.at[slot], base + k, other, asend_sem, arecv_sem) for k, other in enumerate(others)
        ]

    def vec_step(which, step):
        banks = ((ar0_s, ar1_s, ar2_s), (br0_s, br1_s, br2_s))[which]
        total = None
        if step > 0:
            for cp in vec_copies(which, step - 1):
                cp.wait_recv()
            bank = banks[step - 1]
            total = bank[0]
            for k in range(1, bank.shape[0]):
                total = total + bank[k]
        if step < 3:
            if step > 0:
                banks[step][xy if step == 1 else c] = total
            for cp in vec_copies(which, step):
                cp.start()
        elif which == 0:
            for k, ref in enumerate((v_fg, v_fs, v_db, v_ag, v_as, v_pb)):
                ref[...] = total[k : k + 1].reshape(width)
            v_ub[...] = jnp.concatenate([total[6 + k : 7 + k] for k in range(kinds)], axis=1).reshape(ff)
        else:
            v_qb[...] = jnp.concatenate([total[k : k + 1] for k in range(groups)], axis=1).reshape(width)
            v_vb[...] = jnp.concatenate([total[groups + k : groups + k + 1] for k in range(groups)], axis=1).reshape(width)

    def put_unit(unit, res):
        w = bufs(unit)[0]
        for d in range(8 * depth):
            cc, xx, yy, zz = d % 2, d // 2 % 2, d // 4 % 2, d // 8
            f, s = (yy, xx) if unit["first"] == "y" else (xx, yy)
            piece = res[d * strip : (d + 1) * strip]
            w[cc, f, s, zz] = jnp.concatenate([piece[:, :half], piece[:, half:]], axis=0).astype(BF16)

    n2_load.wait()
    stat_load.wait()
    for r in range(rows):
        rsl = slice(r * row_len, (r + 1) * row_len)
        seg = lax.broadcasted_iota(jnp.int32, (SEGS, row_len), 0)
        member = (seg == ids_ref[r : r + 1, :]).astype(BF16)
        gp = grad_seg[r * SEGS : (r + 1) * SEGS, :]
        high = gp.astype(BF16)
        rest = (gp - high.astype(F32)).astype(BF16)
        grad_y = dot_tn(member, high) + dot_tn(member, rest)
        n2 = gq_s[rsl, :].astype(F32)
        ar0_s[z, 0:1, :] += colsum(grad_y * n2)
        ar0_s[z, 1:2, :] += colsum(grad_y)
        grad_r2 = norm_back_k(grad_y * fg_ref[...].reshape(1, width), n2, stat_s[rsl, 1:2])
        gdl = grad_r2.astype(BF16)
        tg_s[rsl, :] = grad_r2
        g_s[rsl, :] = gdl
        ar0_s[z, 2:3, :] += colsum(gdl.astype(F32))

    for j in range(kinds):
        at_stream = items.index(("der", j))
        at = (j % 2) * 2
        loads = ffn_weights(j)
        loads[0].wait()
        stream(at_stream).wait()
        for b in range(3):
            bsl = slice(b * 256, (b + 1) * 256)
            grad_act = dot_nt(g_s[...], wst_s[at, bsl, :])
            gul = (grad_act * stream_s[at_stream % 2, :, bsl].astype(F32)).astype(BF16)
            gq_s[:, bsl] = gul
            ar0_s[z, 6 + j : 7 + j, bsl] = colsum(gul.astype(F32))
        stream_next(at_stream)
        put_unit(units[3 + j], dot_nn(low_t[...], gq_s[...]))
        after("up%d" % j)
        loads[1].wait()
        for b in range(3):
            bsl = slice(b * 256, (b + 1) * 256)
            tg_s[:, bsl] += dot_nt(gq_s[...], wst_s[at + 1, bsl, :])
        if j + 2 < kinds:
            for cp in ffn_weights(j + 2):
                cp.start()
        after("first%d" % j)
        for m in range(depth if j == DOWN_AFTER else 0):
            stream(at_stream + 1 + m).wait()
            res = dot_tn(stream_s[(at_stream + 1 + m) % 2], g_s[...])
            stream_next(at_stream + 1 + m)
            for i in range(8):
                cc, xx, yy = i % 2, i // 2 % 2, i // 4
                piece = res[i * 2 * UNIT_ROWS : (i + 1) * 2 * UNIT_ROWS]
                for j in range(3):
                    f, s = (yy, xx) if units[j]["first"] == "y" else (xx, yy)
                    blk = piece[:, j * 256 : (j + 1) * 256]
                    wd_s[j, cc, f, s, m] = jnp.concatenate([blk[:UNIT_ROWS], blk[UNIT_ROWS:]], axis=1).astype(BF16)
            after("down%d" % m)

    for g in range(groups):
        for cp in weight_loads(g):
            cp.start()
    n1_load.wait()
    wp_load.wait()
    rinv_load.wait()
    for r in range(rows):
        rsl = slice(r * row_len, (r + 1) * row_len)
        grad_first = tg_s[rsl, :]
        n1 = qg_s[1, rsl, :].astype(F32)
        ar0_s[z, 3:4, :] += colsum(grad_first * n1)
        ar0_s[z, 4:5, :] += colsum(grad_first)
        grad_r1 = norm_back_k(grad_first * ag_ref[...].reshape(1, width), n1, stat_s[rsl, 0:1])
        tg_s[rsl, :] = grad_r1
        gal = grad_r1.astype(BF16)
        g_s[rsl, :] = gal
        ar0_s[z, 5:6, :] += colsum(gal.astype(F32))
        grad_ctx = dot_nt(gal, wp_s[...]).astype(BF16)
        rdo_s[rsl, :] = (grad_ctx.astype(F32) * tok_s[rsl, :].astype(F32)).astype(BF16)
        after("norm%d" % r)
    vec_step(0, 0)
    ctx_load.wait()
    put_unit(units[7], dot_tn(ctx_s[...], g_s[...]))
    after("proj")

    lane = lax.broadcasted_iota(jnp.int32, (row_len, 2 * PAIR), 1)
    first = lax.rem(lane, PAIR) < HEAD_DIM
    ones = jnp.ones((row_len, PAIR), BF16)
    scale = HEAD_DIM**-0.5
    grads = [stream_s.at[0], stream_s.at[1], gq_s]
    for g in range(groups):
        for cp in group_loads(g):
            cp.wait()
        if g + 1 < groups:
            for cp in group_loads(g + 1):
                cp.start()

        def attend(i, carry):
            r, pp = i // 2, lax.rem(i, 2)
            slot = lax.rem(i, 2)
            exp_load(r, 2 * g + pp, slot).wait()

            @pl.when(i + 1 < 2 * rows)
            def _():
                exp_load((i + 1) // 2, 2 * g + lax.rem(i + 1, 2), 1 - slot).start()

            if g + 1 < groups:

                @pl.when(i + 1 == 2 * rows)
                def _():
                    exp_load(0, 2 * (g + 1), 0).start()

            rsl = pl.ds(pl.multiple_of(r * row_len, row_len), row_len)
            lanes = lambda base: pl.ds(pl.multiple_of(base + pp * PAIR, PAIR), PAIR)
            q = qg_s[g % 2, rsl, lanes(0)]
            k = qg_s[g % 2, rsl, lanes(2 * PAIR)]
            v = qg_s[g % 2, rsl, lanes(4 * PAIR)]
            do = rdo_s[rsl, lanes(g * 2 * PAIR)]
            ctx = ctx_s[rsl, lanes(g * 2 * PAIR)]
            neg = -(do.astype(F32) * ctx.astype(F32))
            lhs = jnp.concatenate([do, neg.astype(BF16)], axis=1)
            rhs = jnp.concatenate([v, ones], axis=1)
            do_t = jnp.transpose(do)
            q_t = jnp.transpose(q)
            dq, dk, dv = [], [], []
            for h in range(2):
                lh = jnp.where(first if h == 0 else ~first, lhs, jnp.zeros_like(lhs))
                e = exp_s[slot, h]
                ds = (e.astype(F32) * dot_nt(lh, rhs)).astype(BF16)
                hs = slice(h * HEAD_DIM, (h + 1) * HEAD_DIM)
                dv.append(dot_nn(do_t[hs], e))
                dk.append(dot_nn(q_t[hs], ds))
                dq.append(dot_nn(ds, k))
            dq = (jnp.where(first[:, :PAIR], dq[0], dq[1]) * scale).astype(BF16)
            dk = jnp.transpose((jnp.concatenate(dk, axis=0) * scale).astype(BF16))
            dv = jnp.transpose(jnp.concatenate(dv, axis=0).astype(BF16))
            grads[g][rsl, lanes(0)] = dq
            grads[g][rsl, lanes(2 * PAIR)] = dk
            grads[g][rsl, lanes(4 * PAIR)] = dv
            br0_s[z, g : g + 1, lanes(0)] += colsum(dq.astype(F32))
            br0_s[z, groups + g : groups + g + 1, lanes(0)] += colsum(dv.astype(F32))
            for step in range(2 * rows):
                if plan[places.index("attn%d%d" % (g, step))]:

                    @pl.when(i == step)
                    def _():
                        after("attn%d%d" % (g, step))

            return carry

        lax.fori_loop(0, 2 * rows, attend, 0)
        put_unit(units[8 + g], dot_nn(tok_t[...], grads[g][...]))
        after("dqkv%d" % g)
        vec_step(0, g + 1)
    vec_step(1, 0)
    for g in range(groups):
        for cp in weight_loads(g):
            cp.wait()
        for b in range(3):
            bsl = slice(b * 256, (b + 1) * 256)
            tg_s[:, bsl] += dot_nt(grads[g][...], wst_s[g, bsl, :])
        after("tok%d" % g)
    tg_out = local(tg_s, tg_hbm, out_sem)
    tg_out.start()
    left = plan[-1]
    marks = {len(left) * (k + 1) // 4: k + 1 for k in range(3)}
    for k, (uid, step) in enumerate(left):
        if k in marks:
            vec_step(1, marks[k])
        take(units[uid], step)
    for stage in range(3):
        for cp in gather(stage):
            cp.wait_send()
    for step in range(4):
        for unit in units:
            if step < last_step(unit):
                for cp in unit_copies(unit, step):
                    cp.wait_send()
    for which in range(2):
        for stage in range(3):
            for cp in vec_copies(which, stage):
                cp.wait_send()
    tg_out.wait()


def backward_call(n, ids, pair, zed, invn, cnt, ag, fg, low, tok, n2, stat, act, der, wd, wu, n1, wp, rinv, ctx, qkv, exps, wqkv):
    depth = n // 8
    toks, width = tok.shape
    ff = act.shape[1]
    row_len = exps.shape[2]
    groups = width // (2 * PAIR)
    half = width // 2
    segs = zed.shape[0]
    sds = jax.ShapeDtypeStruct
    vm = pl.BlockSpec(memory_space=pltpu.VMEM)
    hb = pl.BlockSpec(memory_space=pl.ANY)
    flat = lambda cols, rws: sds((rws // n * cols // 128, 128), F32)
    v = lambda k: sds((k,), F32)
    wide = lambda *lead: [pltpu.VMEM((8,) + lead + (UNIT_ROWS, half), BF16), pltpu.VMEM((3,) + lead + (UNIT_ROWS, 512), BF16)]
    big = pltpu.VMEM((toks, width), BF16)
    turned = pltpu.VMEM((width, toks), BF16)
    sem = lambda k: pltpu.SemaphoreType.DMA((k,))
    scratch = wide(2, 2, 2, depth) + wide(2, 2, depth) + wide(2, depth) + wide(2, depth)
    scratch += [
        pltpu.VMEM((depth, 4, 2, segs, width + 128), BF16),
        turned,
        turned,
        big,
        pltpu.VMEM((2, toks, width), BF16),
        big,
        big,
        big,
        pltpu.VMEM((2, toks, 6 * PAIR), BF16),
        pltpu.VMEM((2, 2, row_len, row_len), BF16),
        big,
        pltpu.VMEM((toks, width), F32),
        pltpu.VMEM((4, width, width), BF16),
        pltpu.VMEM((width, width), BF16),
        pltpu.VMEM((toks, 128), F32),
        pltpu.VMEM((depth, 16, width), F32),
        pltpu.VMEM((4, 16, width), F32),
        pltpu.VMEM((2, 16, width), F32),
        pltpu.VMEM((depth, 8, 2 * PAIR), F32),
        pltpu.VMEM((4, 8, 2 * PAIR), F32),
        pltpu.VMEM((2, 8, 2 * PAIR), F32),
        sem(11 * (3 + depth)),
        sem(11 * (3 + depth)),
        sem(depth + 3),
        sem(depth + 3),
        sem(2 * (depth + 3)),
        sem(2 * (depth + 3)),
        sem(8),
        sem(2),
        sem(4 + 3 * groups),
        sem(6),
        sem(2),
        pltpu.SemaphoreType.DMA,
    ]
    return pl.pallas_call(
        functools.partial(backward_kernel, depth),
        out_shape=(
            sds((toks, width), F32), sds((8, 128), F32),
            flat(3 * width, width), flat(width, width), flat(ff, width), flat(width, ff),
            v(width), v(width), v(width), v(width), v(width), v(ff), v(width), v(width), v(width),
        ),
        in_specs=[vm] * 7 + [hb] * 15,
        out_specs=[hb] + [vm] * 14,
        scratch_shapes=scratch,
        compiler_params=pltpu.CompilerParams(collective_id=1, has_side_effects=True, vmem_limit_bytes=63 * MIB),
        name="backward",
    )(ids, pair, zed, invn, cnt, ag, fg, low, tok, n2, stat, act, der, wd, wu, n1, wp, rinv, ctx, qkv, exps, wqkv)


def deliver_kernel(loss_ref, *refs):
    count = (len(refs) - 2) // 3
    ins, loss_out, outs, held, sems = refs[:count], refs[count], refs[count + 1 : 2 * count + 1], refs[2 * count + 1 : -1], refs[-1]
    moves = []
    for src, dst, mid in zip(ins, outs, held):
        parts = 8 if src.shape[0] >= 1024 and len(src.shape) == 2 else 1
        step = src.shape[0] // parts
        for k in range(parts):
            part = pl.ds(k * step, step)
            at = 2 * len(moves)
            moves.append(
                (
                    pltpu.make_async_copy(src.at[part], mid.at[part], sems.at[at]),
                    pltpu.make_async_copy(mid.at[part], dst.at[part], sems.at[at + 1]),
                )
            )
    for load, _ in moves:
        load.start()
    loss_out[0] = loss_ref[0, 0]
    for load, store in moves:
        load.wait()
        store.start()
    for _, store in moves:
        store.wait()


def deliver_call(arrays):
    hb = pl.BlockSpec(memory_space=pl.ANY)
    big, loss, *rest = arrays
    moved = [big] + rest
    same = [jax.ShapeDtypeStruct(a.shape, a.dtype) for a in moved]
    loss, *moved = pl.pallas_call(
        deliver_kernel,
        out_shape=tuple([jax.ShapeDtypeStruct((1,), F32)] + same),
        in_specs=[pl.BlockSpec(memory_space=pltpu.VMEM)] + [hb] * len(moved),
        out_specs=[pl.BlockSpec(memory_space=pltpu.SMEM)] + [hb] * len(moved),
        scratch_shapes=[pltpu.VMEM(a.shape, a.dtype) for a in moved] + [pltpu.SemaphoreType.DMA((2 * (8 + len(moved)),))],
        name="deliver",
    )(loss, *moved)
    return [moved[0], loss] + list(moved[1:])

def norm_back(grad_out, normed, inv_std, gain):
    grad_n = grad_out * gain
    return inv_std * (
        grad_n
        - jnp.mean(grad_n, axis=-1, keepdims=True)
        - normed * jnp.mean(grad_n * normed, axis=-1, keepdims=True)
    )


def attend_back(entry):
    qkv_row, exps, rinv, ctx, grad_row = entry
    row_len = qkv_row.shape[0]
    split = qkv_row.reshape(row_len, 3, HEADS, HEAD_DIM)
    queries, key_vecs, values = split[:, 0], split[:, 1], split[:, 2]
    exps = exps.reshape(HEADS, row_len, row_len)
    scaled = (grad_row.astype(F32) * rinv.astype(F32)).astype(BF16)
    delta = jnp.sum(scaled.astype(F32).reshape(row_len, HEADS, HEAD_DIM) * ctx.astype(F32).reshape(row_len, HEADS, HEAD_DIM), axis=-1)
    scaled = scaled.reshape(row_len, HEADS, HEAD_DIM)
    grad_probs = jnp.einsum("qhd,khd->hqk", scaled, values, preferred_element_type=F32)
    grad_values = jnp.einsum("hqk,qhd->khd", exps, scaled, preferred_element_type=F32)
    grad_scores = (exps.astype(F32) * (grad_probs - delta.T[..., None])).astype(BF16)
    grad_queries = jnp.einsum("hqk,khd->qhd", grad_scores, key_vecs, preferred_element_type=F32) * HEAD_DIM**-0.5
    grad_keys = jnp.einsum("hqk,qhd->khd", grad_scores, queries, preferred_element_type=F32) * HEAD_DIM**-0.5
    stacked = jnp.stack([grad_queries, grad_keys, grad_values], axis=1)
    return stacked.reshape(row_len, 3 * HEADS * HEAD_DIM).astype(BF16)


def per_device(
    tokens, segment_ids, pair_index, qkv_weight, query_bias, value_bias, proj_weight, proj_bias,
    attn_gain, attn_shift, up_weight, up_bias, down_weight, down_bias, ffn_gain, ffn_shift,
):
    n = lax.axis_size("batch")
    rows, row_len = segment_ids.shape
    toks, width = tokens.shape
    (exps, qkv, context, rinv, normed_one, first_low, acted, deriv, normed_two, layer_out, stat, z, invn, cnt) = forward_call(
        tokens, segment_ids, qkv_weight, query_bias, value_bias, proj_weight, proj_bias, attn_gain, attn_shift,
        up_weight, up_bias, down_weight, down_bias, ffn_gain, ffn_shift)
    if width % (8 * n) == 0 and n // 8 * 2 * UNIT_ROWS * 8 == up_weight.shape[1]:
        grads = deliver_call(backward_call(
            n, segment_ids, pair_index, z, invn, cnt, attn_gain, ffn_gain, first_low, tokens, normed_two, stat, acted,
            deriv, down_weight, up_weight, normed_one, proj_weight, rinv, context, qkv, exps, qkv_weight))
        return (grads[1].reshape(()), layer_out, grads[0]) + tuple(v.reshape(-1) for v in grads[2:])
    loss, grad_seg = contrast_call(n, z.astype(BF16), z, invn, cnt, pair_index)
    inv_one = stat[:, :1]
    inv_two = stat[:, 1:2]
    normed_one = normed_one.astype(F32)
    normed_two = normed_two.astype(F32)
    row_base = (jnp.arange(rows, dtype=jnp.int32) * SEGS)[:, None]
    local_ids = jnp.where(segment_ids >= 0, segment_ids + row_base, -1).reshape(toks)
    member = (local_ids[None, :] == jnp.arange(rows * SEGS, dtype=jnp.int32)[:, None]).astype(F32)
    grad_y = lax.dot_general(member, grad_seg, (((0,), (0,)), ((), ())), precision=lax.Precision.HIGHEST)
    ffn_gain_part = jnp.sum(grad_y * normed_two, axis=0)
    ffn_shift_part = jnp.sum(grad_y, axis=0)
    grad_r2 = norm_back(grad_y, normed_two, inv_two, ffn_gain)
    grad_down_low = grad_r2.astype(BF16)
    down_bias_part = jnp.sum(grad_down_low.astype(F32), axis=0)
    down_weight_part = dot_tn(acted, grad_down_low)
    grad_up_low = (dot_nt(grad_down_low, down_weight) * deriv.astype(F32)).astype(BF16)
    up_bias_part = jnp.sum(grad_up_low.astype(F32), axis=0)
    up_weight_part = dot_tn(first_low, grad_up_low)
    grad_first = grad_r2 + dot_nt(grad_up_low, up_weight)
    attn_gain_part = jnp.sum(grad_first * normed_one, axis=0)
    attn_shift_part = jnp.sum(grad_first, axis=0)
    grad_r1 = norm_back(grad_first, normed_one, inv_one, attn_gain)
    grad_att_low = grad_r1.astype(BF16)
    proj_bias_part = jnp.sum(grad_att_low.astype(F32), axis=0)
    proj_weight_part = dot_tn(context, grad_att_low)
    grad_context = dot_nt(grad_att_low, proj_weight).astype(BF16)
    by_row = lambda v: v.reshape(rows, row_len, -1)
    grad_qkv = lax.map(
        attend_back,
        (by_row(qkv), exps.reshape(rows, -1, 2, row_len, row_len), by_row(rinv), by_row(context), by_row(grad_context)),
    ).reshape(toks, 3 * width)
    qkv_bias_part = jnp.sum(grad_qkv.astype(F32), axis=0)
    qkv_weight_part = dot_tn(tokens, grad_qkv)
    tokens_grad = grad_r1 + dot_nt(grad_qkv, qkv_weight)
    scatter = lambda v: lax.psum_scatter(v.reshape(-1), "batch", scatter_dimension=0, tiled=True)
    sums = lax.psum(
        (qkv_bias_part[:width], qkv_bias_part[2 * width :], proj_bias_part, attn_gain_part, attn_shift_part,
         up_bias_part, down_bias_part, ffn_gain_part, ffn_shift_part),
        "batch",
    )
    return (loss[0, 0], layer_out, tokens_grad, scatter(qkv_weight_part), scatter(proj_weight_part),
            scatter(up_weight_part), scatter(down_weight_part)) + tuple(sums)


def solution(mesh):
    split, whole = P("batch"), P()
    return jax.shard_map(
        per_device,
        mesh=mesh,
        in_specs=(P("batch", None), P("batch", None), split) + (whole,) * 13,
        out_specs=(whole, P("batch", None), P("batch", None)) + (split,) * 4 + (whole,) * 9,
        check_vma=False,
    )
```

```python
import functools
import jax
import jax.numpy as jnp
from jax import lax
from jax.experimental import pallas as pl
from jax.experimental.pallas import tpu as pltpu
from jax.sharding import PartitionSpec as P

F32 = jnp.float32
BF16 = jnp.bfloat16
HEADS = 12
HEAD_DIM = 64
SEGS = 8
PAIR = 2 * HEAD_DIM
LN_EPS = 1e-12
NORM_EPS = 1e-06
MIB = 2**20


def dot_nn(a, b):
    return lax.dot_general(a, b, (((1,), (0,)), ((), ())), preferred_element_type=F32)


def dot_nt(a, b):
    return lax.dot_general(a, b, (((1,), (1,)), ((), ())), preferred_element_type=F32)


def dot_tn(a, b):
    return lax.dot_general(a, b, (((0,), (0,)), ((), ())), preferred_element_type=F32)


def gelu_parts(pre):
    half = 0.5 * pre
    cdf = 0.5 + 0.5 * lax.erf(pre * 0.7071067811865476)
    pdf = jnp.exp(-half * pre) * 0.3989422804014327
    return pre * cdf, cdf + pre * pdf


def normalize(resid):
    width = resid.shape[-1]
    average = jnp.sum(resid, axis=-1, keepdims=True) * (1.0 / width)
    centred = resid - average
    variance = jnp.sum(centred * centred, axis=-1, keepdims=True) * (1.0 / width)
    inv_std = lax.rsqrt(variance + LN_EPS)
    return centred * inv_std, inv_std


def forward_kernel(
    ids_ref, qb_ref, vb_ref, pb_ref, ag_ref, as_ref, ub_ref, db_ref, fg_ref, fs_ref,
    tok_hbm, wqkv_hbm, wp_hbm, wu_hbm, wd_hbm,
    exp_hbm, qkv_hbm, ctx_hbm, rinv_hbm, n1_hbm, low_hbm, act_hbm, der_hbm, n2_hbm, out_hbm,
    stat_ref, z_ref, invn_ref, cnt_ref,
    tok_s, wqkv_s, wp_s, wu_s, wd_s, qkv_s, ctx_s, rinv_s, bias_s, exp_s,
    n1_s, low_s, act_s, der_s, n2_s, out_s, in_sem, out_sem, exp_sem,
):
    rows, row_len = ids_ref.shape
    toks, width = tok_s.shape
    pairs = width // PAIR
    ff = wu_s.shape[1]
    qb, vb, pb, ag, ash, db, fg, fs = (
        ref[...].reshape(1, width) for ref in (qb_ref, vb_ref, pb_ref, ag_ref, as_ref, db_ref, fg_ref, fs_ref)
    )
    ub = ub_ref[...].reshape(1, ff)

    thirds = [
        (wqkv_hbm.at[:, k * width : (k + 1) * width], wqkv_s.at[:, k * width : (k + 1) * width]) for k in range(3)
    ]
    loads = [
        pltpu.make_async_copy(src, dst, in_sem.at[i])
        for i, (src, dst) in enumerate([(tok_hbm, tok_s)] + thirds + [(wp_hbm, wp_s), (wu_hbm, wu_s), (wd_hbm, wd_s)])
    ]
    for cp in loads:
        cp.start()
    loads[0].wait()

    tok = tok_s[...]
    blk = 256
    for j in range(3 * width // blk):
        third, off = divmod(j * blk, width)
        if off == 0:
            loads[1 + third].wait()
        piece = dot_nn(tok, wqkv_s[:, j * blk : (j + 1) * blk])
        if third == 0:
            piece = piece + qb[:, off : off + blk]
        elif third == 2:
            piece = piece + vb[:, off : off + blk]
        qkv_s[:, j * blk : (j + 1) * blk] = piece.astype(BF16)
    qkv_out = pltpu.make_async_copy(qkv_s, qkv_hbm, out_sem.at[0])
    qkv_out.start()

    lane = lax.broadcasted_iota(jnp.int32, (row_len, PAIR), 1)
    first = lane < HEAD_DIM
    ones = jnp.ones((row_len, PAIR), BF16)

    for r in range(rows):
        ids_row = ids_ref[r : r + 1, :].astype(F32)
        ids_col = jnp.transpose(jnp.broadcast_to(ids_row, (128, row_len)))
        for c in range(row_len // 128):
            bias_s[r, :, c * 128 : (c + 1) * 128] = jnp.where(
                ids_col == ids_row[:, c * 128 : (c + 1) * 128], 0.0, -1e9
            )

    def exp_store(it, slot):
        return pltpu.make_async_copy(exp_s.at[slot], exp_hbm.at[pl.ds(2 * it, 2)], exp_sem.at[slot])

    def attend(it, carry):
        r = it // (pairs // 2)
        g = lax.rem(it, pairs // 2)
        rsl = pl.ds(pl.multiple_of(r * row_len, row_len), row_len)
        slot = lax.rem(it, 2)

        @pl.when(it >= 2)
        def _():
            exp_store(it - 2, slot).wait()

        for pp in range(2):
            col = lambda base: pl.ds(pl.multiple_of(base + (2 * g + pp) * PAIR, PAIR), PAIR)
            q = qkv_s[rsl, col(0)] * jnp.asarray(HEAD_DIM**-0.5, BF16)
            k = qkv_s[rsl, col(width)]
            v = jnp.concatenate([qkv_s[rsl, col(2 * width)], ones], axis=1)
            parts = []
            for h in range(2):
                qh = jnp.where(first if h == 0 else ~first, q, jnp.zeros_like(q))
                halves = []
                for t in range(2):
                    ts = slice(t * (row_len // 2), (t + 1) * (row_len // 2))
                    s = dot_nt(qh[ts], k) + bias_s[r, ts]
                    e = jnp.exp(s - jnp.max(s, axis=1, keepdims=True)).astype(BF16)
                    exp_s[slot, pp, h, ts] = e
                    halves.append(dot_nn(e, v))
                oe = jnp.concatenate(halves, axis=0)
                rinv = 1.0 / oe[:, PAIR:]
                parts.append((oe[:, :PAIR] * rinv, rinv))
            ctx_s[rsl, col(0)] = jnp.where(first, parts[0][0], parts[1][0]).astype(BF16)
            rinv_s[rsl, col(0)] = jnp.where(first, parts[0][1], parts[1][1]).astype(BF16)
        exp_store(it, slot).start()
        return carry

    lax.fori_loop(0, rows * pairs // 2, attend, 0)
    ctx_out = pltpu.make_async_copy(ctx_s, ctx_hbm, out_sem.at[1])
    ctx_out.start()
    rinv_out = pltpu.make_async_copy(rinv_s, rinv_hbm, out_sem.at[2])
    rinv_out.start()
    for cp in loads[4:]:
        cp.wait()

    outs = [(n1_s, n1_hbm), (low_s, low_hbm), (act_s, act_hbm), (der_s, der_hbm), (n2_s, n2_hbm), (out_s, out_hbm)]

    def store(i, rsl, csl=slice(None)):
        src, dst = outs[i]
        pltpu.make_async_copy(src.at[rsl, csl], dst.at[rsl, csl], out_sem.at[3 + i]).start()

    def ffn(r, carry):
        rsl = pl.ds(pl.multiple_of(r * row_len, row_len), row_len)
        resid = tok_s[rsl, :].astype(F32) + (dot_nn(ctx_s[rsl, :], wp_s[...]) + pb)
        normed, inv_std = normalize(resid)
        n1_s[rsl, :] = normed.astype(BF16)
        first_norm = normed * ag + ash
        low = first_norm.astype(BF16)
        low_s[rsl, :] = low
        store(0, rsl)
        store(1, rsl)
        for j in range(ff // blk):
            pre = dot_nn(low, wu_s[:, j * blk : (j + 1) * blk]) + ub[:, j * blk : (j + 1) * blk]
            act, der = gelu_parts(pre)
            act_s[rsl, j * blk : (j + 1) * blk] = act.astype(BF16)
            der_s[rsl, j * blk : (j + 1) * blk] = der.astype(BF16)
            if (j + 1) * blk % width == 0:
                store(2, rsl, slice((j + 1) * blk - width, (j + 1) * blk))
                store(3, rsl, slice((j + 1) * blk - width, (j + 1) * blk))
        down = dot_nn(act_s[rsl, :], wd_s[...]) + db
        normed2, inv_std2 = normalize(first_norm + down)
        n2_s[rsl, :] = normed2.astype(BF16)
        stat_ref[rsl, :] = jnp.where(lane == 0, inv_std, inv_std2)
        y = normed2 * fg + fs
        high = y.astype(BF16)
        out_s[rsl, :] = high
        rest = (y - high.astype(F32)).astype(BF16)
        seg = lax.broadcasted_iota(jnp.int32, (SEGS, row_len), 0)
        member = (seg == ids_ref[pl.ds(r, 1), :]).astype(F32)
        count = jnp.sum(member, axis=1, keepdims=True)
        member = member.astype(BF16)
        pooled = (dot_nn(member, high) + dot_nn(member, rest)) / count
        inv_norm = lax.rsqrt(jnp.sum(pooled * pooled, axis=1, keepdims=True) + NORM_EPS)
        z = pooled * inv_norm
        ssl = pl.ds(pl.multiple_of(r * SEGS, SEGS), SEGS)
        z_ref[ssl, :] = z
        invn_ref[ssl, :] = jnp.broadcast_to(inv_norm, (SEGS, 128))
        cnt_ref[ssl, :] = jnp.broadcast_to(count, (SEGS, 128))
        store(4, rsl)
        store(5, rsl)
        return carry

    lax.fori_loop(0, rows, ffn, 0)
    for i, (src, dst) in enumerate(outs):
        pltpu.make_async_copy(src, dst, out_sem.at[3 + i]).wait()
    qkv_out.wait()
    ctx_out.wait()
    rinv_out.wait()
    for slot in range(2):
        exp_store(slot, slot).wait()


def forward_call(tokens, ids, wqkv, qb, vb, wp, pb, ag, ash, wu, ub, wd, db, fg, fs):
    toks, width = tokens.shape
    rows, row_len = ids.shape
    ff = wu.shape[1]
    pairs = width // PAIR
    segs = rows * SEGS
    sds = jax.ShapeDtypeStruct
    vm = pl.BlockSpec(memory_space=pltpu.VMEM)
    hb = pl.BlockSpec(memory_space=pl.ANY)
    return pl.pallas_call(
        forward_kernel,
        out_shape=(
            sds((rows * pairs, 2, row_len, row_len), BF16),
            sds((toks, 3 * width), BF16),
            sds((toks, width), BF16),
            sds((toks, width), BF16),
            sds((toks, width), BF16),
            sds((toks, width), BF16),
            sds((toks, ff), BF16),
            sds((toks, ff), BF16),
            sds((toks, width), BF16),
            sds((toks, width), BF16),
            sds((toks, 128), F32),
            sds((segs, width), F32),
            sds((segs, 128), F32),
            sds((segs, 128), F32),
        ),
        in_specs=[vm] * 10 + [hb] * 5,
        out_specs=[hb] * 10 + [vm] * 4,
        scratch_shapes=[
            pltpu.VMEM((toks, width), BF16),
            pltpu.VMEM(wqkv.shape, BF16),
            pltpu.VMEM(wp.shape, BF16),
            pltpu.VMEM(wu.shape, BF16),
            pltpu.VMEM(wd.shape, BF16),
            pltpu.VMEM((toks, 3 * width), BF16),
            pltpu.VMEM((toks, width), BF16),
            pltpu.VMEM((toks, width), BF16),
            pltpu.VMEM((rows, row_len, row_len), F32),
            pltpu.VMEM((2, 2, 2, row_len, row_len), BF16),
            pltpu.VMEM((toks, width), BF16),
            pltpu.VMEM((toks, width), BF16),
            pltpu.VMEM((toks, ff), BF16),
            pltpu.VMEM((toks, ff), BF16),
            pltpu.VMEM((toks, width), BF16),
            pltpu.VMEM((toks, width), BF16),
            pltpu.SemaphoreType.DMA((7,)),
            pltpu.SemaphoreType.DMA((9,)),
            pltpu.SemaphoreType.DMA((2,)),
        ],
        compiler_params=pltpu.CompilerParams(vmem_limit_bytes=60 * MIB),
        name="forward",
    )(ids, qb, vb, pb, ag, ash, ub, db, fg, fs, tokens, wqkv, wp, wu, wd)

MESH = pl.DeviceIdType.MESH
INV_TEMP = 100.0
NEG = -1000000000.0


def axis_groups(n):
    groups = []
    rest = n // 2
    while rest > 1:
        size = 4 if rest % 4 == 0 else (2 if rest % 2 == 0 else rest)
        groups.append(size)
        rest //= size
    return groups + [2]


def digits_of(me, groups):
    digits = []
    for size in reversed(groups):
        digits.append(lax.rem(me, size))
        me = me // size
    return digits[::-1]


def index_of(digits, groups):
    me = 0
    for digit, size in zip(digits, groups):
        me = me * size + digit
    return me


def contrast_math(every, msg, me, z, invn, cnt):
    total, wide = every.shape
    seg_here, width = z.shape
    emb = every[:, :width]
    own = msg[:, :width]
    own_row = (me * seg_here).astype(F32)
    own_pair = msg[:, width : width + 128].astype(F32)
    own_pair = own_pair[:, 0:1] * 256.0 + own_pair[:, 1:2]

    scores = dot_nt(own, emb) * INV_TEMP
    column = lax.broadcasted_iota(jnp.int32, scores.shape, 1).astype(F32)
    row = lax.broadcasted_iota(jnp.int32, scores.shape, 0).astype(F32) + own_row
    masked = jnp.where(column == row, NEG, scores)
    peak = jnp.max(masked, axis=1, keepdims=True)
    log_norm = peak + jnp.log(jnp.sum(jnp.exp(masked - peak), axis=1, keepdims=True))
    weight = jnp.exp(masked - log_norm) - (column == own_pair).astype(F32)
    grad = dot_nn(weight.astype(BF16), emb)

    blk = min(total, 512)
    loss = jnp.zeros((1, 1), F32)
    for b in range(total // blk):
        part = emb[b * blk : (b + 1) * blk]
        pair = every[b * blk : (b + 1) * blk, width:].astype(F32)
        pair = pair[:, 0:1] * 256.0 + pair[:, 1:2]
        scores = dot_nt(part, emb) * INV_TEMP
        column = lax.broadcasted_iota(jnp.int32, scores.shape, 1).astype(F32)
        row = lax.broadcasted_iota(jnp.int32, scores.shape, 0).astype(F32) + float(b * blk)
        masked = jnp.where(column == row, NEG, scores)
        peak = jnp.max(masked, axis=1, keepdims=True)
        log_norm = peak + jnp.log(jnp.sum(jnp.exp(masked - peak), axis=1, keepdims=True))
        positive = jnp.sum(jnp.where(column == pair, scores, 0.0), axis=1, keepdims=True)
        loss = loss + jnp.sum(log_norm - positive, axis=0, keepdims=True)
        scores = dot_nt(part, own) * INV_TEMP
        column = lax.broadcasted_iota(jnp.int32, scores.shape, 1).astype(F32) + own_row
        row = lax.broadcasted_iota(jnp.int32, scores.shape, 0).astype(F32) + float(b * blk)
        weight = jnp.where(column == row, 0.0, jnp.exp(jnp.where(column == row, NEG, scores) - log_norm))
        weight = weight - (column == pair).astype(F32)
        grad = grad + dot_tn(weight.astype(BF16), part)
    grad = grad * INV_TEMP
    pooled_grad = invn * (grad - z * jnp.sum(grad * z, axis=1, keepdims=True))
    return loss * (1.0 / total), pooled_grad / cnt


def contrast_kernel(groups, msg_ref, z_ref, invn_ref, cnt_ref, loss_ref, gp_ref, all_s, send_sem, recv_sem):
    n = 1
    for size in groups:
        n *= size
    me = lax.axis_index("batch")
    mine = digits_of(me, groups)
    seg_here, wide = msg_ref.shape
    width = z_ref.shape[1]
    total = n * seg_here
    stages = len(groups)

    def peer(stage, step):
        other = lax.rem(mine[stage] + step, groups[stage])
        return other, index_of(mine[:stage] + [other] + mine[stage + 1 :], groups)

    barrier = pltpu.get_barrier_semaphore()
    hops = 0
    for stage in range(stages):
        for step in range(1, groups[stage]):
            pl.semaphore_signal(barrier, inc=1, device_id=(peer(stage, step)[1],), device_id_type=MESH)
            hops += 1
    all_s[tuple(mine)] = msg_ref[...]
    pl.semaphore_wait(barrier, hops)

    slot = 0
    for stage in range(stages):
        copies = []
        for step in range(1, groups[stage]):
            block = all_s.at[(slice(None),) * stage + tuple(mine[stage:])]
            copies.append(
                pltpu.make_async_remote_copy(
                    src_ref=block,
                    dst_ref=block,
                    send_sem=send_sem.at[slot],
                    recv_sem=recv_sem.at[slot],
                    device_id=(peer(stage, step)[1],),
                    device_id_type=MESH,
                )
            )
            slot += 1
        for cp in copies:
            cp.start()
        for cp in copies:
            cp.wait()

    loss, grad = contrast_math(
        all_s[...].reshape(total, wide), msg_ref[...], me, z_ref[...], invn_ref[:, 0:1], cnt_ref[:, 0:1]
    )
    loss_ref[...] = jnp.broadcast_to(loss, loss_ref.shape)
    gp_ref[...] = grad


def contrast_call(n, emb_low, z, invn, cnt, pair_index):
    groups = axis_groups(n)
    seg_here, width = emb_low.shape
    high = (pair_index // 256).astype(BF16)[:, None]
    rest = (pair_index % 256).astype(BF16)[:, None]
    msg = jnp.concatenate([emb_low, high, rest, jnp.zeros((seg_here, 126), BF16)], axis=1)
    copies = sum(size - 1 for size in groups)
    vm = pl.BlockSpec(memory_space=pltpu.VMEM)
    return pl.pallas_call(
        functools.partial(contrast_kernel, groups),
        out_shape=(jax.ShapeDtypeStruct((8, 128), F32), jax.ShapeDtypeStruct((seg_here, width), F32)),
        in_specs=[vm] * 4,
        out_specs=[vm] * 2,
        scratch_shapes=[
            pltpu.VMEM(tuple(groups) + msg.shape, BF16),
            pltpu.SemaphoreType.DMA((copies,)),
            pltpu.SemaphoreType.DMA((copies,)),
        ],
        compiler_params=pltpu.CompilerParams(collective_id=0, has_side_effects=True, vmem_limit_bytes=56 * MIB),
        name="contrast",
    )(msg, z, invn, cnt)

UNIT_ROWS = 48


def event_plan(pieces, units):
    core, axis, hop, own = 2.4, 6.8, 2.8, 0.1
    free = {"x": 0.0, "y": 0.0, "z": 0.0}
    pending = []
    plan = []
    now = 0.0

    def advance(unit, step, at):
        size = unit["size"]
        if step == 0:
            return at + core * size
        if step == 1 and unit["flat"]:
            free["x"] = free["y"] = max(at, free["x"], free["y"]) + axis * size
            return free["x"] + hop
        if step == 1:
            lane, cost = unit["first"], axis
        elif unit["flat"]:
            lane, cost = "z", axis / 2
        elif unit["z_last"]:
            lane, cost = (unit["second"], axis / 2) if step == 2 else ("z", axis / 2)
        else:
            lane, cost = ("z", axis) if step == 2 else (unit["second"], axis / 8)
        start = max(at, free[lane])
        free[lane] = start + cost * size
        return start + cost * size + hop

    def serve(entry, steps):
        nonlocal now
        at, uid, step = entry
        now = max(now, at) + own
        steps.append((uid, step))
        if step < last_step(units[uid]):
            pending.append((advance(units[uid], step, now), uid, step + 1))
            pending.sort()

    for name, cost in pieces:
        now += cost
        steps = []
        for unit in units:
            if unit["after"] == name:
                steps.append((unit["id"], 0))
                pending.append((advance(unit, 0, now), unit["id"], 1))
        pending.sort()
        while pending and pending[0][0] <= now:
            serve(pending.pop(0), steps)
        plan.append(steps)
    steps = []
    while pending:
        serve(pending.pop(0), steps)
    plan.append(steps)
    return plan, now


def last_step(unit):
    return 3 if unit["flat"] else 4


def unit_list(depth, groups, orders):
    names = (
        [("down", j, "down%d" % (depth - 1), 4 / 3) for j in range(3)]
        + [("up", u, "up%d" % u, 1.0) for u in range(4)]
        + [("proj", 4, "proj", 1.0)]
        + [("qkv", 5 + g, "dqkv%d" % g, 1.0) for g in range(groups)]
    )
    units = []
    for uid, ((kind, at, after, size), order) in enumerate(zip(names, orders)):
        units.append(
            {
                "id": uid, "kind": kind, "at": at, "after": after, "size": size, "z_last": order[-1] == "z", "flat": len(order) == 2,
                "first": order[0][0], "second": order[1] if order[-1] == "z" else order[2],
            }
        )
    return units


def piece_list(depth, groups, rows):
    pieces = []
    for j in range(4):
        pieces.append(("up%d" % j, 3.0))
        if j == DOWN_AFTER:
            pieces += [("down%d" % m, 1.6) for m in range(depth)]
        pieces.append(("first%d" % j, 1.7))
    pieces += [("norm%d" % r, 2.0) for r in range(rows)] + [("proj", 1.5)]
    for g in range(groups):
        pieces += [("attn%d%d" % (g, i), 1.6) for i in range(2 * rows)] + [("dqkv%d" % g, 1.5)]
    return pieces + [("tok%d" % g, 2.0) for g in range(groups)]


DOWN_AFTER = 0
ORDERS = ("yzx", "xyz", "xyz", "pz", "yzx", "yxz", "xzy", "yxz", "xyz", "pz", "pz")


def colsum(v):
    return jnp.sum(v, axis=0, keepdims=True)


def norm_back_k(grad_n, normed, inv_std):
    scale = 1.0 / grad_n.shape[-1]
    mean = jnp.sum(grad_n, axis=-1, keepdims=True) * scale
    dots = jnp.sum(grad_n * normed, axis=-1, keepdims=True) * scale
    return inv_std * (grad_n - mean - normed * dots)


def backward_kernel(
    depth,
    ids_ref, pair_ref, z_ref, invn_ref, cnt_ref, ag_ref, fg_ref,
    low_hbm, tok_hbm, n2_hbm, stat_hbm, act_hbm, der_hbm, wd_hbm, wu_hbm, n1_hbm, wp_hbm, rinv_hbm, ctx_hbm,
    qkv_hbm, exp_hbm, wqkv_hbm,
    tg_hbm, loss_ref, oq_ref, op_ref, ou_ref, od_ref, v_qb, v_vb, v_pb, v_ag, v_as, v_ub, v_db, v_fg, v_fs,
    w_s, wd_s, rc_s, rcd_s, r2_s, r2d_s, q_s, qd_s,
    all_s, low_t, tok_t, tok_s, stream_s, g_s, ctx_s, rdo_s, qg_s, exp_s, gq_s, tg_s, wst_s, wp_s, stat_s,
    sum_s, ar0_s, ar1_s, ar2_s, br0_s, br1_s, br2_s,
    send_sem, recv_sem, gsend_sem, grecv_sem, asend_sem, arecv_sem, in_sem, str_sem, wst_sem, grp_sem, exp_sem, out_sem,
):
    toks, width = tok_s.shape
    half = width // 2
    ff = act_hbm.shape[1]
    kinds = ff // width
    row_len = exp_s.shape[3]
    rows = toks // row_len
    strip = width // (8 * depth)
    groups = width // (2 * PAIR)
    seg_here = z_ref.shape[0]
    me = lax.axis_index("batch")
    c = lax.rem(me, 2)
    x = lax.rem(me // 2, 2)
    y = lax.rem(me // 4, 2)
    z = me // 8
    xy = y * 2 + x

    def index(zz, yy, xx, cc):
        return ((zz * 2 + yy) * 2 + xx) * 2 + cc

    core_peer = index(z, y, x, 1 - c)
    x_peer = index(z, y, 1 - x, c)
    y_peer = index(z, 1 - y, x, c)
    xy_peer = index(z, 1 - y, 1 - x, c)
    z_peers = [index(lax.rem(z + step, depth), y, x, c) for step in range(1, depth)]
    everyone = [core_peer, x_peer, y_peer, xy_peer] + z_peers

    barrier = pltpu.get_barrier_semaphore()
    for other in everyone:
        pl.semaphore_signal(barrier, inc=1, device_id=(other,), device_id_type=MESH)

    local = pltpu.make_async_copy

    items = []
    for j in range(kinds):
        items.append(("der", j))
        if j == DOWN_AFTER:
            items += [("act", m) for m in range(depth)]

    def stream(k):
        name, off = items[k]
        src = der_hbm if name == "der" else act_hbm
        return local(src.at[:, off * width : (off + 1) * width], stream_s.at[k % 2], str_sem.at[k % 2])

    def stream_next(k):
        if k + 2 < len(items):
            stream(k + 2).start()

    def ffn_weights(j):
        at = (j % 2) * 2
        return [
            local(wd_hbm.at[j * width : (j + 1) * width, :], wst_s.at[at], wst_sem.at[at]),
            local(wu_hbm.at[:, j * width : (j + 1) * width], wst_s.at[at + 1], wst_sem.at[at + 1]),
        ]

    def group_loads(g):
        return [
            local(
                qkv_hbm.at[:, third * width + g * 2 * PAIR : third * width + (g + 1) * 2 * PAIR],
                qg_s.at[g % 2, :, third * 2 * PAIR : (third + 1) * 2 * PAIR],
                grp_sem.at[(g % 2) * 3 + third],
            )
            for third in range(3)
        ]

    def weight_loads(g):
        return [
            local(
                wqkv_hbm.at[:, third * width + g * 2 * PAIR : third * width + (g + 1) * 2 * PAIR],
                wst_s.at[g, :, third * 2 * PAIR : (third + 1) * 2 * PAIR],
                wst_sem.at[4 + g * 3 + third],
            )
            for third in range(3)
        ]

    def exp_load(r, p, slot):
        return local(exp_hbm.at[r * (width // PAIR) + p], exp_s.at[slot], exp_sem.at[slot])

    low_load = local(low_hbm, tok_s, in_sem.at[0])
    tok_load = local(tok_hbm, tok_s, in_sem.at[1])
    n2_load = local(n2_hbm, gq_s, in_sem.at[2])
    stat_load = local(stat_hbm, stat_s, in_sem.at[3])
    n1_load = local(n1_hbm, qg_s.at[1], in_sem.at[4])
    rinv_load = local(rinv_hbm, tok_s, in_sem.at[5])
    wp_load = local(wp_hbm, wp_s, in_sem.at[6])
    ctx_load = local(ctx_hbm, ctx_s, in_sem.at[7])
    low_load.start()
    n2_load.start()
    stat_load.start()
    stream(0).start()
    stream(1).start()
    for j in range(2):
        for cp in ffn_weights(j):
            cp.start()
    n1_load.start()
    wp_load.start()
    ctx_load.start()
    for cp in group_loads(0):
        cp.start()
    exp_load(0, 0, 0).start()

    def remote(src, dst, slot, device, ssem=send_sem, rsem=recv_sem):
        return pltpu.make_async_remote_copy(
            src_ref=src, dst_ref=dst, send_sem=ssem.at[slot], recv_sem=rsem.at[slot], device_id=(device,), device_id_type=MESH
        )

    pair_row = jnp.broadcast_to(pair_ref[...].reshape(1, seg_here), (seg_here, seg_here))
    here = lax.broadcasted_iota(jnp.int32, (seg_here, seg_here), 0) == lax.broadcasted_iota(
        jnp.int32, (seg_here, seg_here), 1
    )
    as_column = lambda v: jnp.sum(jnp.where(here, v.astype(F32), 0.0), axis=1, keepdims=True)
    lane = lax.broadcasted_iota(jnp.int32, (seg_here, 128), 1)
    tag = jnp.where(lane == 0, as_column(pair_row // 256), 0.0) + jnp.where(lane == 1, as_column(pair_row % 256), 0.0)
    msg = jnp.concatenate([z_ref[...].astype(BF16), tag.astype(BF16)], axis=1)
    all_s[z, xy, c] = msg

    def gather(stage):
        if stage == 0:
            ref, others = all_s.at[z, xy, c], z_peers
        elif stage == 1:
            ref, others = all_s.at[:, xy, c], [x_peer, y_peer, xy_peer]
        else:
            ref, others = all_s.at[:, :, c], [core_peer]
        base = (0, depth - 1, depth + 2)[stage]
        return [remote(ref, ref, base + k, other, gsend_sem, grecv_sem) for k, other in enumerate(others)]

    pl.semaphore_wait(barrier, len(everyone))
    for cp in gather(0):
        cp.start()
    low_load.wait()
    low_t[...] = jnp.transpose(tok_s[...])
    tok_load.start()
    for cp in gather(0):
        cp.wait_recv()
    for cp in gather(1):
        cp.start()
    for cp in gather(1):
        cp.wait_recv()
    for cp in gather(2):
        cp.start()
    tok_load.wait()
    tok_t[...] = jnp.transpose(tok_s[...])
    rinv_load.start()
    br0_s[z] = jnp.zeros(br0_s.shape[1:], F32)
    sum_s[...] = jnp.zeros_like(sum_s)
    for cp in gather(2):
        cp.wait_recv()
    loss, grad_seg = contrast_math(
        all_s[...].reshape(8 * depth * seg_here, msg.shape[1]), msg, me, z_ref[...], invn_ref[:, 0:1], cnt_ref[:, 0:1]
    )
    loss_ref[...] = jnp.broadcast_to(loss, loss_ref.shape)

    units = unit_list(depth, groups, ORDERS)
    pieces = piece_list(depth, groups, rows)
    plan, _ = event_plan(pieces, units)
    places = [name for name, _ in pieces]

    def bufs(unit):
        if unit["kind"] == "down":
            return [ref.at[unit["at"]] for ref in (wd_s, rcd_s, r2d_s, qd_s)]
        return [ref.at[unit["at"]] for ref in (w_s, rc_s, r2_s, q_s)]

    def unit_copies(unit, step):
        w, rc, r2, q = bufs(unit)
        f, s = (y, x) if unit["first"] == "y" else (x, y)
        f_peer, s_peer = (y_peer, x_peer) if unit["first"] == "y" else (x_peer, y_peer)
        base = unit["id"] * (3 + depth)
        if step == 0:
            return [remote(w.at[1 - c], rc, base, core_peer)]
        if unit["flat"] and step == 1:
            return [
                remote(w.at[c, 1 - x, y], r2.at[0], base + 1, x_peer),
                remote(w.at[c, x, 1 - y], r2.at[1], base + 2, y_peer),
                remote(w.at[c, 1 - x, 1 - y], q.at[0], base + 2 + depth, xy_peer),
            ]
        if unit["flat"]:
            return [
                remote(w.at[c, x, y, lax.rem(z + k, depth)], q.at[1, z], base + 2 + k, z_peers[k - 1])
                for k in range(1, depth)
            ]
        if step == 1:
            return [remote(w.at[c, 1 - f], r2, base + 1, f_peer)]
        if unit["z_last"]:
            if step == 2:
                return [remote(w.at[c, f, 1 - s], q.at[0], base + 2, s_peer)]
            return [
                remote(w.at[c, f, s, lax.rem(z + k, depth)], q.at[1, z], base + 2 + k, z_peers[k - 1])
                for k in range(1, depth)
            ]
        if step == 2:
            return [
                remote(w.at[c, f, :, lax.rem(z + k, depth)], q.at[:, z], base + 2 + k, z_peers[k - 1])
                for k in range(1, depth)
            ]
        return [remote(w.at[c, f, 1 - s, z], q.at[0, z], base + 2, s_peer)]

    def finish(unit, total):
        kind, at = unit["kind"], unit["at"]
        if kind == "down":
            per = width // 128
            for k in range(4):
                start = (k // 2) * UNIT_ROWS * per + at * 2 + k % 2
                od_ref[pl.ds(start, UNIT_ROWS, stride=per), :] = total[:, k * 128 : (k + 1) * 128]
            return
        for k in range(6):
            piece = total[(k // 3) * strip : (k // 3 + 1) * strip, (k % 3) * 128 : (k % 3 + 1) * 128]
            if kind == "up":
                ref, per, col = ou_ref, ff // 128, at * 6 + k
            elif kind == "proj":
                ref, per, col = op_ref, width // 128, k
            else:
                ref, per, col = oq_ref, 3 * width // 128, (k // 2) * (width // 128) + (at - 5) * 2 + k % 2
            ref[pl.ds(col, strip, stride=per), :] = piece

    def take(unit, step):
        w, rc, r2, q = bufs(unit)
        f, s = (y, x) if unit["first"] == "y" else (x, y)
        z_last = unit["z_last"]
        if step > 0:
            for cp in unit_copies(unit, step - 1):
                cp.wait_recv()
        f32 = lambda v: v.astype(F32)
        two = lambda a, b: f32(w[c, f, a, b]) + f32(rc[f, a, b]) + f32(r2[a, b])
        four = lambda b: f32(w[c, x, y, b]) + f32(rc[x, y, b]) + f32(r2[0, b]) + f32(r2[1, b]) + f32(q[0, b])
        if step == 1 and unit["flat"]:

            def body(i, carry):
                b = lax.rem(i, depth)
                k = 1 + i // depth
                a1, a2 = lax.rem(x + k % 2, 2), lax.rem(y + k // 2, 2)
                w[c, a1, a2, b] = (f32(w[c, a1, a2, b]) + f32(rc[a1, a2, b])).astype(BF16)
                return carry

            lax.fori_loop(0, 3 * depth, body, 0)
        elif unit["flat"] and step == 2:

            def body(k, carry):
                b = lax.rem(z + k, depth)
                w[c, x, y, b] = four(b).astype(BF16)
                return carry

            lax.fori_loop(1, depth, body, 0)
        elif unit["flat"] and step == 3:
            total = four(z)
            for k in range(1, depth):
                total = total + f32(q[1, lax.rem(z + k, depth)])
            finish(unit, total)
        elif step == 1:

            def body(i, carry):
                a, b = i // depth, lax.rem(i, depth)
                w[c, 1 - f, a, b] = (f32(w[c, 1 - f, a, b]) + f32(rc[1 - f, a, b])).astype(BF16)
                return carry

            lax.fori_loop(0, 2 * depth, body, 0)
        elif step == 2 and z_last:

            def body(b, carry):
                w[c, f, 1 - s, b] = two(1 - s, b).astype(BF16)
                return carry

            lax.fori_loop(0, depth, body, 0)
        elif step == 3 and z_last:

            def body(k, carry):
                b = lax.rem(z + k, depth)
                w[c, f, s, b] = (two(s, b) + f32(q[0, b])).astype(BF16)
                return carry

            lax.fori_loop(1, depth, body, 0)
        elif step == 2:

            def body(k, carry):
                b = lax.rem(z + 1 + k // 2, depth)
                a = lax.rem(k, 2)
                w[c, f, a, b] = two(a, b).astype(BF16)
                return carry

            lax.fori_loop(0, 2 * (depth - 1), body, 0)
        elif step == 3:
            total = two(1 - s, z)
            for k in range(1, depth):
                total = total + f32(q[1 - s, lax.rem(z + k, depth)])
            w[c, f, 1 - s, z] = total.astype(BF16)
        elif step == 4:
            total = two(s, z) + f32(q[0, z])
            for k in range(1, depth):
                total = total + f32(q[1 if z_last else s, lax.rem(z + k, depth)])
            finish(unit, total)
        if step < last_step(unit):
            for cp in unit_copies(unit, step):
                cp.start()

    def after(name):
        for uid, step in plan[places.index(name)]:
            take(units[uid], step)

    def vec_copies(which, stage):
        bank = ((ar0_s, ar1_s, ar2_s), (br0_s, br1_s, br2_s))[which][stage]
        base = which * (depth + 3) + (0, depth - 1, depth + 2)[stage]
        slot, others = ((z, z_peers), (xy, [x_peer, y_peer, xy_peer]), (c, [core_peer]))[stage]
        return [
            remote(bank.at[slot], bank.at[slot], base + k, other, asend_sem, arecv_sem) for k, other in enumerate(others)
        ]

    def vec_step(which, step):
        banks = ((ar0_s, ar1_s, ar2_s), (br0_s, br1_s, br2_s))[which]
        total = None
        if step > 0:
            for cp in vec_copies(which, step - 1):
                cp.wait_recv()
            bank = banks[step - 1]
            total = bank[0].astype(F32)
            for k in range(1, bank.shape[0]):
                total = total + bank[k].astype(F32)
        if step < 3:
            if step > 0:
                banks[step][xy if step == 1 else c] = total.astype(banks[step].dtype)
            for cp in vec_copies(which, step):
                cp.start()
        elif which == 0:
            for k, ref in enumerate((v_fg, v_fs, v_db, v_ag, v_as, v_pb)):
                ref[...] = total[k : k + 1].reshape(width)
            v_ub[...] = jnp.concatenate([total[6 + k : 7 + k] for k in range(kinds)], axis=1).reshape(ff)
        else:
            v_qb[...] = jnp.concatenate([total[k : k + 1] for k in range(groups)], axis=1).reshape(width)
            v_vb[...] = jnp.concatenate([total[groups + k : groups + k + 1] for k in range(groups)], axis=1).reshape(width)

    def put_unit(unit, res):
        w = bufs(unit)[0]
        for d in range(8 * depth):
            cc, xx, yy, zz = d % 2, d // 2 % 2, d // 4 % 2, d // 8
            f, s = (yy, xx) if unit["first"] == "y" else (xx, yy)
            piece = res[d * strip : (d + 1) * strip]
            w[cc, f, s, zz] = jnp.concatenate([piece[:, :half], piece[:, half:]], axis=0).astype(BF16)

    n2_load.wait()
    stat_load.wait()
    for r in range(rows):
        rsl = slice(r * row_len, (r + 1) * row_len)
        seg = lax.broadcasted_iota(jnp.int32, (SEGS, row_len), 0)
        member = (seg == ids_ref[r : r + 1, :]).astype(BF16)
        gp = grad_seg[r * SEGS : (r + 1) * SEGS, :]
        high = gp.astype(BF16)
        rest = (gp - high.astype(F32)).astype(BF16)
        grad_y = dot_tn(member, high) + dot_tn(member, rest)
        n2 = gq_s[rsl, :].astype(F32)
        sum_s[0:1, :] += colsum(grad_y * n2)
        sum_s[1:2, :] += colsum(grad_y)
        grad_r2 = norm_back_k(grad_y * fg_ref[...].reshape(1, width), n2, stat_s[rsl, 1:2])
        gdl = grad_r2.astype(BF16)
        tg_s[rsl, :] = grad_r2
        g_s[rsl, :] = gdl
        sum_s[2:3, :] += colsum(gdl.astype(F32))

    for j in range(kinds):
        at_stream = items.index(("der", j))
        at = (j % 2) * 2
        loads = ffn_weights(j)
        loads[0].wait()
        stream(at_stream).wait()
        for b in range(3):
            bsl = slice(b * 256, (b + 1) * 256)
            grad_act = dot_nt(g_s[...], wst_s[at, bsl, :])
            gul = (grad_act * stream_s[at_stream % 2, :, bsl].astype(F32)).astype(BF16)
            gq_s[:, bsl] = gul
            sum_s[6 + j : 7 + j, bsl] = colsum(gul.astype(F32))
        stream_next(at_stream)
        put_unit(units[3 + j], dot_nn(low_t[...], gq_s[...]))
        after("up%d" % j)
        for m in range(depth if j == DOWN_AFTER else 0):
            stream(at_stream + 1 + m).wait()
            res = dot_tn(stream_s[(at_stream + 1 + m) % 2], g_s[...])
            stream_next(at_stream + 1 + m)
            for i in range(8):
                cc, xx, yy = i % 2, i // 2 % 2, i // 4
                piece = res[i * 2 * UNIT_ROWS : (i + 1) * 2 * UNIT_ROWS]
                for k in range(3):
                    f, s = (yy, xx) if units[k]["first"] == "y" else (xx, yy)
                    blk = piece[:, k * 256 : (k + 1) * 256]
                    wd_s[k, cc, f, s, m] = jnp.concatenate([blk[:UNIT_ROWS], blk[UNIT_ROWS:]], axis=1).astype(BF16)
            after("down%d" % m)
        loads[1].wait()
        for b in range(3):
            bsl = slice(b * 256, (b + 1) * 256)
            tg_s[:, bsl] += dot_nt(gq_s[...], wst_s[at + 1, bsl, :])
        if j + 2 < kinds:
            for cp in ffn_weights(j + 2):
                cp.start()
        after("first%d" % j)

    for g in range(groups):
        for cp in weight_loads(g):
            cp.start()
    n1_load.wait()
    wp_load.wait()
    rinv_load.wait()
    for r in range(rows):
        rsl = slice(r * row_len, (r + 1) * row_len)
        grad_first = tg_s[rsl, :]
        n1 = qg_s[1, rsl, :].astype(F32)
        sum_s[3:4, :] += colsum(grad_first * n1)
        sum_s[4:5, :] += colsum(grad_first)
        grad_r1 = norm_back_k(grad_first * ag_ref[...].reshape(1, width), n1, stat_s[rsl, 0:1])
        tg_s[rsl, :] = grad_r1
        gal = grad_r1.astype(BF16)
        g_s[rsl, :] = gal
        sum_s[5:6, :] += colsum(gal.astype(F32))
        grad_ctx = dot_nt(gal, wp_s[...]).astype(BF16)
        rdo_s[rsl, :] = (grad_ctx.astype(F32) * tok_s[rsl, :].astype(F32)).astype(BF16)
        after("norm%d" % r)
    ar0_s[z] = sum_s[...].astype(BF16)
    vec_step(0, 0)
    ctx_load.wait()
    put_unit(units[7], dot_tn(ctx_s[...], g_s[...]))
    after("proj")

    lane = lax.broadcasted_iota(jnp.int32, (row_len, 2 * PAIR), 1)
    first = lax.rem(lane, PAIR) < HEAD_DIM
    ones = jnp.ones((row_len, PAIR), BF16)
    scale = HEAD_DIM**-0.5
    grads = [stream_s.at[0], stream_s.at[1], gq_s]
    for g in range(groups):
        for cp in group_loads(g):
            cp.wait()
        if g + 1 < groups:
            for cp in group_loads(g + 1):
                cp.start()

        def attend(i, carry):
            r, pp = i // 2, lax.rem(i, 2)
            slot = lax.rem(i, 2)
            exp_load(r, 2 * g + pp, slot).wait()

            @pl.when(i + 1 < 2 * rows)
            def _():
                exp_load((i + 1) // 2, 2 * g + lax.rem(i + 1, 2), 1 - slot).start()

            if g + 1 < groups:

                @pl.when(i + 1 == 2 * rows)
                def _():
                    exp_load(0, 2 * (g + 1), 0).start()

            rsl = pl.ds(pl.multiple_of(r * row_len, row_len), row_len)
            lanes = lambda base: pl.ds(pl.multiple_of(base + pp * PAIR, PAIR), PAIR)
            q = qg_s[g % 2, rsl, lanes(0)]
            k = qg_s[g % 2, rsl, lanes(2 * PAIR)]
            v = qg_s[g % 2, rsl, lanes(4 * PAIR)]
            do = rdo_s[rsl, lanes(g * 2 * PAIR)]
            ctx = ctx_s[rsl, lanes(g * 2 * PAIR)]
            neg = -(do.astype(F32) * ctx.astype(F32))
            lhs = jnp.concatenate([do, neg.astype(BF16)], axis=1)
            rhs = jnp.concatenate([v, ones], axis=1)
            do_t = jnp.transpose(do)
            q_t = jnp.transpose(q)
            dq, dk, dv = [], [], []
            for h in range(2):
                lh = jnp.where(first if h == 0 else ~first, lhs, jnp.zeros_like(lhs))
                e = exp_s[slot, h]
                ds = (e.astype(F32) * dot_nt(lh, rhs)).astype(BF16)
                hs = slice(h * HEAD_DIM, (h + 1) * HEAD_DIM)
                dv.append(dot_nn(do_t[hs], e))
                dk.append(dot_nn(q_t[hs], ds))
                dq.append(dot_nn(ds, k))
            dq = (jnp.where(first[:, :PAIR], dq[0], dq[1]) * scale).astype(BF16)
            dk = jnp.transpose((jnp.concatenate(dk, axis=0) * scale).astype(BF16))
            dv = jnp.transpose(jnp.concatenate(dv, axis=0).astype(BF16))
            grads[g][rsl, lanes(0)] = dq
            grads[g][rsl, lanes(2 * PAIR)] = dk
            grads[g][rsl, lanes(4 * PAIR)] = dv
            br0_s[z, g : g + 1, lanes(0)] += colsum(dq.astype(F32))
            br0_s[z, groups + g : groups + g + 1, lanes(0)] += colsum(dv.astype(F32))
            for step in range(2 * rows):
                if plan[places.index("attn%d%d" % (g, step))]:

                    @pl.when(i == step)
                    def _():
                        after("attn%d%d" % (g, step))

            return carry

        lax.fori_loop(0, 2 * rows, attend, 0)
        put_unit(units[8 + g], dot_nn(tok_t[...], grads[g][...]))
        after("dqkv%d" % g)
        vec_step(0, g + 1)
    vec_step(1, 0)
    for g in range(groups):
        for cp in weight_loads(g):
            cp.wait()
        for b in range(3):
            bsl = slice(b * 256, (b + 1) * 256)
            tg_s[:, bsl] += dot_nt(grads[g][...], wst_s[g, bsl, :])
        after("tok%d" % g)
    tg_out = local(tg_s, tg_hbm, out_sem)
    tg_out.start()
    left = plan[-1]
    marks = {len(left) * (k + 1) // 4: k + 1 for k in range(3)}
    for k, (uid, step) in enumerate(left):
        if k in marks:
            vec_step(1, marks[k])
        take(units[uid], step)
    for stage in range(3):
        for cp in gather(stage):
            cp.wait_send()
    for step in range(4):
        for unit in units:
            if step < last_step(unit):
                for cp in unit_copies(unit, step):
                    cp.wait_send()
    for which in range(2):
        for stage in range(3):
            for cp in vec_copies(which, stage):
                cp.wait_send()
    tg_out.wait()


def backward_call(n, ids, pair, zed, invn, cnt, ag, fg, low, tok, n2, stat, act, der, wd, wu, n1, wp, rinv, ctx, qkv, exps, wqkv):
    depth = n // 8
    toks, width = tok.shape
    ff = act.shape[1]
    row_len = exps.shape[2]
    groups = width // (2 * PAIR)
    half = width // 2
    segs = zed.shape[0]
    sds = jax.ShapeDtypeStruct
    vm = pl.BlockSpec(memory_space=pltpu.VMEM)
    hb = pl.BlockSpec(memory_space=pl.ANY)
    flat = lambda cols, rws: sds((rws // n * cols // 128, 128), F32)
    v = lambda k: sds((k,), F32)
    wide = lambda *lead: [pltpu.VMEM((8,) + lead + (UNIT_ROWS, half), BF16), pltpu.VMEM((3,) + lead + (UNIT_ROWS, 512), BF16)]
    big = pltpu.VMEM((toks, width), BF16)
    turned = pltpu.VMEM((width, toks), BF16)
    sem = lambda k: pltpu.SemaphoreType.DMA((k,))
    scratch = wide(2, 2, 2, depth) + wide(2, 2, depth) + wide(2, depth) + wide(2, depth)
    scratch += [
        pltpu.VMEM((depth, 4, 2, segs, width + 128), BF16),
        turned,
        turned,
        big,
        pltpu.VMEM((2, toks, width), BF16),
        big,
        big,
        big,
        pltpu.VMEM((2, toks, 6 * PAIR), BF16),
        pltpu.VMEM((2, 2, row_len, row_len), BF16),
        big,
        pltpu.VMEM((toks, width), F32),
        pltpu.VMEM((4, width, width), BF16),
        pltpu.VMEM((width, width), BF16),
        pltpu.VMEM((toks, 128), F32),
        pltpu.VMEM((16, width), F32),
        pltpu.VMEM((depth, 16, width), BF16),
        pltpu.VMEM((4, 16, width), BF16),
        pltpu.VMEM((2, 16, width), BF16),
        pltpu.VMEM((depth, 8, 2 * PAIR), F32),
        pltpu.VMEM((4, 8, 2 * PAIR), F32),
        pltpu.VMEM((2, 8, 2 * PAIR), F32),
        sem(11 * (3 + depth)),
        sem(11 * (3 + depth)),
        sem(depth + 3),
        sem(depth + 3),
        sem(2 * (depth + 3)),
        sem(2 * (depth + 3)),
        sem(8),
        sem(2),
        sem(4 + 3 * groups),
        sem(6),
        sem(2),
        pltpu.SemaphoreType.DMA,
    ]
    return pl.pallas_call(
        functools.partial(backward_kernel, depth),
        out_shape=(
            sds((toks, width), F32), sds((8, 128), F32),
            flat(3 * width, width), flat(width, width), flat(ff, width), flat(width, ff),
            v(width), v(width), v(width), v(width), v(width), v(ff), v(width), v(width), v(width),
        ),
        in_specs=[vm] * 7 + [hb] * 15,
        out_specs=[hb] + [vm] * 14,
        scratch_shapes=scratch,
        compiler_params=pltpu.CompilerParams(collective_id=1, has_side_effects=True, vmem_limit_bytes=63 * MIB),
        name="backward",
    )(ids, pair, zed, invn, cnt, ag, fg, low, tok, n2, stat, act, der, wd, wu, n1, wp, rinv, ctx, qkv, exps, wqkv)


def deliver_kernel(loss_ref, *refs):
    count = (len(refs) - 2) // 3
    ins, loss_out, outs, held, sems = refs[:count], refs[count], refs[count + 1 : 2 * count + 1], refs[2 * count + 1 : -1], refs[-1]
    moves = []
    for src, dst, mid in zip(ins, outs, held):
        parts = 8 if src.shape[0] >= 1024 and len(src.shape) == 2 else 1
        step = src.shape[0] // parts
        for k in range(parts):
            part = pl.ds(k * step, step)
            at = 2 * len(moves)
            moves.append(
                (
                    pltpu.make_async_copy(src.at[part], mid.at[part], sems.at[at]),
                    pltpu.make_async_copy(mid.at[part], dst.at[part], sems.at[at + 1]),
                )
            )
    for load, _ in moves:
        load.start()
    loss_out[0] = loss_ref[0, 0]
    for load, store in moves:
        load.wait()
        store.start()
    for _, store in moves:
        store.wait()


def deliver_call(arrays):
    hb = pl.BlockSpec(memory_space=pl.ANY)
    big, loss, *rest = arrays
    moved = [big] + rest
    same = [jax.ShapeDtypeStruct(a.shape, a.dtype) for a in moved]
    loss, *moved = pl.pallas_call(
        deliver_kernel,
        out_shape=tuple([jax.ShapeDtypeStruct((1,), F32)] + same),
        in_specs=[pl.BlockSpec(memory_space=pltpu.VMEM)] + [hb] * len(moved),
        out_specs=[pl.BlockSpec(memory_space=pltpu.SMEM)] + [hb] * len(moved),
        scratch_shapes=[pltpu.VMEM(a.shape, a.dtype) for a in moved] + [pltpu.SemaphoreType.DMA((2 * (8 + len(moved)),))],
        name="deliver",
    )(loss, *moved)
    return [moved[0], loss] + list(moved[1:])

def norm_back(grad_out, normed, inv_std, gain):
    grad_n = grad_out * gain
    return inv_std * (
        grad_n
        - jnp.mean(grad_n, axis=-1, keepdims=True)
        - normed * jnp.mean(grad_n * normed, axis=-1, keepdims=True)
    )


def attend_back(entry):
    qkv_row, exps, rinv, ctx, grad_row = entry
    row_len = qkv_row.shape[0]
    split = qkv_row.reshape(row_len, 3, HEADS, HEAD_DIM)
    queries, key_vecs, values = split[:, 0], split[:, 1], split[:, 2]
    exps = exps.reshape(HEADS, row_len, row_len)
    scaled = (grad_row.astype(F32) * rinv.astype(F32)).astype(BF16)
    delta = jnp.sum(scaled.astype(F32).reshape(row_len, HEADS, HEAD_DIM) * ctx.astype(F32).reshape(row_len, HEADS, HEAD_DIM), axis=-1)
    scaled = scaled.reshape(row_len, HEADS, HEAD_DIM)
    grad_probs = jnp.einsum("qhd,khd->hqk", scaled, values, preferred_element_type=F32)
    grad_values = jnp.einsum("hqk,qhd->khd", exps, scaled, preferred_element_type=F32)
    grad_scores = (exps.astype(F32) * (grad_probs - delta.T[..., None])).astype(BF16)
    grad_queries = jnp.einsum("hqk,khd->qhd", grad_scores, key_vecs, preferred_element_type=F32) * HEAD_DIM**-0.5
    grad_keys = jnp.einsum("hqk,qhd->khd", grad_scores, queries, preferred_element_type=F32) * HEAD_DIM**-0.5
    stacked = jnp.stack([grad_queries, grad_keys, grad_values], axis=1)
    return stacked.reshape(row_len, 3 * HEADS * HEAD_DIM).astype(BF16)


def per_device(
    tokens, segment_ids, pair_index, qkv_weight, query_bias, value_bias, proj_weight, proj_bias,
    attn_gain, attn_shift, up_weight, up_bias, down_weight, down_bias, ffn_gain, ffn_shift,
):
    n = lax.axis_size("batch")
    rows, row_len = segment_ids.shape
    toks, width = tokens.shape
    (exps, qkv, context, rinv, normed_one, first_low, acted, deriv, normed_two, layer_out, stat, z, invn, cnt) = forward_call(
        tokens, segment_ids, qkv_weight, query_bias, value_bias, proj_weight, proj_bias, attn_gain, attn_shift,
        up_weight, up_bias, down_weight, down_bias, ffn_gain, ffn_shift)
    if width % (8 * n) == 0 and n // 8 * 2 * UNIT_ROWS * 8 == up_weight.shape[1]:
        grads = deliver_call(backward_call(
            n, segment_ids, pair_index, z, invn, cnt, attn_gain, ffn_gain, first_low, tokens, normed_two, stat, acted,
            deriv, down_weight, up_weight, normed_one, proj_weight, rinv, context, qkv, exps, qkv_weight))
        return (grads[1].reshape(()), layer_out, grads[0]) + tuple(v.reshape(-1) for v in grads[2:])
    loss, grad_seg = contrast_call(n, z.astype(BF16), z, invn, cnt, pair_index)
    inv_one = stat[:, :1]
    inv_two = stat[:, 1:2]
    normed_one = normed_one.astype(F32)
    normed_two = normed_two.astype(F32)
    row_base = (jnp.arange(rows, dtype=jnp.int32) * SEGS)[:, None]
    local_ids = jnp.where(segment_ids >= 0, segment_ids + row_base, -1).reshape(toks)
    member = (local_ids[None, :] == jnp.arange(rows * SEGS, dtype=jnp.int32)[:, None]).astype(F32)
    grad_y = lax.dot_general(member, grad_seg, (((0,), (0,)), ((), ())), precision=lax.Precision.HIGHEST)
    ffn_gain_part = jnp.sum(grad_y * normed_two, axis=0)
    ffn_shift_part = jnp.sum(grad_y, axis=0)
    grad_r2 = norm_back(grad_y, normed_two, inv_two, ffn_gain)
    grad_down_low = grad_r2.astype(BF16)
    down_bias_part = jnp.sum(grad_down_low.astype(F32), axis=0)
    down_weight_part = dot_tn(acted, grad_down_low)
    grad_up_low = (dot_nt(grad_down_low, down_weight) * deriv.astype(F32)).astype(BF16)
    up_bias_part = jnp.sum(grad_up_low.astype(F32), axis=0)
    up_weight_part = dot_tn(first_low, grad_up_low)
    grad_first = grad_r2 + dot_nt(grad_up_low, up_weight)
    attn_gain_part = jnp.sum(grad_first * normed_one, axis=0)
    attn_shift_part = jnp.sum(grad_first, axis=0)
    grad_r1 = norm_back(grad_first, normed_one, inv_one, attn_gain)
    grad_att_low = grad_r1.astype(BF16)
    proj_bias_part = jnp.sum(grad_att_low.astype(F32), axis=0)
    proj_weight_part = dot_tn(context, grad_att_low)
    grad_context = dot_nt(grad_att_low, proj_weight).astype(BF16)
    by_row = lambda v: v.reshape(rows, row_len, -1)
    grad_qkv = lax.map(
        attend_back,
        (by_row(qkv), exps.reshape(rows, -1, 2, row_len, row_len), by_row(rinv), by_row(context), by_row(grad_context)),
    ).reshape(toks, 3 * width)
    qkv_bias_part = jnp.sum(grad_qkv.astype(F32), axis=0)
    qkv_weight_part = dot_tn(tokens, grad_qkv)
    tokens_grad = grad_r1 + dot_nt(grad_qkv, qkv_weight)
    scatter = lambda v: lax.psum_scatter(v.reshape(-1), "batch", scatter_dimension=0, tiled=True)
    sums = lax.psum(
        (qkv_bias_part[:width], qkv_bias_part[2 * width :], proj_bias_part, attn_gain_part, attn_shift_part,
         up_bias_part, down_bias_part, ffn_gain_part, ffn_shift_part),
        "batch",
    )
    return (loss[0, 0], layer_out, tokens_grad, scatter(qkv_weight_part), scatter(proj_weight_part),
            scatter(up_weight_part), scatter(down_weight_part)) + tuple(sums)


def solution(mesh):
    split, whole = P("batch"), P()
    return jax.shard_map(
        per_device,
        mesh=mesh,
        in_specs=(P("batch", None), P("batch", None), split) + (whole,) * 13,
        out_specs=(whole, P("batch", None), P("batch", None)) + (split,) * 4 + (whole,) * 9,
        check_vma=False,
    )
```
